128 devices in a mesh: dom: 128 (over z, x, y, core).
Axes of the slice: x: 4, y: 4, z: 4, core: 2. Of those that a mesh axis runs over, the one named last changes fastest.
Arguments:
- adjoint: float32 [9, 512, 16384], P(None, None, 'dom'), may hold values from -6 to 6
- snapshots: float32 [2, 3, 512, 16384], P(None, None, None, 'dom'), may hold values from -6 to 6
- density: float32 [16384], P('dom'), may hold values from 1 to 3
- lame_lambda: float32 [16384], P('dom'), may hold values from 0.5 to 2
- lame_mu: float32 [16384], P('dom'), may hold values from 0.5 to 2
- element_order: int32 [16384], P('dom'), may hold values from 3 to 7
- orient: int32 [16384], P('dom'), may hold values from 0 to 3
- new_owner: int32 [16384], P('dom'), may hold values from 0 to 127, as said below
- new_slot: int32 [16384], P('dom'), may hold values from 0 to 127
Outputs:
- adjoint_out: float32 [9, 512, 16384], P(None, None, 'dom')
- gradients: float32 [2, 16384], P(None, 'dom')
The draws below stay inside these ranges and needn't reach their ends.
Inputs may be any that keep to these rules, and one draw needn't show every extreme that they name: (new_owner, new_slot) is a one-to-one map of all elements onto all (device, slot) pairs; an element whose new owner is its present device keeps its slot; each device sends away exactly 96 elements and receives exactly 96; at most 2 go from one device to any one other device, and exactly 2 to some.
All inputs are finite; a program needn't handle non-finite values.
Results may differ from the reference program's by a relative error of at most 0.0003.
Values sent between devices are 32-bit elements; how exact they have to be, the bound alone decides.
No kernel may reach another device: no remote copies, remote signals or barrier semaphores. Data moves between devices by JAX's collectives and lax.ppermute only.
A program may use at most 256 MiB of HBM per device.

```python
import math
import jax
import jax.numpy as jnp
from jax import lax

NP = 8
NM = 512
ORD_MIN = 3
EX = 8
E_DEV = 128
ELEMENTS = 16384
STEPS = 2
N_DOM = 128


def migration_plan(key):
    devices = N_DOM
    moving = 3 * devices // 4
    doubled = devices // 8
    slot_keys = jax.random.split(jax.random.fold_in(key, 11), devices)

    def shuffle_slots(one_key):
        return jax.random.permutation(one_key, E_DEV)
    shuffled = jax.vmap(shuffle_slots)(slot_keys)
    mover_slots = shuffled[:, :moving].astype(jnp.int32)
    shift_pool = jax.random.permutation(jax.random.fold_in(key, 12), devices - 1) + 1
    mover_rank = jnp.arange(moving)
    shifts = shift_pool[jnp.where(mover_rank < 2 * doubled, mover_rank // 2, mover_rank - doubled)]
    sources = jnp.arange(devices)
    targets = ((sources[:, None] + shifts[None, :]) % devices).astype(jnp.int32)
    target_slots = mover_slots[targets, mover_rank[None, :]]
    owner_table = jnp.broadcast_to(sources[:, None], (devices, E_DEV)).astype(jnp.int32)
    slot_table = jnp.broadcast_to(jnp.arange(E_DEV)[None, :], (devices, E_DEV)).astype(jnp.int32)
    source_rows = jnp.broadcast_to(sources[:, None], (devices, moving))
    owner_table = owner_table.at[source_rows, mover_slots].set(targets)
    slot_table = slot_table.at[source_rows, mover_slots].set(target_slots)
    return (owner_table.reshape(-1), slot_table.reshape(-1))


def draw_new_owner(key, part):
    planned = migration_plan(key)
    return planned[0]


def draw_new_slot(key, part):
    planned = migration_plan(key)
    return planned[1]


def set_ends(result, key, least, high):
    spot = [jax.random.randint(jax.random.fold_in(key, axis), (), 0, length) for axis, length in enumerate(result.shape)]
    widest = result.shape.index(max(result.shape))
    neighbour = spot[:widest] + [(spot[widest] + 1) % result.shape[widest]] + spot[widest + 1:]
    return result.at[tuple(spot)].set(least).at[tuple(neighbour)].set(high)


def levels(own_key, shape, cuts, low, largest):
    def one(axis_at, parts):
        steps = jax.random.uniform(jax.random.fold_in(jax.random.fold_in(own_key, 6), axis_at), (parts,), jnp.float32, low / len(cuts), largest / len(cuts))
        return jnp.repeat(jnp.exp(steps), shape[axis_at] // parts).reshape((-1,) + (1,) * (len(shape) - axis_at - 1))

    level = one(*cuts[0])
    for cut in cuts[1:]:
        level = level * one(*cut)
    return level


def normal_values(rng, shape, deviation, reach, cuts=(), kind=jnp.bfloat16):
    result = jax.random.normal(rng, shape, jnp.float32) * deviation
    if len(cuts) > 0:
        result = levels(rng, shape, cuts, -0.22, 0.18) * result
    return jnp.clip(result, min=-reach, max=reach).astype(kind)


def setup_inputs(seed: int = 0) -> dict:
    seeds = jax.random.split(jax.random.key(seed), 10)
    adjoint = normal_values(seeds[0], (9, NM, ELEMENTS), 1.0, 6.0, ((2, 128),), jnp.float32)
    snapshots = normal_values(seeds[1], (STEPS, 3, NM, ELEMENTS), 1.0, 6.0, ((3, 128),), jnp.float32)
    density = jnp.clip(jnp.exp(math.log(3.0) - 1.0986123 * jax.random.uniform(seeds[2], (ELEMENTS,), jnp.float32) ** levels(seeds[2], (ELEMENTS,), ((0, 128),), -0.2, 0.2)), 1.0, 3.0)
    lame_lambda = jnp.clip(jnp.exp(math.log(2.0) - 1.3862944 * jax.random.uniform(seeds[3], (ELEMENTS,), jnp.float32) ** levels(seeds[3], (ELEMENTS,), ((0, 128),), -0.2, 0.2)), 0.5, 2.0)
    lame_mu = jnp.clip(jnp.exp(math.log(2.0) - 1.3862944 * jax.random.uniform(seeds[4], (ELEMENTS,), jnp.float32) ** levels(seeds[4], (ELEMENTS,), ((0, 128),), -0.2, 0.2)), 0.5, 2.0)
    element_order = set_ends(jax.random.randint(seeds[5], (ELEMENTS,), ORD_MIN, NP), jax.random.fold_in(seeds[5], 1), ORD_MIN, NP - 1).astype(jnp.int32)
    orient = set_ends(jax.random.randint(seeds[6], (ELEMENTS,), 0, 4), jax.random.fold_in(seeds[6], 1), 0, 3).astype(jnp.int32)
    new_owner = draw_new_owner(jax.random.fold_in(seeds[9], 71), 0)
    new_slot = draw_new_slot(jax.random.fold_in(seeds[9], 71), 0)
    return {"adjoint": adjoint, "snapshots": snapshots, "density": density, "lame_lambda": lame_lambda, "lame_mu": lame_mu, "element_order": element_order, "orient": orient, "new_owner": new_owner, "new_slot": new_slot}


precise = lax.Precision.HIGHEST
step_dt = 0.01
voigt_index = ((3, 8, 7), (8, 4, 6), (7, 6, 5))
stress_pairs = ((0, 0), (1, 1), (2, 2), (1, 2), (0, 2), (0, 1))
trace_forms = ('i,fijke->fjke', 'j,fijke->fike', 'k,fijke->fije')
lift_forms = ('i,fjke->fijke', 'j,fike->fijke', 'k,fije->fijke')
slope_forms = ('mi,fijke->fmjke', 'mj,fijke->fimke', 'mk,fijke->fijme')

def basis_tables(modes_count):
    mode_ranks = jnp.arange(modes_count)
    lower_rank = mode_ranks[:, None]
    higher_rank = mode_ranks[None, :]
    derivative = jnp.where((higher_rank > lower_rank) & ((higher_rank + lower_rank) % 2 == 1), 2.0 * lower_rank + 1.0, 0.0).astype(jnp.float32)
    all_ones = jnp.ones((modes_count,), jnp.float32)
    alternating = jnp.where(mode_ranks % 2 == 0, 1.0, -1.0).astype(jnp.float32)
    lift_scale = mode_ranks.astype(jnp.float32) + 0.5
    mass_weight = 2.0 / (2.0 * mode_ranks.astype(jnp.float32) + 1.0)
    return (derivative, all_ones, alternating, lift_scale, mass_weight)

def frame_tables(element_order, orient, modes_count):
    mode_ranks = jnp.arange(modes_count)
    odd_mode = (mode_ranks % 2 == 1)[:, None]
    sign_x = jnp.where(odd_mode & (orient % 2 == 1)[None, :], -1.0, 1.0).astype(jnp.float32)
    sign_y = jnp.where(odd_mode & (orient // 2 == 1)[None, :], -1.0, 1.0).astype(jnp.float32)
    frame_sign = sign_x[:, None, None, :] * sign_y[None, :, None, :]
    keep_mode = jnp.where(mode_ranks[:, None] <= element_order[None, :], 1.0, 0.0).astype(jnp.float32)
    order_mask = keep_mode[:, None, None, :] * keep_mode[None, :, None, :] * keep_mode[None, None, :, :]
    return (frame_sign, order_mask)

def apply_flux(values, direction, density, lame_lambda, lame_mu):
    velocity_part = [values[voigt_index[component][direction]] / density for component in range(3)]
    stress_part = []
    for index_b, index_c in stress_pairs:
        summed = jnp.zeros_like(values[0])
        if index_b == index_c:
            summed = summed + lame_lambda * values[direction]
        if index_b == direction:
            summed = summed + lame_mu * values[index_c]
        if index_c == direction:
            summed = summed + lame_mu * values[index_b]
        stress_part.append(summed)
    return jnp.stack(velocity_part + stress_part)

def shifted(values, offset):
    padding = jnp.zeros(values.shape[:-1] + (abs(offset),), values.dtype)
    if offset > 0:
        return jnp.concatenate([values[..., offset:], padding], axis=-1)
    return jnp.concatenate([padding, values[..., :offset]], axis=-1)

def volume_part(wavefield, density, lame_lambda, lame_mu):
    derivative = basis_tables(wavefield.shape[1])[0]
    summed = jnp.zeros_like(wavefield)
    for direction in range(3):
        derived = jnp.einsum(slope_forms[direction], derivative, wavefield, precision=precise)
        summed = summed + apply_flux(derived, direction, density, lame_lambda, lame_mu)
    return summed

def surface_part(wavefield, z_upper, z_lower, from_below, from_above, density, lame_lambda, lame_mu):
    tables = basis_tables(wavefield.shape[1])
    wave_speed = jnp.sqrt((lame_lambda + 2.0 * lame_mu) / density)
    column = jnp.arange(wavefield.shape[-1]) % EX
    keep_right = jnp.where(column != EX - 1, 1.0, 0.0).astype(wavefield.dtype)
    keep_left = jnp.where(column != 0, 1.0, 0.0).astype(wavefield.dtype)
    summed = jnp.zeros_like(wavefield)
    for direction in range(3):
        if direction < 2:
            face_upper = jnp.einsum(trace_forms[direction], tables[1], wavefield, precision=precise)
            face_lower = jnp.einsum(trace_forms[direction], tables[2], wavefield, precision=precise)
        else:
            face_upper = z_upper
            face_lower = z_lower
        if direction == 0:
            outer_upper = shifted(face_lower, 1) * keep_right
            outer_lower = shifted(face_upper, -1) * keep_left
        elif direction == 1:
            outer_upper = shifted(face_lower, EX)
            outer_lower = shifted(face_upper, -EX)
        else:
            outer_upper = from_above
            outer_lower = from_below
        jump_upper = face_upper - outer_upper
        jump_lower = face_lower - outer_lower
        flux_upper = -0.5 * (apply_flux(jump_upper, direction, density, lame_lambda, lame_mu) + wave_speed * jump_upper)
        flux_lower = -0.5 * (-apply_flux(jump_lower, direction, density, lame_lambda, lame_mu) + wave_speed * jump_lower)
        summed = summed + jnp.einsum(lift_forms[direction], tables[3], flux_upper, precision=precise)
        summed = summed + jnp.einsum(lift_forms[direction], tables[3] * tables[2], flux_lower, precision=precise)
    return summed

def gradient_terms(wavefield, velocity):
    tables = basis_tables(wavefield.shape[1])
    weight_vec = tables[4]
    mass_cube = weight_vec[:, None, None, None] * weight_vec[None, :, None, None] * weight_vec[None, None, :, None]
    slopes = [jnp.einsum(slope_forms[d], tables[0], velocity, precision=precise) for d in range(3)]
    divergence = slopes[0][0] + slopes[1][1] + slopes[2][2]
    trace_stress = wavefield[3] + wavefield[4] + wavefield[5]
    lambda_part = lax.optimization_barrier(jnp.sum(mass_cube * trace_stress * divergence, axis=(0, 1, 2)))
    shear_sum = jnp.zeros_like(divergence)
    for position, (index_b, index_c) in enumerate(stress_pairs):
        shear_sum = shear_sum + wavefield[3 + position] * (slopes[index_b][index_c] + slopes[index_c][index_b])
    shear_part = lax.optimization_barrier(jnp.sum(mass_cube * shear_sum, axis=(0, 1, 2)))
    return jnp.stack([lambda_part, shear_part])

def to_layers(values):
    shaped = values.reshape(values.shape[:-1] + (N_DOM, E_DEV))
    return jnp.moveaxis(shaped, -2, 0)

def from_layers(values):
    shaped = jnp.moveaxis(values, 0, -2)
    return shaped.reshape(shaped.shape[:-2] + (N_DOM * E_DEV,))

def reference(adjoint, snapshots, density, lame_lambda, lame_mu, element_order, orient, new_owner, new_slot):
    target = (new_owner * E_DEV + new_slot).astype(jnp.int32)

    def place(values):
        return to_layers(jnp.zeros_like(values).at[..., target].set(values))
    wave_layers = place(adjoint).reshape((N_DOM, 9, NP, NP, NP, E_DEV))
    snap_layers = place(snapshots).reshape((N_DOM, STEPS, 3, NP, NP, NP, E_DEV))
    layer_density = place(density)
    layer_lambda = place(lame_lambda)
    layer_mu = place(lame_mu)
    layer_order = place(element_order)
    layer_orient = place(orient)

    def frames(order_row, orient_row):
        return frame_tables(order_row, orient_row, NP)
    frame_sign, order_mask = jax.vmap(frames)(layer_order, layer_orient)
    wavefield = frame_sign[:, None] * order_mask[:, None] * wave_layers
    velocity = frame_sign[:, None, None] * order_mask[:, None, None] * snap_layers
    tables = basis_tables(NP)

    def full_rhs(current):
        z_upper = jnp.einsum('k,zfijke->zfije', tables[1], current, precision=precise)
        z_lower = jnp.einsum('k,zfijke->zfije', tables[2], current, precision=precise)
        from_below = jnp.concatenate([jnp.zeros_like(z_upper[:1]), z_upper[:-1]], axis=0)
        from_above = jnp.concatenate([z_lower[1:], jnp.zeros_like(z_lower[:1])], axis=0)

        def one_layer(layer_items):
            field_now, upper_now, lower_now, below_now, above_now, dens_now, lambda_now, shear_now, mask_now = layer_items
            volume = volume_part(field_now, dens_now, lambda_now, shear_now)
            surface = surface_part(field_now, upper_now, lower_now, below_now, above_now, dens_now, lambda_now, shear_now)
            return (volume + surface) * mask_now
        return lax.map(one_layer, (current, z_upper, z_lower, from_below, from_above, layer_density, layer_lambda, layer_mu, order_mask))

    def layer_gradient(layer_items):
        return gradient_terms(layer_items[0], layer_items[1])
    gradient_sum = jnp.zeros((N_DOM, 2, E_DEV), jnp.float32)
    for step_index in range(STEPS):
        section_one = wavefield + step_dt * full_rhs(wavefield)
        section_two = section_one + step_dt * full_rhs(section_one)
        wavefield = 0.5 * (wavefield + section_two)
        gradient_sum = gradient_sum + step_dt * lax.map(layer_gradient, (wavefield, velocity[:, step_index]))
    adjoint_out = (frame_sign[:, None] * wavefield).reshape((N_DOM, 9, NP * NP * NP, E_DEV))
    return (from_layers(adjoint_out), from_layers(gradient_sum))
```

```python
import jax
import jax.numpy as jnp
from jax import lax
from jax.experimental import pallas as pl
from jax.experimental.pallas import tpu as pltpu
from jax.sharding import PartitionSpec as P

NP = 8
NM = 512
EX = 8
NE = 128
STEPS = 2
DEV = 128
FIELDS = 9
SNAPS = 6
BLOCK_A = 10
BLOCK_B = 5
DT = 0.01
VMEM_LIMIT = 16 * 1024 * 1024
f32 = jnp.float32
bf16 = jnp.bfloat16

VOIGT = ((3, 8, 7), (8, 4, 6), (7, 6, 5))
ACTIVE = tuple((0, 1, 2) + VOIGT[a] for a in range(3))


def split3(x):
    high = x.astype(bf16)
    rest = x - high.astype(f32)
    middle = rest.astype(bf16)
    low = (rest - middle.astype(f32)).astype(bf16)
    return high, middle, low


def call(kernel, operands, out_shape, scratch_shapes=(), flops=0, nbytes=0):
    return pl.pallas_call(
        kernel,
        in_specs=[
            pl.BlockSpec(memory_space=pltpu.SMEM if x.shape == (1,) else pltpu.VMEM)
            for x in operands
        ],
        out_specs=[pl.BlockSpec(memory_space=pltpu.VMEM) for _ in out_shape],
        out_shape=out_shape,
        scratch_shapes=list(scratch_shapes),
        compiler_params=pltpu.CompilerParams(vmem_limit_bytes=VMEM_LIMIT),
        cost_estimate=pl.CostEstimate(flops=flops, bytes_accessed=nbytes, transcendentals=0),
    )(*operands)


def array(*shape, dtype=f32):
    return jax.ShapeDtypeStruct(shape, dtype)


def scatter_rows(hot, x, out_ref, row):
    parts = jnp.concatenate(split3(x), axis=1)
    hots = jnp.concatenate([hot, hot, hot], axis=1)
    rows = lax.dot_general(hots, parts, (((1,), (1,)), ((), ())), preferred_element_type=f32)
    for r in range(2):
        for q in range(4):
            out_ref[:, row + r * 4 + q, :] = rows[r * DEV : (r + 1) * DEV, q * 128 : (q + 1) * 128]


def pack_a_kernel(me_ref, owner_ref, meta_ref, adj_ref, snap_ref, out_ref, hot_ref):
    owner_row = owner_ref[...]
    owner_all = jnp.broadcast_to(owner_row, (NE, NE))
    owner_col = jnp.transpose(owner_all)
    at0 = lax.broadcasted_iota(jnp.int32, (NE, NE), 0)
    at1 = lax.broadcasted_iota(jnp.int32, (NE, NE), 1)
    earlier = jnp.where((owner_col == owner_all) & (at0 < at1), 1.0, 0.0)
    rank = jnp.sum(earlier, axis=0, keepdims=True)
    dest = jnp.where(owner_row != me_ref[0], owner_row, -1)
    for r in range(2):
        chosen = (at0 == dest) & (rank == float(r))
        hot_ref[r * DEV : (r + 1) * DEV, :] = jnp.where(chosen, 1.0, 0.0).astype(bf16)

    @pl.loop(0, FIELDS)
    def _(g):
        scatter_rows(hot_ref[...], adj_ref[g], out_ref, pl.multiple_of(g * 8, 8))

    first = jnp.where(
        lax.broadcasted_iota(jnp.int32, (8, NE), 0) < 6, meta_ref[...], snap_ref[0, 0:8, :]
    )
    block = jnp.concatenate([first, snap_ref[0, 8:, :]], axis=0)
    scatter_rows(hot_ref[...], block, out_ref, FIELDS * 8)


def pack_b_kernel(hot_ref, snap_ref, out_ref):
    row0 = lax.broadcasted_iota(jnp.int32, (8, NE), 0) == 0

    @pl.loop(0, BLOCK_B)
    def _(g):
        moved = snap_ref[0, pl.ds(g + 1, 1), :]
        first = jnp.where(row0, jnp.broadcast_to(moved, (8, NE)), snap_ref[g + 1, 0:8, :])
        block = jnp.concatenate([first, snap_ref[g + 1, 8:, :]], axis=0)
        scatter_rows(hot_ref[...], block, out_ref, pl.multiple_of(g * 8, 8))


def pack(me, owner, meta, adjoint, snaps):
    send_a, hot = call(
        pack_a_kernel,
        (me, owner, meta, adjoint, snaps),
        [array(DEV, BLOCK_A * 8, 128), array(2 * DEV, NE, dtype=bf16)],
    )
    (send_b,) = call(pack_b_kernel, (hot, snaps), [array(DEV, BLOCK_B * 8, 128)])
    return send_a, send_b


def gather_elements(pick, got_ref, row):
    slots = [
        jnp.concatenate([got_ref[:, row + r * 4 + q, :] for q in range(4)], axis=1) for r in range(2)
    ]
    parts = jnp.concatenate(split3(jnp.concatenate(slots, axis=0)), axis=0)
    picks = jnp.concatenate([pick, pick, pick], axis=1)
    placed = lax.dot_general(picks, parts, (((1,), (0,)), ((), ())), preferred_element_type=f32)
    return jnp.transpose(placed)


def mode_indices(shape):
    mode = lax.broadcasted_iota(jnp.int32, shape, 0)
    return mode // 64, (mode // 8) % 8, mode % 8


def mask_and_sign(order, orient):
    i, j, k = mode_indices((NM, NE))
    highest = jnp.maximum(jnp.maximum(i, j), k).astype(f32)
    flip_x = (orient == 1.0) | (orient == 3.0)
    flip_y = orient >= 2.0
    sign_x = jnp.where(i % 2 == 1, jnp.where(flip_x, -1.0, 1.0), 1.0)
    sign_y = jnp.where(j % 2 == 1, jnp.where(flip_y, -1.0, 1.0), 1.0)
    return jnp.where(highest <= order, sign_x * sign_y, 0.0)


def face_traces(modes, row):
    low4, low2, even = row < 4, row % 4 < 2, row % 2 == 0
    fours = []
    for j in range(4):
        first, second = modes[j], modes[j + 4]
        other = jnp.where(low4, second, first)
        fours.append(jnp.where(low4, first, second) + pltpu.roll(other, 4, 0))
    twos = []
    for j in range(2):
        first, second = fours[j], fours[j + 2]
        twos.append(
            jnp.where(low2, first + pltpu.roll(first, 6, 0), second + pltpu.roll(second, 2, 0))
        )
    first, second = twos
    next_first, next_second = pltpu.roll(first, 7, 0), pltpu.roll(second, 1, 0)
    upper = jnp.where(even, first + next_first, second + next_second)
    lower = jnp.where(even, first - next_first, next_second - second)
    return upper, lower


def place_kernel(
    me_ref, owner_ref, meta_ref, got_ref, adj_ref,
    wave_ref, upper_ref, lower_ref, rows_ref, pick_ref, head_ref, frame_ref,
):
    keep = owner_ref[...] == me_ref[0]
    at1 = lax.broadcasted_iota(jnp.int32, (DEV, NE), 1).astype(f32)
    for r in range(2):
        slot = got_ref[:, FIELDS * 8 + r * 4, 5:6]
        chosen = jnp.where(slot == at1 + 1.0, 1.0, 0.0)
        pick_ref[:, r * DEV : (r + 1) * DEV] = jnp.transpose(chosen).astype(bf16)
    block = gather_elements(pick_ref[...], got_ref, FIELDS * 8)
    head_ref[...] = block
    meta = jnp.where(keep, meta_ref[...], block[0:8])
    density, lam, mu = meta[0:1], meta[1:2], meta[2:3]
    order, orient = meta[3:4], meta[4:5]
    rows_ref[0:1, :] = 1.0 / density
    rows_ref[1:2, :] = lam
    rows_ref[2:3, :] = mu
    rows_ref[3:4, :] = jnp.sqrt((lam + 2.0 * mu) / density)
    rows_ref[4:5, :] = order
    rows_ref[5:6, :] = orient
    rows_ref[6:8, :] = jnp.zeros((2, NE), f32)
    frame_ref[...] = mask_and_sign(order, orient)

    @pl.loop(0, FIELDS)
    def _(f):
        block = gather_elements(pick_ref[...], got_ref, pl.multiple_of(f * 8, 8))
        wave = jnp.where(keep, adj_ref[f], block) * frame_ref[...]
        wave = wave.reshape(64, NP, NE)
        wave_ref[f] = wave
        row = lax.broadcasted_iota(jnp.int32, (NP, NE), 0)
        for i in range(NP):
            upper, lower = face_traces([wave[i * NP + j] for j in range(NP)], row)
            upper_ref[f, i * NP : (i + 1) * NP, :] = upper
            lower_ref[f, i * NP : (i + 1) * NP, :] = lower


def place(me, owner, meta, got, adjoint):
    return call(
        place_kernel,
        (me, owner, meta, got, adjoint),
        [
            array(FIELDS, 64, NP, NE),
            array(FIELDS, 64, NE),
            array(FIELDS, 64, NE),
            array(8, NE),
            array(NE, 2 * DEV, dtype=bf16),
            array(NM, NE),
        ],
        [pltpu.VMEM((NM, NE), f32)],
    )


def materials(rows_ref):
    full = lambda r: jnp.broadcast_to(rows_ref[r : r + 1, :], (NP, NE))
    return full(0), full(1), full(2), full(3)


def apply_b(values, direction, rinv, lam, mu):
    out = [None] * FIELDS
    for c in range(3):
        out[c] = values[VOIGT[c][direction]] * rinv
    spread = lam * values[direction]
    for b in range(3):
        out[3 + b] = spread
    out[3 + direction] = spread + 2.0 * mu * values[direction]
    for c in range(3):
        if c != direction:
            out[VOIGT[c][direction]] = mu * values[c]
    return out


def face_flux(total, difference, direction, rinv, lam, mu, speed):
    even_b = apply_b(difference, direction, rinv, lam, mu)
    odd_b = apply_b(total, direction, rinv, lam, mu)
    even, odd = [], []
    for f in range(FIELDS):
        pen_even, pen_odd = speed * total[f], speed * difference[f]
        if even_b[f] is not None:
            pen_even, pen_odd = pen_even + even_b[f], pen_odd + odd_b[f]
        even.append(-0.25 * pen_even)
        odd.append(-0.25 * pen_odd)
    return even, odd


def local_flux(evens, odds, direction, offset, keep_up, keep_down, rinv, lam, mu, speed):
    total, difference = [], []
    for f in range(FIELDS):
        upper, lower = evens[f] + odds[f], evens[f] - odds[f]
        above = pltpu.roll(lower, NE - offset, 1) * keep_up
        below = pltpu.roll(upper, offset, 1) * keep_down
        total.append((upper - above) + (lower - below))
        difference.append((upper - above) - (lower - below))
    return face_flux(total, difference, direction, rinv, lam, mu, speed)


def lane_keeps():
    lane = lax.broadcasted_iota(jnp.int32, (NP, NE), 1)
    one = lambda cond: jnp.where(cond, 1.0, 0.0)
    column = lane % EX
    return (
        (one(column != EX - 1), one(column != 0)),
        (one(lane < NE - EX), one(lane >= EX)),
    )


def mode_rows():
    k = lax.broadcasted_iota(jnp.int32, (NP, NE), 0)
    one = lambda cond: jnp.where(cond, 1.0, 0.0)
    return one(k < 7), one(k < 6), one(k < 4), (2 * k + 1).astype(f32)


def sums_above(x, keep1, keep2, keep4):
    x = pltpu.roll(x, 7, 0) * keep1
    x = x + pltpu.roll(x, 6, 0) * keep2
    return x + pltpu.roll(x, 4, 0) * keep4


def inner_kernel(wave_ref, rows_ref, out_ref, flux_ref, run_ref, fluxy_ref):
    rinv, lam, mu, speed = materials(rows_ref)
    keeps_x, keeps_y = lane_keeps()
    keep1, keep2, keep4, factor_z = mode_rows()
    run_ref[...] = jnp.zeros_like(run_ref)

    @pl.loop(0, NP)
    def _(g):
        i = NP - 1 - g
        parity = lax.rem(i, 2)
        factor_x = (2 * i + 1).astype(f32)

        evens, odds = [], []
        for f in range(FIELDS):
            col = [wave_ref[f, i * NP + j] for j in range(NP)]
            evens.append((col[0] + col[2]) + (col[4] + col[6]))
            odds.append((col[1] + col[3]) + (col[5] + col[7]))
        even, odd = local_flux(evens, odds, 1, EX, *keeps_y, rinv, lam, mu, speed)
        for f in range(FIELDS):
            fluxy_ref[0, f] = even[f]
            fluxy_ref[1, f] = odd[f]

        sums_y = {f: [None, None] for f in ACTIVE[1]}
        for j in range(NP - 1, -1, -1):
            here = [wave_ref[f, i * NP + j] for f in range(FIELDS)]
            slope = [{}, {}, {}]
            for f in ACTIVE[0]:
                slope[0][f] = factor_x * run_ref[parity, f, j]
            for f in ACTIVE[1]:
                if sums_y[f][j % 2] is not None:
                    slope[1][f] = (2.0 * j + 1.0) * sums_y[f][j % 2]
            for f in ACTIVE[2]:
                slope[2][f] = factor_z * sums_above(here[f], keep1, keep2, keep4)

            def total(pairs):
                found = [slope[a][f] for a, f in pairs if f in slope[a]]
                result = found[0]
                for item in found[1:]:
                    result = result + item
                return result

            result = [None] * FIELDS
            for c in range(3):
                result[c] = rinv * total([(a, VOIGT[c][a]) for a in range(3)])
            spread = lam * total([(a, a) for a in range(3)])
            for b in range(3):
                if b in slope[b]:
                    result[3 + b] = spread + 2.0 * mu * slope[b][b]
                else:
                    result[3 + b] = spread
            for b, c in ((1, 2), (0, 2), (0, 1)):
                result[VOIGT[b][c]] = mu * total([(b, c), (c, b)])
            for f in range(FIELDS):
                out_ref[f, i * NP + j] = result[f] + (2.0 * j + 1.0) * fluxy_ref[j % 2, f]

            for f in ACTIVE[1]:
                before = sums_y[f][1 - j % 2]
                sums_y[f][1 - j % 2] = here[f] if before is None else before + here[f]
            for f in range(FIELDS):
                run_ref[1 - parity, f, j] += here[f]

    @pl.loop(0, NP)
    def _(j):
        even_x, odd_x = local_flux(
            [run_ref[1, f, j] for f in range(FIELDS)],
            [run_ref[0, f, j] for f in range(FIELDS)],
            0, 1, *keeps_x, rinv, lam, mu, speed,
        )
        for f in range(FIELDS):
            flux_ref[0, f, j] = even_x[f]
            flux_ref[1, f, j] = odd_x[f]


def inner(wave, rows):
    return call(
        inner_kernel,
        (wave, rows),
        [array(FIELDS, 64, NP, NE), array(2, FIELDS, NP, NP, NE)],
        [pltpu.VMEM((2, FIELDS, NP, NP, NE), f32), pltpu.VMEM((2, FIELDS, NP, NE), f32)],
    )


def update_kernel(last, half, *refs):
    refs = list(refs)
    base_ref = refs.pop(0) if half else None
    (wave_ref, part_ref, flux_ref, upper_ref, lower_ref, below_ref, above_ref, rows_ref,
     *outs, fluxz_ref) = refs
    rinv, lam, mu, speed = materials(rows_ref)
    order = jnp.broadcast_to(rows_ref[4:5, :], (NP, NE))
    orient = jnp.broadcast_to(rows_ref[5:6, :], (NP, NE))
    k = lax.broadcasted_iota(jnp.int32, (NP, NE), 0)
    k_even = k % 2 == 0
    factor_z = (2 * k + 1).astype(f32)
    step = 0.5 * DT if half else DT

    @pl.loop(0, NP)
    def _(i):
        parity = lax.rem(i, 2)
        factor_x = (2 * i + 1).astype(f32)
        at = pl.multiple_of(i * NP, NP)
        rows = pl.ds(at, NP)
        total, difference = [], []
        for f in range(FIELDS):
            jump_upper = upper_ref[f, rows] - above_ref[f, rows]
            jump_lower = lower_ref[f, rows] - below_ref[f, rows]
            total.append(jump_upper + jump_lower)
            difference.append(jump_upper - jump_lower)
        even, odd = face_flux(total, difference, 2, rinv, lam, mu, speed)
        for f in range(FIELDS):
            fluxz_ref[0, f] = even[f]
            fluxz_ref[1, f] = odd[f]

        masks = []
        for j in range(NP):
            highest = jnp.maximum(k, jnp.maximum(i, j)).astype(f32)
            masks.append(jnp.where(highest <= order, step, 0.0))
        if last:
            flip_x = ((orient == 1.0) | (orient == 3.0)) & (parity == 1)
            sign_x = jnp.where(flip_x, -1.0, 1.0)
            sign_y = jnp.where(orient >= 2.0, -1.0, 1.0)
            signs = [sign_x, sign_x * sign_y]

        for f in range(FIELDS):
            fresh = []
            for j in range(NP):
                lifted = jnp.where(
                    k_even,
                    jnp.broadcast_to(fluxz_ref[0, f, j : j + 1, :], (NP, NE)),
                    jnp.broadcast_to(fluxz_ref[1, f, j : j + 1, :], (NP, NE)),
                )
                slope = part_ref[f, at + j] + factor_x * flux_ref[parity, f, j] + factor_z * lifted
                start = wave_ref[f, at + j]
                if half:
                    start = 0.5 * (base_ref[f, at + j] + start)
                new = start + masks[j] * slope
                if last:
                    outs[1][f, at + j] = new * signs[j % 2]
                    if f >= 3:
                        outs[0][0, f - 3, at + j] = base_ref[f, at + j]
                        outs[0][1, f - 3, at + j] = new
                else:
                    outs[0][f, at + j] = new
                fresh.append(new)
            if not last:
                outs[1][f, rows], outs[2][f, rows] = face_traces(fresh, k)


def update(base, wave, part, flux, upper, lower, below, above, rows, last):
    half = base is not None
    whole, trace = array(FIELDS, 64, NP, NE), array(FIELDS, 64, NE)
    operands = (wave, part, flux, upper, lower, below, above, rows)
    both = array(STEPS, 6, 64, NP, NE)

    def kernel(*refs):
        update_kernel(last, half, *refs)

    return call(
        kernel,
        (base,) + operands if half else operands,
        [both, whole] if last else [whole, trace, trace],
        [pltpu.VMEM((2, FIELDS, NP, NE), f32)],
    )


def gradient_kernel(
    me_ref, owner_ref, rows_ref, pick_ref, head_ref, snap_ref, got_ref, stress_ref,
    out_ref, vel_ref, moved_ref, frame_ref,
):
    keep = owner_ref[...] == me_ref[0]
    row = lax.broadcasted_iota(jnp.int32, (8, NE), 0)
    out_ref[...] = jnp.zeros_like(out_ref)
    frame_ref[...] = mask_and_sign(rows_ref[4:5, :], rows_ref[5:6, :])

    @pl.loop(0, SNAPS)
    def _(g):
        index = jnp.where(g < BLOCK_B, g + 1, 0)
        step, c = index // 3, lax.rem(index, 3)

        def settle(block):
            velocity = jnp.where(keep, snap_ref[index], block) * frame_ref[...]
            vel_ref[...] = velocity.reshape(64, NP, NE)

        @pl.when(g < BLOCK_B)
        def _():
            block = gather_elements(pick_ref[...], got_ref, pl.multiple_of(g * 8, 8))
            moved_ref[pl.ds(g + 1, 1), :] = block[0:1]
            first = jnp.where(row == 0, 0.0, block[0:8])
            settle(jnp.concatenate([first, block[8:]], axis=0))

        @pl.when(g == BLOCK_B)
        def _():
            first = jnp.where(
                row == 0, 0.0, jnp.where(row < 6, moved_ref[...], head_ref[0:8, :])
            )
            settle(jnp.concatenate([first, head_ref[8:, :]], axis=0))

        keep1, keep2, keep4, factor_z = mode_rows()
        weight_z = 2.0 / factor_z
        is_x, is_y, is_z = c == 0, c == 1, c == 2

        def pick3(x, y, z):
            return jnp.where(is_x, x, jnp.where(is_y, y, z))

        sum_lambda = jnp.zeros((NP, NE), f32)
        sum_shear = jnp.zeros((NP, NE), f32)
        runs = [[None] * NP, [None] * NP]
        for i in range(NP - 1, -1, -1):
            run_y = [None, None]
            for j in range(NP - 1, -1, -1):
                at = i * NP + j
                here = vel_ref[at]
                weight_x, weight_y = 2.0 / (2.0 * i + 1.0), 2.0 / (2.0 * j + 1.0)
                zero = jnp.zeros((NP, NE), f32)
                slope_x = zero if runs[i % 2][j] is None else runs[i % 2][j]
                slope_y = zero if run_y[j % 2] is None else run_y[j % 2]
                slope_x = (2.0 * weight_y) * (weight_z * slope_x)
                slope_y = (2.0 * weight_x) * (weight_z * slope_y)
                slope_z = (2.0 * weight_x * weight_y) * sums_above(here, keep1, keep2, keep4)
                sxx, syy, szz = (stress_ref[step, f, at] for f in range(3))
                syz, sxz, sxy = (stress_ref[step, f, at] for f in range(3, 6))
                own = pick3(slope_x, slope_y, slope_z)
                sum_lambda = sum_lambda + own * (sxx + syy + szz)
                sum_shear = (
                    sum_shear
                    + slope_x * pick3(2.0 * sxx, sxy, sxz)
                    + slope_y * pick3(sxy, 2.0 * syy, syz)
                    + slope_z * pick3(sxz, syz, 2.0 * szz)
                )
                for store, spot in ((run_y, 1 - j % 2), (runs[1 - i % 2], j)):
                    store[spot] = here if store[spot] is None else store[spot] + here
        out_ref[0:1, :] += DT * jnp.sum(sum_lambda, axis=0, keepdims=True)
        out_ref[1:2, :] += DT * jnp.sum(sum_shear, axis=0, keepdims=True)


def gradient(me, owner, rows, pick, head, snaps, got, stress):
    (result,) = call(
        gradient_kernel,
        (me, owner, rows, pick, head, snaps, got, stress),
        [array(2, NE)],
        [pltpu.VMEM((64, NP, NE), f32), pltpu.VMEM((8, NE), f32), pltpu.VMEM((NM, NE), f32)],
    )
    return result


def exchange(send):
    return lax.all_to_all(send, "dom", split_axis=0, concat_axis=0, tiled=True)


def traces_of_neighbours(upper, lower):
    up = [(d, d + 1) for d in range(DEV - 1)]
    down = [(d + 1, d) for d in range(DEV - 1)]
    return lax.ppermute(upper, "dom", up), lax.ppermute(lower, "dom", down)


def body(
    adjoint, snapshots, density, lame_lambda, lame_mu, element_order, orient, new_owner, new_slot
):
    me = jnp.reshape(lax.axis_index("dom"), (1,)).astype(jnp.int32)
    owner = new_owner.reshape(1, NE)
    nothing = jnp.zeros_like(density)
    meta = jnp.stack(
        [
            density,
            lame_lambda,
            lame_mu,
            element_order.astype(f32),
            orient.astype(f32),
            new_slot.astype(f32) + 1.0,
            nothing,
            nothing,
        ]
    )
    snaps = snapshots.reshape(SNAPS, NM, NE)
    send_a, send_b = pack(me, owner, meta, adjoint, snaps)
    got_a = exchange(send_a)
    got_b = exchange(send_b)
    wave, upper, lower, rows, pick, head = place(me, owner, meta, got_a, adjoint)
    for step in range(STEPS):
        start = wave
        for half in (False, True):
            below, above = traces_of_neighbours(upper, lower)
            part, flux = inner(wave, rows)
            last = half and step == STEPS - 1
            base = start if half else None
            results = update(base, wave, part, flux, upper, lower, below, above, rows, last)
            if last:
                stress, signed = results
            else:
                wave, upper, lower = results
    gradients = gradient(me, owner, rows, pick, head, snaps, got_b, stress)
    return signed.reshape(FIELDS, NM, NE), gradients


def solution(mesh):
    shard = P("dom")
    in_specs = (P(None, None, "dom"), P(None, None, None, "dom")) + (shard,) * 7
    out_specs = (P(None, None, "dom"), P(None, "dom"))
    return jax.shard_map(body, mesh=mesh, in_specs=in_specs, out_specs=out_specs, check_vma=False)
```

```python
import jax
import jax.numpy as jnp
from jax import lax
from jax.experimental import pallas as pl
from jax.experimental.pallas import tpu as pltpu
from jax.sharding import PartitionSpec as P

NP = 8
NM = 512
EX = 8
NE = 128
STEPS = 2
DEV = 128
FIELDS = 9
SNAPS = 6
BLOCKS = FIELDS + SNAPS
DT = 0.01
f32 = jnp.float32
bf16 = jnp.bfloat16

VOIGT = ((3, 8, 7), (8, 4, 6), (7, 6, 5))
ACTIVE = tuple((0, 1, 2) + VOIGT[a] for a in range(3))


def split3(x):
    high = x.astype(bf16)
    rest = x - high.astype(f32)
    middle = rest.astype(bf16)
    low = (rest - middle.astype(f32)).astype(bf16)
    return high, middle, low


def call(kernel, operands, out_shape, scratch_shapes=(), hbm=(), hbm_out=(), limit=16):
    def space(position, x):
        return pltpu.HBM if position in hbm else pltpu.VMEM

    return pl.pallas_call(
        kernel,
        in_specs=[pl.BlockSpec(memory_space=space(n, x)) for n, x in enumerate(operands)],
        out_specs=[
            pl.BlockSpec(memory_space=pltpu.HBM if n in hbm_out else pltpu.VMEM)
            for n in range(len(out_shape))
        ],
        out_shape=out_shape,
        scratch_shapes=list(scratch_shapes),
        compiler_params=pltpu.CompilerParams(vmem_limit_bytes=limit * 1024 * 1024),
        cost_estimate=pl.CostEstimate(flops=0, bytes_accessed=0, transcendentals=0),
    )(*operands)


def array(*shape, dtype=f32):
    return jax.ShapeDtypeStruct(shape, dtype)


def scatter_rows(hot, x, out_ref, row):
    parts = jnp.concatenate(split3(x), axis=1)
    hots = jnp.concatenate([hot, hot, hot], axis=1)
    rows = lax.dot_general(hots, parts, (((1,), (1,)), ((), ())), preferred_element_type=f32)
    for r in range(2):
        for q in range(4):
            out_ref[:, row + r * 4 + q, :] = rows[r * DEV : (r + 1) * DEV, q * 128 : (q + 1) * 128]


def pack_kernel(*refs):
    (owner_hbm, density_hbm, lambda_hbm, mu_hbm, order_hbm, orient_hbm, slot_hbm, adj_hbm,
     snap_hbm, out_hbm, meta_ref, owner_ref, floats_ref, ints_ref, hot_ref, block_ref, out_ref,
     row_sem, in_sem, out_sem) = refs
    small = [pltpu.make_async_copy(owner_hbm, owner_ref, row_sem.at[0])]
    for n, source in enumerate((density_hbm, lambda_hbm, mu_hbm)):
        small.append(pltpu.make_async_copy(source, floats_ref.at[n], row_sem.at[1 + n]))
    for n, source in enumerate((order_hbm, orient_hbm, slot_hbm)):
        small.append(pltpu.make_async_copy(source, ints_ref.at[n], row_sem.at[4 + n]))
    arrive = []
    for b in range(BLOCKS):
        source = adj_hbm.at[b] if b < FIELDS else snap_hbm.at[b - FIELDS]
        arrive.append(pltpu.make_async_copy(source, block_ref.at[b], in_sem.at[b]))
    for copy in small + arrive:
        copy.start()
    for copy in small:
        copy.wait()
    for n in range(3):
        meta_ref[n : n + 1, :] = floats_ref[n]
        meta_ref[3 + n : 4 + n, :] = ints_ref[n].astype(f32)
    meta_ref[5:6, :] += 1.0
    meta_ref[6:7, :] = jnp.where(owner_ref[...] == lax.axis_index("dom"), 1.0, 0.0)
    meta_ref[7:8, :] = jnp.zeros((1, NE), f32)
    owner_row = owner_ref[...]
    owner_all = jnp.broadcast_to(owner_row, (NE, NE))
    owner_col = jnp.transpose(owner_all)
    at0 = lax.broadcasted_iota(jnp.int32, (NE, NE), 0)
    at1 = lax.broadcasted_iota(jnp.int32, (NE, NE), 1)
    earlier = jnp.where((owner_col == owner_all) & (at0 < at1), 1.0, 0.0)
    rank = jnp.sum(earlier, axis=0, keepdims=True)
    dest = jnp.where(owner_row != lax.axis_index("dom"), owner_row, -1)
    for r in range(2):
        chosen = (at0 == dest) & (rank == float(r))
        hot_ref[r * DEV : (r + 1) * DEV, :] = jnp.where(chosen, 1.0, 0.0).astype(bf16)

    first_row = lax.broadcasted_iota(jnp.int32, (8, NE), 0) == 0
    leave = []
    for b in range(BLOCKS):
        arrive[b].wait()
        block = block_ref[b]
        if b >= FIELDS:
            n = b - FIELDS
            row = jnp.broadcast_to(meta_ref[n : n + 1, :], (8, NE))
            block = jnp.concatenate([jnp.where(first_row, row, block[0:8]), block[8:]], axis=0)
        scatter_rows(hot_ref[...], block, out_ref, b * 8)
        rows = pl.ds(b * 8, 8)
        leave.append(
            pltpu.make_async_copy(out_ref.at[:, rows, :], out_hbm.at[:, rows, :], out_sem.at[b])
        )
        leave[b].start()
    for copy in leave:
        copy.wait()


def pack(rows, adjoint, snaps):
    return call(
        pack_kernel,
        (*rows, adjoint, snaps),
        [array(DEV, BLOCKS * 8, 128), array(8, NE)],
        [
            pltpu.VMEM((1, NE), jnp.int32),
            pltpu.VMEM((3, 1, NE), f32),
            pltpu.VMEM((3, 1, NE), jnp.int32),
            pltpu.VMEM((2 * DEV, NE), bf16),
            pltpu.VMEM((BLOCKS, NM, NE), f32),
            pltpu.VMEM((DEV, BLOCKS * 8, 128), f32),
            pltpu.SemaphoreType.DMA((7,)),
            pltpu.SemaphoreType.DMA((BLOCKS,)),
            pltpu.SemaphoreType.DMA((BLOCKS,)),
        ],
        hbm=tuple(range(9)),
        hbm_out=(0,),
        limit=63,
    )


def select_slots(pick, slots):
    parts = jnp.concatenate(split3(slots), axis=0)
    picks = jnp.concatenate([pick, pick, pick], axis=1)
    placed = lax.dot_general(picks, parts, (((1,), (0,)), ((), ())), preferred_element_type=f32)
    return jnp.transpose(placed)


def gather_elements(pick, got_ref, row):
    slots = [
        jnp.concatenate([got_ref[:, row + r * 4 + q, :] for q in range(4)], axis=1) for r in range(2)
    ]
    return select_slots(pick, jnp.concatenate(slots, axis=0))


def mode_indices(shape):
    mode = lax.broadcasted_iota(jnp.int32, shape, 0)
    return mode // 64, (mode // 8) % 8, mode % 8


def mask_and_sign(order, orient):
    i, j, k = mode_indices((NM, NE))
    highest = jnp.maximum(jnp.maximum(i, j), k).astype(f32)
    flip_x = (orient == 1.0) | (orient == 3.0)
    flip_y = orient >= 2.0
    sign_x = jnp.where(i % 2 == 1, jnp.where(flip_x, -1.0, 1.0), 1.0)
    sign_y = jnp.where(j % 2 == 1, jnp.where(flip_y, -1.0, 1.0), 1.0)
    return jnp.where(highest <= order, sign_x * sign_y, 0.0)


def odd_device():
    return jnp.full((NP, NE), lax.axis_index("dom"), jnp.int32) % 2 == 1


def face_traces(modes, row):
    low4, low2, even = row < 4, row % 4 < 2, row % 2 == 0
    fours = []
    for j in range(4):
        first, second = modes[j], modes[j + 4]
        other = jnp.where(low4, second, first)
        fours.append(jnp.where(low4, first, second) + pltpu.roll(other, 4, 0))
    twos = []
    for j in range(2):
        first, second = fours[j], fours[j + 2]
        twos.append(
            jnp.where(low2, first + pltpu.roll(first, 6, 0), second + pltpu.roll(second, 2, 0))
        )
    first, second = twos
    next_first, next_second = pltpu.roll(first, 7, 0), pltpu.roll(second, 1, 0)
    upper = jnp.where(even, first + next_first, second + next_second)
    lower = jnp.where(even, first - next_first, next_second - second)
    return upper, lower


def place_kernel(
    meta_ref, got_ref, adj_ref, wave_ref, cross_ref, paired_ref, rows_ref, pick_ref, frame_ref
):
    keep = meta_ref[6:7, :] > 0.5
    odd = odd_device()
    lane = lax.broadcasted_iota(jnp.int32, (DEV, NE), 1)
    columns = []
    for r in range(2):
        column = jnp.zeros((DEV, NE), f32)
        for n in range(SNAPS):
            value = got_ref[:, (FIELDS + n) * 8 + r * 4, 0:1]
            column = jnp.where(lane == n, value, column)
        columns.append(column)
        chosen = jnp.where(column[:, 5:6] == lane.astype(f32) + 1.0, 1.0, 0.0)
        pick_ref[:, r * DEV : (r + 1) * DEV] = jnp.transpose(chosen).astype(bf16)
    arrived = select_slots(pick_ref[...], jnp.concatenate(columns, axis=0))
    meta = jnp.where(keep, meta_ref[...], arrived[0:8])
    density, lam, mu = meta[0:1], meta[1:2], meta[2:3]
    order, orient = meta[3:4], meta[4:5]
    rows_ref[0:1, :] = 1.0 / density
    rows_ref[1:2, :] = lam
    rows_ref[2:3, :] = mu
    rows_ref[3:4, :] = jnp.sqrt((lam + 2.0 * mu) / density)
    rows_ref[4:5, :] = order
    rows_ref[5:6, :] = orient
    rows_ref[6:8, :] = jnp.zeros((2, NE), f32)
    frame_ref[...] = mask_and_sign(order, orient)

    row = lax.broadcasted_iota(jnp.int32, (NP, NE), 0)
    for f in range(FIELDS):
        block = gather_elements(pick_ref[...], got_ref, f * 8)
        wave = jnp.where(keep, adj_ref[f], block) * frame_ref[...]
        wave = wave.reshape(64, NP, NE)
        wave_ref[f] = wave
        for i in range(NP):
            upper, lower = face_traces([wave[i * NP + j] for j in range(NP)], row)
            cross_ref[f, i * NP : (i + 1) * NP, :] = jnp.where(odd, upper, lower)
            paired_ref[f, i * NP : (i + 1) * NP, :] = jnp.where(odd, lower, upper)


def place(meta, got, adjoint):
    return call(
        place_kernel,
        (meta, got, adjoint),
        [
            array(FIELDS, 64, NP, NE),
            array(FIELDS, 64, NE),
            array(FIELDS, 64, NE),
            array(8, NE),
            array(NE, 2 * DEV, dtype=bf16),
            array(NM, NE),
        ],
    )


def materials(rows_ref):
    full = lambda r: jnp.broadcast_to(rows_ref[r : r + 1, :], (NP, NE))
    return full(0), full(1), full(2), full(3)


def apply_b(values, direction, rinv, lam, mu):
    out = [None] * FIELDS
    for c in range(3):
        out[c] = values[VOIGT[c][direction]] * rinv
    spread = lam * values[direction]
    for b in range(3):
        out[3 + b] = spread
    out[3 + direction] = spread + 2.0 * mu * values[direction]
    for c in range(3):
        if c != direction:
            out[VOIGT[c][direction]] = mu * values[c]
    return out


def face_flux(total, difference, direction, rinv, lam, mu, speed):
    even_b = apply_b(difference, direction, rinv, lam, mu)
    odd_b = apply_b(total, direction, rinv, lam, mu)
    even, odd = [], []
    for f in range(FIELDS):
        pen_even, pen_odd = speed * total[f], speed * difference[f]
        if even_b[f] is not None:
            pen_even, pen_odd = pen_even + even_b[f], pen_odd + odd_b[f]
        even.append(-0.25 * pen_even)
        odd.append(-0.25 * pen_odd)
    return even, odd


def local_flux(evens, odds, direction, offset, keep_up, keep_down, rinv, lam, mu, speed):
    total, difference = [], []
    for f in range(FIELDS):
        upper, lower = evens[f] + odds[f], evens[f] - odds[f]
        above = pltpu.roll(lower, NE - offset, 1) * keep_up
        below = pltpu.roll(upper, offset, 1) * keep_down
        total.append((upper - above) + (lower - below))
        difference.append((upper - above) - (lower - below))
    return face_flux(total, difference, direction, rinv, lam, mu, speed)


def lane_keeps():
    lane = lax.broadcasted_iota(jnp.int32, (NP, NE), 1)
    one = lambda cond: jnp.where(cond, 1.0, 0.0)
    column = lane % EX
    return (
        (one(column != EX - 1), one(column != 0)),
        (one(lane < NE - EX), one(lane >= EX)),
    )


def mode_rows():
    k = lax.broadcasted_iota(jnp.int32, (NP, NE), 0)
    one = lambda cond: jnp.where(cond, 1.0, 0.0)
    return one(k < 7), one(k < 6), one(k < 4), (2 * k + 1).astype(f32)


def sums_above(x, keep1, keep2, keep4):
    x = pltpu.roll(x, 7, 0) * keep1
    x = x + pltpu.roll(x, 6, 0) * keep2
    return x + pltpu.roll(x, 4, 0) * keep4


def inner_kernel(wave_ref, rows_ref, out_ref, flux_ref, run_ref, fluxy_ref):
    rinv, lam, mu, speed = materials(rows_ref)
    keeps_x, keeps_y = lane_keeps()
    keep1, keep2, keep4, factor_z = mode_rows()
    run_ref[...] = jnp.zeros_like(run_ref)

    @pl.loop(0, NP)
    def _(g):
        i = NP - 1 - g
        parity = lax.rem(i, 2)
        factor_x = (2 * i + 1).astype(f32)

        evens, odds = [], []
        for f in range(FIELDS):
            col = [wave_ref[f, i * NP + j] for j in range(NP)]
            evens.append((col[0] + col[2]) + (col[4] + col[6]))
            odds.append((col[1] + col[3]) + (col[5] + col[7]))
        even, odd = local_flux(evens, odds, 1, EX, *keeps_y, rinv, lam, mu, speed)
        for f in range(FIELDS):
            fluxy_ref[0, f] = even[f]
            fluxy_ref[1, f] = odd[f]

        sums_y = {f: [None, None] for f in ACTIVE[1]}
        for j in range(NP - 1, -1, -1):
            here = [wave_ref[f, i * NP + j] for f in range(FIELDS)]
            slope = [{}, {}, {}]
            for f in ACTIVE[0]:
                slope[0][f] = factor_x * run_ref[parity, f, j]
            for f in ACTIVE[1]:
                if sums_y[f][j % 2] is not None:
                    slope[1][f] = (2.0 * j + 1.0) * sums_y[f][j % 2]
            for f in ACTIVE[2]:
                slope[2][f] = factor_z * sums_above(here[f], keep1, keep2, keep4)

            def total(pairs):
                found = [slope[a][f] for a, f in pairs if f in slope[a]]
                result = found[0]
                for item in found[1:]:
                    result = result + item
                return result

            result = [None] * FIELDS
            for c in range(3):
                result[c] = rinv * total([(a, VOIGT[c][a]) for a in range(3)])
            spread = lam * total([(a, a) for a in range(3)])
            for b in range(3):
                if b in slope[b]:
                    result[3 + b] = spread + 2.0 * mu * slope[b][b]
                else:
                    result[3 + b] = spread
            for b, c in ((1, 2), (0, 2), (0, 1)):
                result[VOIGT[b][c]] = mu * total([(b, c), (c, b)])
            for f in range(FIELDS):
                out_ref[f, i * NP + j] = result[f] + (2.0 * j + 1.0) * fluxy_ref[j % 2, f]

            for f in ACTIVE[1]:
                before = sums_y[f][1 - j % 2]
                sums_y[f][1 - j % 2] = here[f] if before is None else before + here[f]
            for f in range(FIELDS):
                run_ref[1 - parity, f, j] += here[f]

    @pl.loop(0, NP)
    def _(j):
        even_x, odd_x = local_flux(
            [run_ref[1, f, j] for f in range(FIELDS)],
            [run_ref[0, f, j] for f in range(FIELDS)],
            0, 1, *keeps_x, rinv, lam, mu, speed,
        )
        for f in range(FIELDS):
            flux_ref[0, f, j] = even_x[f]
            flux_ref[1, f, j] = odd_x[f]


def inner(wave, rows):
    return call(
        inner_kernel,
        (wave, rows),
        [array(FIELDS, 64, NP, NE), array(2, FIELDS, NP, NP, NE)],
        [pltpu.VMEM((2, FIELDS, NP, NP, NE), f32), pltpu.VMEM((2, FIELDS, NP, NE), f32)],
    )


def update_kernel(last, half, *refs):
    refs = list(refs)
    base_ref = refs.pop(0) if half else None
    (wave_ref, part_ref, flux_ref, cross_ref, paired_ref, got_cross_ref, got_paired_ref,
     rows_ref, *rest) = refs
    if last:
        strain_ref, first_ref, out_ref, gradient_ref, fluxz_ref, sums_ref = rest
        sums_ref[...] = jnp.zeros_like(sums_ref)
    else:
        out_ref, out_cross_ref, out_paired_ref, fluxz_ref = rest
    rinv, lam, mu, speed = materials(rows_ref)
    order = jnp.broadcast_to(rows_ref[4:5, :], (NP, NE))
    orient = jnp.broadcast_to(rows_ref[5:6, :], (NP, NE))
    odd = odd_device()
    side = jnp.where(odd, 1.0, -1.0)
    k = lax.broadcasted_iota(jnp.int32, (NP, NE), 0)
    k_even = k % 2 == 0
    factor_z = (2 * k + 1).astype(f32)
    step = 0.5 * DT if half else DT

    @pl.loop(0, NP)
    def _(i):
        parity = lax.rem(i, 2)
        factor_x = (2 * i + 1).astype(f32)
        at = pl.multiple_of(i * NP, NP)
        rows = pl.ds(at, NP)
        total, difference = [], []
        for f in range(FIELDS):
            jump_cross = cross_ref[f, rows] - got_cross_ref[f, rows]
            jump_paired = paired_ref[f, rows] - got_paired_ref[f, rows]
            total.append(jump_cross + jump_paired)
            difference.append(side * (jump_cross - jump_paired))
        even, odds = face_flux(total, difference, 2, rinv, lam, mu, speed)
        for f in range(FIELDS):
            fluxz_ref[0, f] = even[f]
            fluxz_ref[1, f] = odds[f]

        masks = []
        for j in range(NP):
            highest = jnp.maximum(k, jnp.maximum(i, j)).astype(f32)
            masks.append(jnp.where(highest <= order, step, 0.0))
        if last:
            flip_x = ((orient == 1.0) | (orient == 3.0)) & (parity == 1)
            sign_x = jnp.where(flip_x, -1.0, 1.0)
            sign_y = jnp.where(orient >= 2.0, -1.0, 1.0)
            signs = [sign_x, sign_x * sign_y]
            stresses = [[] for _ in range(NP)]

        for f in range(FIELDS):
            fresh = []
            for j in range(NP):
                lifted = jnp.where(
                    k_even,
                    jnp.broadcast_to(fluxz_ref[0, f, j : j + 1, :], (NP, NE)),
                    jnp.broadcast_to(fluxz_ref[1, f, j : j + 1, :], (NP, NE)),
                )
                slope = part_ref[f, at + j] + factor_x * flux_ref[parity, f, j] + factor_z * lifted
                start = wave_ref[f, at + j]
                if half:
                    start = 0.5 * (base_ref[f, at + j] + start)
                new = start + masks[j] * slope
                if last:
                    out_ref[f, at + j] = new * signs[j % 2]
                    if f >= 3:
                        stresses[j].append(new)
                else:
                    out_ref[f, at + j] = new
                fresh.append(new)
            if not last:
                upper, lower = face_traces(fresh, k)
                out_cross_ref[f, rows] = jnp.where(odd, upper, lower)
                out_paired_ref[f, rows] = jnp.where(odd, lower, upper)
        if last:
            for j in range(NP):
                add_gradient(sums_ref, stresses[j], [strain_ref[f, at + j] for f in range(6)])

    if last:
        gradient_ref[...] = first_ref[...] + gradient_rows(sums_ref)


def update(base, wave, part, flux, traces, got, rows, last=None):
    half = base is not None
    whole, trace = array(FIELDS, 64, NP, NE), array(FIELDS, 64, NE)
    operands = ([base] if half else []) + [wave, part, flux, *traces, *got, rows]
    scratch = [pltpu.VMEM((2, FIELDS, NP, NE), f32)]
    out = [whole, trace, trace]
    if last is not None:
        operands += list(last)
        scratch.append(pltpu.VMEM((2, NP, NE), f32))
        out = [whole, array(2, NE)]

    def kernel(*refs):
        update_kernel(last is not None, half, *refs)

    return call(kernel, operands, out, scratch)


def add_gradient(sums_ref, stress, strain):
    normal = (stress[0] + stress[1]) + stress[2]
    sums_ref[0] += normal * ((strain[0] + strain[1]) + strain[2])
    shear = stress[0] * strain[0]
    for f in range(1, 6):
        shear = shear + stress[f] * strain[f]
    sums_ref[1] += shear


def gradient_rows(sums_ref):
    first = (0.5 * DT) * jnp.sum(sums_ref[0], axis=0, keepdims=True)
    second = DT * jnp.sum(sums_ref[1], axis=0, keepdims=True)
    return jnp.concatenate([first, second], axis=0)


def velocity_kernel(second, meta_ref, pick_ref, frame_ref, *refs):
    if second:
        snap_ref, got_ref, strain_ref, *rest = refs
    else:
        wave_ref, snap_ref, got_ref, gradient_ref, *rest = refs
    vel_ref, run_ref, sums_ref = rest
    start = 3 if second else 0
    keep = meta_ref[6:7, :] > 0.5
    row = lax.broadcasted_iota(jnp.int32, (8, NE), 0)
    keep1, keep2, keep4, factor_z = mode_rows()
    weight_z = 2.0 / factor_z
    sums_ref[...] = jnp.zeros_like(sums_ref)

    def settle(c):
        block = gather_elements(pick_ref[...], got_ref, (FIELDS + start + c) * 8)
        block = jnp.concatenate([jnp.where(row == 0, 0.0, block[0:8]), block[8:]], axis=0)
        velocity = jnp.where(keep, snap_ref[start + c], block) * frame_ref[...]
        vel_ref[c] = velocity.reshape(64, NP, NE)

    def strains(use):
        run_ref[...] = jnp.zeros_like(run_ref)

        @pl.loop(0, NP)
        def _(g):
            i = NP - 1 - g
            parity = lax.rem(i, 2)
            at = pl.multiple_of(i * NP, NP)
            weight_x = 2.0 / jnp.full((NP, NE), 2 * i + 1, jnp.int32).astype(f32)
            weight_xz = 2.0 * weight_x * weight_z
            zero = jnp.zeros((NP, NE), f32)
            run_y = [[zero, zero] for _ in range(3)]
            for j in range(NP - 1, -1, -1):
                weight_y = 2.0 / (2.0 * j + 1.0)
                slopes = []
                for c in range(3):
                    here = vel_ref[c, at + j]
                    slopes.append([
                        (2.0 * weight_y) * (weight_z * run_ref[parity, c, j]),
                        weight_xz * run_y[c][j % 2],
                        (2.0 * weight_y) * (weight_x * sums_above(here, keep1, keep2, keep4)),
                    ])
                    run_y[c][1 - j % 2] = run_y[c][1 - j % 2] + here
                    run_ref[1 - parity, c, j] += here
                use(at + j, [
                    2.0 * slopes[0][0], 2.0 * slopes[1][1], 2.0 * slopes[2][2],
                    slopes[2][1] + slopes[1][2], slopes[2][0] + slopes[0][2],
                    slopes[1][0] + slopes[0][1],
                ])

    for c in range(3):
        settle(c)
    if second:

        def keep_strains(at, strain):
            for f in range(6):
                strain_ref[f, at] = strain[f]

        strains(keep_strains)
    else:
        strains(
            lambda at, strain: add_gradient(
                sums_ref, [wave_ref[3 + f, at] for f in range(6)], strain
            )
        )
        gradient_ref[...] = gradient_rows(sums_ref)


def velocities(meta, pick, frame, wave, snaps, got):
    second = wave is None
    operands = [meta, pick, frame] + ([] if second else [wave]) + [snaps, got]

    def kernel(*refs):
        velocity_kernel(second, *refs)

    (result,) = call(
        kernel,
        operands,
        [array(6, 64, NP, NE) if second else array(2, NE)],
        [
            pltpu.VMEM((3, 64, NP, NE), f32),
            pltpu.VMEM((2, 3, NP, NP, NE), f32),
            pltpu.VMEM((2, NP, NE), f32),
        ],
    )
    return result


def exchange(send):
    return lax.all_to_all(send, "dom", split_axis=0, concat_axis=0, tiled=True)


def swap_traces(cross, paired):
    ups = [(d, d + 1) for d in range(1, DEV - 1, 2)]
    pairs = [(d, d + 1) for d in range(0, DEV, 2)]
    both = lambda steps: steps + [(b, a) for a, b in steps]
    return lax.ppermute(cross, "dom", both(ups)), lax.ppermute(paired, "dom", both(pairs))


def body(
    adjoint, snapshots, density, lame_lambda, lame_mu, element_order, orient, new_owner, new_slot
):
    rows = [
        x.reshape(1, NE)
        for x in (new_owner, density, lame_lambda, lame_mu, element_order, orient, new_slot)
    ]
    snaps = snapshots.reshape(SNAPS, NM, NE)
    send, meta = pack(rows, adjoint, snaps)
    got = lax.all_to_all(send, "dom", split_axis=0, concat_axis=0, tiled=True)
    wave, *traces, rows, pick, frame = place(meta, got, adjoint)
    stage = 0
    for step in range(STEPS):
        start = wave
        for half in (False, True):
            outer = swap_traces(*traces)
            part, flux = inner(wave, rows)
            base = start if half else None
            if stage == 2:
                strain = velocities(meta, pick, frame, None, snaps, got)
                part, strain = lax.optimization_barrier((part, strain))
            if stage == 3:
                first = velocities(meta, pick, frame, start, snaps, got)
                signed, gradients = update(
                    base, wave, part, flux, traces, outer, rows, (strain, first)
                )
            else:
                wave, *traces = update(base, wave, part, flux, traces, outer, rows)
            stage += 1
    return signed.reshape(FIELDS, NM, NE), gradients


def solution(mesh):
    shard = P("dom")
    in_specs = (P(None, None, "dom"), P(None, None, None, "dom")) + (shard,) * 7
    out_specs = (P(None, None, "dom"), P(None, "dom"))
    return jax.shard_map(body, mesh=mesh, in_specs=in_specs, out_specs=out_specs, check_vma=False)
```

```python
import jax
import jax.numpy as jnp
from jax import lax
from jax.experimental import pallas as pl
from jax.experimental.pallas import tpu as pltpu
from jax.sharding import PartitionSpec as P

NP = 8
NM = 512
EX = 8
NE = 128
STEPS = 2
DEV = 128
FIELDS = 9
SNAPS = 6
BLOCKS = FIELDS + SNAPS
DT = 0.01
f32 = jnp.float32
bf16 = jnp.bfloat16

VOIGT = ((3, 8, 7), (8, 4, 6), (7, 6, 5))
ACTIVE = tuple((0, 1, 2) + VOIGT[a] for a in range(3))


def split3(x):
    high = x.astype(bf16)
    rest = x - high.astype(f32)
    middle = rest.astype(bf16)
    low = (rest - middle.astype(f32)).astype(bf16)
    return high, middle, low


def call(kernel, operands, out_shape, scratch_shapes=(), hbm=(), hbm_out=(), limit=16):
    def space(position, x):
        return pltpu.HBM if position in hbm else pltpu.VMEM

    return pl.pallas_call(
        kernel,
        in_specs=[pl.BlockSpec(memory_space=space(n, x)) for n, x in enumerate(operands)],
        out_specs=[
            pl.BlockSpec(memory_space=pltpu.HBM if n in hbm_out else pltpu.VMEM)
            for n in range(len(out_shape))
        ],
        out_shape=out_shape,
        scratch_shapes=list(scratch_shapes),
        compiler_params=pltpu.CompilerParams(vmem_limit_bytes=limit * 1024 * 1024),
        cost_estimate=pl.CostEstimate(flops=0, bytes_accessed=0, transcendentals=0),
    )(*operands)


def array(*shape, dtype=f32):
    return jax.ShapeDtypeStruct(shape, dtype)


def scatter_rows(hot, x, out_ref, row):
    parts = jnp.concatenate(split3(x), axis=1)
    hots = jnp.concatenate([hot, hot, hot], axis=1)
    rows = lax.dot_general(hots, parts, (((1,), (1,)), ((), ())), preferred_element_type=f32)
    groups = [
        rows[r * DEV : (r + 1) * DEV, q * 128 : (q + 1) * 128].reshape(DEV // 8, 8, 128)
        for r in range(2)
        for q in range(4)
    ]
    tiles = jnp.swapaxes(jnp.stack(groups, axis=1), 1, 2)
    out_ref[:, row : row + 8, :] = tiles.reshape(DEV, 8, 128)


def pack_kernel(*refs):
    (owner_hbm, density_hbm, lambda_hbm, mu_hbm, order_hbm, orient_hbm, slot_hbm, adj_hbm,
     snap_hbm, out_hbm, meta_ref, owner_ref, floats_ref, ints_ref, hot_ref, block_ref, out_ref,
     row_sem, in_sem, out_sem) = refs
    small = [pltpu.make_async_copy(owner_hbm, owner_ref, row_sem.at[0])]
    for n, source in enumerate((density_hbm, lambda_hbm, mu_hbm)):
        small.append(pltpu.make_async_copy(source, floats_ref.at[n], row_sem.at[1 + n]))
    for n, source in enumerate((order_hbm, orient_hbm, slot_hbm)):
        small.append(pltpu.make_async_copy(source, ints_ref.at[n], row_sem.at[4 + n]))
    arrive = []
    for b in range(BLOCKS):
        source = adj_hbm.at[b] if b < FIELDS else snap_hbm.at[b - FIELDS]
        arrive.append(pltpu.make_async_copy(source, block_ref.at[b], in_sem.at[b]))
    for copy in small + arrive:
        copy.start()
    for copy in small:
        copy.wait()
    for n in range(3):
        meta_ref[n : n + 1, :] = floats_ref[n]
        meta_ref[3 + n : 4 + n, :] = ints_ref[n].astype(f32)
    meta_ref[5:6, :] += 1.0
    meta_ref[6:7, :] = jnp.where(owner_ref[...] == lax.axis_index("dom"), 1.0, 0.0)
    meta_ref[7:8, :] = jnp.zeros((1, NE), f32)
    owner_row = owner_ref[...]
    owner_all = jnp.broadcast_to(owner_row, (NE, NE))
    owner_col = jnp.transpose(owner_all)
    at0 = lax.broadcasted_iota(jnp.int32, (NE, NE), 0)
    at1 = lax.broadcasted_iota(jnp.int32, (NE, NE), 1)
    earlier = jnp.where((owner_col == owner_all) & (at0 < at1), 1.0, 0.0)
    rank = jnp.sum(earlier, axis=0, keepdims=True)
    dest = jnp.where(owner_row != lax.axis_index("dom"), owner_row, -1)
    for r in range(2):
        chosen = (at0 == dest) & (rank == float(r))
        hot_ref[r * DEV : (r + 1) * DEV, :] = jnp.where(chosen, 1.0, 0.0).astype(bf16)

    first_row = lax.broadcasted_iota(jnp.int32, (8, NE), 0) == 0
    leave = []
    for b in range(BLOCKS):
        arrive[b].wait()
        block = block_ref[b]
        if b >= FIELDS:
            n = b - FIELDS
            row = jnp.broadcast_to(meta_ref[n : n + 1, :], (8, NE))
            block = jnp.concatenate([jnp.where(first_row, row, block[0:8]), block[8:]], axis=0)
        scatter_rows(hot_ref[...], block, out_ref, b * 8)
        rows = pl.ds(b * 8, 8)
        leave.append(
            pltpu.make_async_copy(out_ref.at[:, rows, :], out_hbm.at[:, rows, :], out_sem.at[b])
        )
        leave[b].start()
    for copy in leave:
        copy.wait()


def pack(rows, adjoint, snaps):
    return call(
        pack_kernel,
        (*rows, adjoint, snaps),
        [array(DEV, BLOCKS * 8, 128), array(8, NE)],
        [
            pltpu.VMEM((1, NE), jnp.int32),
            pltpu.VMEM((3, 1, NE), f32),
            pltpu.VMEM((3, 1, NE), jnp.int32),
            pltpu.VMEM((2 * DEV, NE), bf16),
            pltpu.VMEM((BLOCKS, NM, NE), f32),
            pltpu.VMEM((DEV, BLOCKS * 8, 128), f32),
            pltpu.SemaphoreType.DMA((7,)),
            pltpu.SemaphoreType.DMA((BLOCKS,)),
            pltpu.SemaphoreType.DMA((BLOCKS,)),
        ],
        hbm=tuple(range(9)),
        hbm_out=(0,),
        limit=63,
    )


def select_slots(pick, slots):
    parts = jnp.concatenate(split3(slots), axis=0)
    picks = jnp.concatenate([pick, pick, pick], axis=1)
    placed = lax.dot_general(picks, parts, (((1,), (0,)), ((), ())), preferred_element_type=f32)
    return jnp.transpose(placed)


def gather_elements(pick, got_ref, row):
    tiles = jnp.swapaxes(got_ref[:, row : row + 8, :].reshape(DEV // 8, 8, 8, 128), 1, 2)
    rows = [tiles[:, n].reshape(DEV, 128) for n in range(8)]
    slots = [jnp.concatenate(rows[4 * r : 4 * r + 4], axis=1) for r in range(2)]
    return select_slots(pick, jnp.concatenate(slots, axis=0))


def mode_indices(shape):
    mode = lax.broadcasted_iota(jnp.int32, shape, 0)
    return mode // 64, (mode // 8) % 8, mode % 8


def mask_and_sign(order, orient):
    i, j, k = mode_indices((NM, NE))
    highest = jnp.maximum(jnp.maximum(i, j), k).astype(f32)
    flip_x = (orient == 1.0) | (orient == 3.0)
    flip_y = orient >= 2.0
    sign_x = jnp.where(i % 2 == 1, jnp.where(flip_x, -1.0, 1.0), 1.0)
    sign_y = jnp.where(j % 2 == 1, jnp.where(flip_y, -1.0, 1.0), 1.0)
    return jnp.where(highest <= order, sign_x * sign_y, 0.0)


def odd_device():
    return jnp.full((NP, NE), lax.axis_index("dom"), jnp.int32) % 2 == 1


def face_traces(modes, row):
    low4, low2, even = row < 4, row % 4 < 2, row % 2 == 0
    fours = []
    for j in range(4):
        first, second = modes[j], modes[j + 4]
        other = jnp.where(low4, second, first)
        fours.append(jnp.where(low4, first, second) + pltpu.roll(other, 4, 0))
    twos = []
    for j in range(2):
        first, second = fours[j], fours[j + 2]
        twos.append(
            jnp.where(low2, first + pltpu.roll(first, 6, 0), second + pltpu.roll(second, 2, 0))
        )
    first, second = twos
    next_first, next_second = pltpu.roll(first, 7, 0), pltpu.roll(second, 1, 0)
    upper = jnp.where(even, first + next_first, second + next_second)
    lower = jnp.where(even, first - next_first, next_second - second)
    return upper, lower


def place_kernel(
    meta_ref, got_ref, adj_ref, wave_ref, cross_ref, paired_ref, rows_ref, pick_ref, frame_ref
):
    keep = meta_ref[6:7, :] > 0.5
    odd = odd_device()
    lane = lax.broadcasted_iota(jnp.int32, (DEV, NE), 1)
    columns = []
    for r in range(2):
        column = jnp.zeros((DEV, NE), f32)
        for n in range(SNAPS):
            value = got_ref[:, (FIELDS + n) * 8 + r * 4, 0:1]
            column = jnp.where(lane == n, value, column)
        columns.append(column)
        chosen = jnp.where(column[:, 5:6] == lane.astype(f32) + 1.0, 1.0, 0.0)
        pick_ref[:, r * DEV : (r + 1) * DEV] = jnp.transpose(chosen).astype(bf16)
    arrived = select_slots(pick_ref[...], jnp.concatenate(columns, axis=0))
    meta = jnp.where(keep, meta_ref[...], arrived[0:8])
    density, lam, mu = meta[0:1], meta[1:2], meta[2:3]
    order, orient = meta[3:4], meta[4:5]
    rows_ref[0:1, :] = 1.0 / density
    rows_ref[1:2, :] = lam
    rows_ref[2:3, :] = mu
    rows_ref[3:4, :] = jnp.sqrt((lam + 2.0 * mu) / density)
    rows_ref[4:5, :] = order
    rows_ref[5:6, :] = orient
    rows_ref[6:8, :] = jnp.zeros((2, NE), f32)
    frame_ref[...] = mask_and_sign(order, orient)

    row = lax.broadcasted_iota(jnp.int32, (NP, NE), 0)
    for f in range(FIELDS):
        block = gather_elements(pick_ref[...], got_ref, f * 8)
        wave = jnp.where(keep, adj_ref[f], block) * frame_ref[...]
        wave = wave.reshape(64, NP, NE)
        wave_ref[f] = wave
        for i in range(NP):
            upper, lower = face_traces([wave[i * NP + j] for j in range(NP)], row)
            cross_ref[f, i * NP : (i + 1) * NP, :] = jnp.where(odd, upper, lower)
            paired_ref[f, i * NP : (i + 1) * NP, :] = jnp.where(odd, lower, upper)


def place(meta, got, adjoint):
    return call(
        place_kernel,
        (meta, got, adjoint),
        [
            array(FIELDS, 64, NP, NE),
            array(FIELDS, 64, NE),
            array(FIELDS, 64, NE),
            array(8, NE),
            array(NE, 2 * DEV, dtype=bf16),
            array(NM, NE),
        ],
    )


def materials(rows_ref):
    full = lambda r: jnp.broadcast_to(rows_ref[r : r + 1, :], (NP, NE))
    return full(0), full(1), full(2), full(3)


def apply_b(values, direction, rinv, lam, mu):
    out = [None] * FIELDS
    for c in range(3):
        out[c] = values[VOIGT[c][direction]] * rinv
    spread = lam * values[direction]
    for b in range(3):
        out[3 + b] = spread
    out[3 + direction] = spread + 2.0 * mu * values[direction]
    for c in range(3):
        if c != direction:
            out[VOIGT[c][direction]] = mu * values[c]
    return out


def face_flux(total, difference, direction, rinv, lam, mu, speed):
    even_b = apply_b(difference, direction, rinv, lam, mu)
    odd_b = apply_b(total, direction, rinv, lam, mu)
    even, odd = [], []
    for f in range(FIELDS):
        pen_even, pen_odd = speed * total[f], speed * difference[f]
        if even_b[f] is not None:
            pen_even, pen_odd = pen_even + even_b[f], pen_odd + odd_b[f]
        even.append(-0.25 * pen_even)
        odd.append(-0.25 * pen_odd)
    return even, odd


def local_flux(evens, odds, direction, offset, keep_up, keep_down, rinv, lam, mu, speed):
    total, difference = [], []
    for f in range(FIELDS):
        upper, lower = evens[f] + odds[f], evens[f] - odds[f]
        above = pltpu.roll(lower, NE - offset, 1) * keep_up
        below = pltpu.roll(upper, offset, 1) * keep_down
        total.append((upper - above) + (lower - below))
        difference.append((upper - above) - (lower - below))
    return face_flux(total, difference, direction, rinv, lam, mu, speed)


def lane_keeps():
    lane = lax.broadcasted_iota(jnp.int32, (NP, NE), 1)
    one = lambda cond: jnp.where(cond, 1.0, 0.0)
    column = lane % EX
    return (
        (one(column != EX - 1), one(column != 0)),
        (one(lane < NE - EX), one(lane >= EX)),
    )


def mode_rows():
    k = lax.broadcasted_iota(jnp.int32, (NP, NE), 0)
    one = lambda cond: jnp.where(cond, 1.0, 0.0)
    return one(k < 7), one(k < 6), one(k < 4), (2 * k + 1).astype(f32)


def sums_above(x, keep1, keep2, keep4):
    x = pltpu.roll(x, 7, 0) * keep1
    x = x + pltpu.roll(x, 6, 0) * keep2
    return x + pltpu.roll(x, 4, 0) * keep4


def inner_kernel(wave_ref, rows_ref, out_ref, flux_ref, run_ref, fluxy_ref):
    rinv, lam, mu, speed = materials(rows_ref)
    keeps_x, keeps_y = lane_keeps()
    keep1, keep2, keep4, factor_z = mode_rows()
    run_ref[...] = jnp.zeros_like(run_ref)

    @pl.loop(0, NP)
    def _(g):
        i = NP - 1 - g
        parity = lax.rem(i, 2)
        factor_x = (2 * i + 1).astype(f32)

        evens, odds = [], []
        for f in range(FIELDS):
            col = [wave_ref[f, i * NP + j] for j in range(NP)]
            evens.append((col[0] + col[2]) + (col[4] + col[6]))
            odds.append((col[1] + col[3]) + (col[5] + col[7]))
        even, odd = local_flux(evens, odds, 1, EX, *keeps_y, rinv, lam, mu, speed)
        for f in range(FIELDS):
            fluxy_ref[0, f] = even[f]
            fluxy_ref[1, f] = odd[f]

        sums_y = {f: [None, None] for f in ACTIVE[1]}
        for j in range(NP - 1, -1, -1):
            here = [wave_ref[f, i * NP + j] for f in range(FIELDS)]
            slope = [{}, {}, {}]
            for f in ACTIVE[0]:
                slope[0][f] = factor_x * run_ref[parity, f, j]
            for f in ACTIVE[1]:
                if sums_y[f][j % 2] is not None:
                    slope[1][f] = (2.0 * j + 1.0) * sums_y[f][j % 2]
            for f in ACTIVE[2]:
                slope[2][f] = factor_z * sums_above(here[f], keep1, keep2, keep4)

            def total(pairs):
                found = [slope[a][f] for a, f in pairs if f in slope[a]]
                result = found[0]
                for item in found[1:]:
                    result = result + item
                return result

            result = [None] * FIELDS
            for c in range(3):
                result[c] = rinv * total([(a, VOIGT[c][a]) for a in range(3)])
            spread = lam * total([(a, a) for a in range(3)])
            for b in range(3):
                if b in slope[b]:
                    result[3 + b] = spread + 2.0 * mu * slope[b][b]
                else:
                    result[3 + b] = spread
            for b, c in ((1, 2), (0, 2), (0, 1)):
                result[VOIGT[b][c]] = mu * total([(b, c), (c, b)])
            for f in range(FIELDS):
                out_ref[f, i * NP + j] = result[f] + (2.0 * j + 1.0) * fluxy_ref[j % 2, f]

            for f in ACTIVE[1]:
                before = sums_y[f][1 - j % 2]
                sums_y[f][1 - j % 2] = here[f] if before is None else before + here[f]
            for f in range(FIELDS):
                run_ref[1 - parity, f, j] += here[f]

    @pl.loop(0, NP)
    def _(j):
        even_x, odd_x = local_flux(
            [run_ref[1, f, j] for f in range(FIELDS)],
            [run_ref[0, f, j] for f in range(FIELDS)],
            0, 1, *keeps_x, rinv, lam, mu, speed,
        )
        for f in range(FIELDS):
            flux_ref[0, f, j] = even_x[f]
            flux_ref[1, f, j] = odd_x[f]


def inner(wave, rows):
    return call(
        inner_kernel,
        (wave, rows),
        [array(FIELDS, 64, NP, NE), array(2, FIELDS, NP, NP, NE)],
        [pltpu.VMEM((2, FIELDS, NP, NP, NE), f32), pltpu.VMEM((2, FIELDS, NP, NE), f32)],
    )


def update_kernel(last, half, *refs):
    refs = list(refs)
    base_ref = refs.pop(0) if half else None
    (wave_ref, part_ref, flux_ref, cross_ref, paired_ref, got_cross_ref, got_paired_ref,
     rows_ref, *rest) = refs
    if last:
        strain_ref, first_ref, out_ref, gradient_ref, fluxz_ref, sums_ref = rest
        sums_ref[...] = jnp.zeros_like(sums_ref)
    else:
        out_ref, out_cross_ref, out_paired_ref, fluxz_ref = rest
    rinv, lam, mu, speed = materials(rows_ref)
    order = jnp.broadcast_to(rows_ref[4:5, :], (NP, NE))
    orient = jnp.broadcast_to(rows_ref[5:6, :], (NP, NE))
    odd = odd_device()
    side = jnp.where(odd, 1.0, -1.0)
    k = lax.broadcasted_iota(jnp.int32, (NP, NE), 0)
    k_even = k % 2 == 0
    factor_z = (2 * k + 1).astype(f32)
    step = 0.5 * DT if half else DT

    @pl.loop(0, NP)
    def _(i):
        parity = lax.rem(i, 2)
        factor_x = (2 * i + 1).astype(f32)
        at = pl.multiple_of(i * NP, NP)
        rows = pl.ds(at, NP)
        total, difference = [], []
        for f in range(FIELDS):
            jump_cross = cross_ref[f, rows] - got_cross_ref[f, rows]
            jump_paired = paired_ref[f, rows] - got_paired_ref[f, rows]
            total.append(jump_cross + jump_paired)
            difference.append(side * (jump_cross - jump_paired))
        even, odds = face_flux(total, difference, 2, rinv, lam, mu, speed)
        for f in range(FIELDS):
            fluxz_ref[0, f] = even[f]
            fluxz_ref[1, f] = odds[f]

        masks = []
        for j in range(NP):
            highest = jnp.maximum(k, jnp.maximum(i, j)).astype(f32)
            masks.append(jnp.where(highest <= order, step, 0.0))
        if last:
            flip_x = ((orient == 1.0) | (orient == 3.0)) & (parity == 1)
            sign_x = jnp.where(flip_x, -1.0, 1.0)
            sign_y = jnp.where(orient >= 2.0, -1.0, 1.0)
            signs = [sign_x, sign_x * sign_y]
            stresses = [[] for _ in range(NP)]

        for f in range(FIELDS):
            fresh = []
            for j in range(NP):
                lifted = jnp.where(
                    k_even,
                    jnp.broadcast_to(fluxz_ref[0, f, j : j + 1, :], (NP, NE)),
                    jnp.broadcast_to(fluxz_ref[1, f, j : j + 1, :], (NP, NE)),
                )
                slope = part_ref[f, at + j] + factor_x * flux_ref[parity, f, j] + factor_z * lifted
                start = wave_ref[f, at + j]
                if half:
                    start = 0.5 * (base_ref[f, at + j] + start)
                new = start + masks[j] * slope
                if last:
                    out_ref[f, at + j] = new * signs[j % 2]
                    if f >= 3:
                        stresses[j].append(new)
                else:
                    out_ref[f, at + j] = new
                fresh.append(new)
            if not last:
                upper, lower = face_traces(fresh, k)
                out_cross_ref[f, rows] = jnp.where(odd, upper, lower)
                out_paired_ref[f, rows] = jnp.where(odd, lower, upper)
        if last:
            for j in range(NP):
                add_gradient(sums_ref, stresses[j], [strain_ref[f, at + j] for f in range(6)])

    if last:
        gradient_ref[...] = first_ref[...] + gradient_rows(sums_ref)


def update(base, wave, part, flux, traces, got, rows, last=None):
    half = base is not None
    whole, trace = array(FIELDS, 64, NP, NE), array(FIELDS, 64, NE)
    operands = ([base] if half else []) + [wave, part, flux, *traces, *got, rows]
    scratch = [pltpu.VMEM((2, FIELDS, NP, NE), f32)]
    out = [whole, trace, trace]
    if last is not None:
        operands += list(last)
        scratch.append(pltpu.VMEM((2, NP, NE), f32))
        out = [whole, array(2, NE)]

    def kernel(*refs):
        update_kernel(last is not None, half, *refs)

    return call(kernel, operands, out, scratch)


def add_gradient(sums_ref, stress, strain):
    normal = (stress[0] + stress[1]) + stress[2]
    sums_ref[0] += normal * ((strain[0] + strain[1]) + strain[2])
    shear = stress[0] * strain[0]
    for f in range(1, 6):
        shear = shear + stress[f] * strain[f]
    sums_ref[1] += shear


def gradient_rows(sums_ref):
    first = (0.5 * DT) * jnp.sum(sums_ref[0], axis=0, keepdims=True)
    second = DT * jnp.sum(sums_ref[1], axis=0, keepdims=True)
    return jnp.concatenate([first, second], axis=0)


def velocity_kernel(second, meta_ref, pick_ref, frame_ref, *refs):
    if second:
        snap_ref, got_ref, strain_ref, *rest = refs
    else:
        wave_ref, snap_ref, got_ref, gradient_ref, *rest = refs
    vel_ref, run_ref, sums_ref = rest
    start = 3 if second else 0
    keep = meta_ref[6:7, :] > 0.5
    row = lax.broadcasted_iota(jnp.int32, (8, NE), 0)
    keep1, keep2, keep4, factor_z = mode_rows()
    weight_z = 2.0 / factor_z
    sums_ref[...] = jnp.zeros_like(sums_ref)

    def settle(c):
        block = gather_elements(pick_ref[...], got_ref, (FIELDS + start + c) * 8)
        block = jnp.concatenate([jnp.where(row == 0, 0.0, block[0:8]), block[8:]], axis=0)
        velocity = jnp.where(keep, snap_ref[start + c], block) * frame_ref[...]
        vel_ref[c] = velocity.reshape(64, NP, NE)

    def strains(use):
        run_ref[...] = jnp.zeros_like(run_ref)

        @pl.loop(0, NP)
        def _(g):
            i = NP - 1 - g
            parity = lax.rem(i, 2)
            at = pl.multiple_of(i * NP, NP)
            weight_x = 2.0 / jnp.full((NP, NE), 2 * i + 1, jnp.int32).astype(f32)
            weight_xz = 2.0 * weight_x * weight_z
            zero = jnp.zeros((NP, NE), f32)
            run_y = [[zero, zero] for _ in range(3)]
            for j in range(NP - 1, -1, -1):
                weight_y = 2.0 / (2.0 * j + 1.0)
                slopes = []
                for c in range(3):
                    here = vel_ref[c, at + j]
                    slopes.append([
                        (2.0 * weight_y) * (weight_z * run_ref[parity, c, j]),
                        weight_xz * run_y[c][j % 2],
                        (2.0 * weight_y) * (weight_x * sums_above(here, keep1, keep2, keep4)),
                    ])
                    run_y[c][1 - j % 2] = run_y[c][1 - j % 2] + here
                    run_ref[1 - parity, c, j] += here
                use(at + j, [
                    2.0 * slopes[0][0], 2.0 * slopes[1][1], 2.0 * slopes[2][2],
                    slopes[2][1] + slopes[1][2], slopes[2][0] + slopes[0][2],
                    slopes[1][0] + slopes[0][1],
                ])

    for c in range(3):
        settle(c)
    if second:

        def keep_strains(at, strain):
            for f in range(6):
                strain_ref[f, at] = strain[f]

        strains(keep_strains)
    else:
        strains(
            lambda at, strain: add_gradient(
                sums_ref, [wave_ref[3 + f, at] for f in range(6)], strain
            )
        )
        gradient_ref[...] = gradient_rows(sums_ref)


def velocities(meta, pick, frame, wave, snaps, got):
    second = wave is None
    operands = [meta, pick, frame] + ([] if second else [wave]) + [snaps, got]

    def kernel(*refs):
        velocity_kernel(second, *refs)

    (result,) = call(
        kernel,
        operands,
        [array(6, 64, NP, NE) if second else array(2, NE)],
        [
            pltpu.VMEM((3, 64, NP, NE), f32),
            pltpu.VMEM((2, 3, NP, NP, NE), f32),
            pltpu.VMEM((2, NP, NE), f32),
        ],
    )
    return result


def exchange(send):
    return lax.all_to_all(send, "dom", split_axis=0, concat_axis=0, tiled=True)


def swap_traces(cross, paired):
    ups = [(d, d + 1) for d in range(1, DEV - 1, 2)]
    pairs = [(d, d + 1) for d in range(0, DEV, 2)]
    both = lambda steps: steps + [(b, a) for a, b in steps]
    return lax.ppermute(cross, "dom", both(ups)), lax.ppermute(paired, "dom", both(pairs))


def body(
    adjoint, snapshots, density, lame_lambda, lame_mu, element_order, orient, new_owner, new_slot
):
    rows = [
        x.reshape(1, NE)
        for x in (new_owner, density, lame_lambda, lame_mu, element_order, orient, new_slot)
    ]
    snaps = snapshots.reshape(SNAPS, NM, NE)
    send, meta = pack(rows, adjoint, snaps)
    got = lax.all_to_all(send, "dom", split_axis=0, concat_axis=0, tiled=True)
    wave, *traces, rows, pick, frame = place(meta, got, adjoint)
    stage = 0
    for step in range(STEPS):
        start = wave
        for half in (False, True):
            outer = swap_traces(*traces)
            part, flux = inner(wave, rows)
            base = start if half else None
            if stage == 2:
                strain = velocities(meta, pick, frame, None, snaps, got)
                part, strain = lax.optimization_barrier((part, strain))
            if stage == 3:
                first = velocities(meta, pick, frame, start, snaps, got)
                signed, gradients = update(
                    base, wave, part, flux, traces, outer, rows, (strain, first)
                )
            else:
                wave, *traces = update(base, wave, part, flux, traces, outer, rows)
            stage += 1
    return signed.reshape(FIELDS, NM, NE), gradients


def solution(mesh):
    shard = P("dom")
    in_specs = (P(None, None, "dom"), P(None, None, None, "dom")) + (shard,) * 7
    out_specs = (P(None, None, "dom"), P(None, "dom"))
    return jax.shard_map(body, mesh=mesh, in_specs=in_specs, out_specs=out_specs, check_vma=False)
```

```python
import jax
import jax.numpy as jnp
from jax import lax
from jax.experimental import pallas as pl
from jax.experimental.pallas import tpu as pltpu
from jax.sharding import PartitionSpec as P

NP = 8
NM = 512
EX = 8
NE = 128
STEPS = 2
DEV = 128
FIELDS = 9
SNAPS = 6
BLOCKS = FIELDS + SNAPS
DT = 0.01
f32 = jnp.float32
bf16 = jnp.bfloat16

VOIGT = ((3, 8, 7), (8, 4, 6), (7, 6, 5))
ACTIVE = tuple((0, 1, 2) + VOIGT[a] for a in range(3))


def split3(x):
    high = x.astype(bf16)
    rest = x - high.astype(f32)
    middle = rest.astype(bf16)
    low = (rest - middle.astype(f32)).astype(bf16)
    return high, middle, low


def call(kernel, operands, out_shape, scratch_shapes=(), hbm=(), hbm_out=(), limit=16):
    def space(position, x):
        return pltpu.HBM if position in hbm else pltpu.VMEM

    return pl.pallas_call(
        kernel,
        in_specs=[pl.BlockSpec(memory_space=space(n, x)) for n, x in enumerate(operands)],
        out_specs=[
            pl.BlockSpec(memory_space=pltpu.HBM if n in hbm_out else pltpu.VMEM)
            for n in range(len(out_shape))
        ],
        out_shape=out_shape,
        scratch_shapes=list(scratch_shapes),
        compiler_params=pltpu.CompilerParams(vmem_limit_bytes=limit * 1024 * 1024),
        cost_estimate=pl.CostEstimate(flops=0, bytes_accessed=0, transcendentals=0),
    )(*operands)


def array(*shape, dtype=f32):
    return jax.ShapeDtypeStruct(shape, dtype)


def scatter_rows(hot, x, out_ref, row):
    parts = jnp.concatenate(split3(x), axis=1)
    hots = jnp.concatenate([hot, hot, hot], axis=1)
    rows = lax.dot_general(hots, parts, (((1,), (1,)), ((), ())), preferred_element_type=f32)
    groups = [
        rows[r * DEV : (r + 1) * DEV, q * 128 : (q + 1) * 128].reshape(DEV // 8, 8, 128)
        for r in range(2)
        for q in range(4)
    ]
    tiles = jnp.swapaxes(jnp.stack(groups, axis=1), 1, 2)
    out_ref[:, row : row + 8, :] = tiles.reshape(DEV, 8, 128)


def pack_kernel(*refs):
    (owner_hbm, density_hbm, lambda_hbm, mu_hbm, order_hbm, orient_hbm, slot_hbm, adj_hbm,
     snap_hbm, out_hbm, meta_ref, owner_ref, floats_ref, ints_ref, hot_ref, block_ref, out_ref,
     row_sem, in_sem, out_sem) = refs
    small = [pltpu.make_async_copy(owner_hbm, owner_ref, row_sem.at[0])]
    for n, source in enumerate((density_hbm, lambda_hbm, mu_hbm)):
        small.append(pltpu.make_async_copy(source, floats_ref.at[n], row_sem.at[1 + n]))
    for n, source in enumerate((order_hbm, orient_hbm, slot_hbm)):
        small.append(pltpu.make_async_copy(source, ints_ref.at[n], row_sem.at[4 + n]))
    arrive = []
    for b in range(BLOCKS):
        source = adj_hbm.at[b] if b < FIELDS else snap_hbm.at[b - FIELDS]
        arrive.append(pltpu.make_async_copy(source, block_ref.at[b], in_sem.at[b]))
    for copy in small + arrive:
        copy.start()
    for copy in small:
        copy.wait()
    for n in range(3):
        meta_ref[n : n + 1, :] = floats_ref[n]
        meta_ref[3 + n : 4 + n, :] = ints_ref[n].astype(f32)
    meta_ref[5:6, :] += 1.0
    meta_ref[6:7, :] = jnp.where(owner_ref[...] == lax.axis_index("dom"), 1.0, 0.0)
    meta_ref[7:8, :] = jnp.zeros((1, NE), f32)
    owner_row = owner_ref[...]
    owner_all = jnp.broadcast_to(owner_row, (NE, NE))
    owner_col = jnp.transpose(owner_all)
    at0 = lax.broadcasted_iota(jnp.int32, (NE, NE), 0)
    at1 = lax.broadcasted_iota(jnp.int32, (NE, NE), 1)
    earlier = jnp.where((owner_col == owner_all) & (at0 < at1), 1.0, 0.0)
    rank = jnp.sum(earlier, axis=0, keepdims=True)
    dest = jnp.where(owner_row != lax.axis_index("dom"), owner_row, -1)
    for r in range(2):
        chosen = (at0 == dest) & (rank == float(r))
        hot_ref[r * DEV : (r + 1) * DEV, :] = jnp.where(chosen, 1.0, 0.0).astype(bf16)

    first_row = lax.broadcasted_iota(jnp.int32, (8, NE), 0) == 0
    leave = []
    for b in range(BLOCKS):
        arrive[b].wait()
        block = block_ref[b]
        if b >= FIELDS:
            n = b - FIELDS
            row = jnp.broadcast_to(meta_ref[n : n + 1, :], (8, NE))
            block = jnp.concatenate([jnp.where(first_row, row, block[0:8]), block[8:]], axis=0)
        scatter_rows(hot_ref[...], block, out_ref, b * 8)
        rows = pl.ds(b * 8, 8)
        leave.append(
            pltpu.make_async_copy(out_ref.at[:, rows, :], out_hbm.at[:, rows, :], out_sem.at[b])
        )
        leave[b].start()
    for copy in leave:
        copy.wait()


def pack(rows, adjoint, snaps):
    return call(
        pack_kernel,
        (*rows, adjoint, snaps),
        [array(DEV, BLOCKS * 8, 128), array(8, NE)],
        [
            pltpu.VMEM((1, NE), jnp.int32),
            pltpu.VMEM((3, 1, NE), f32),
            pltpu.VMEM((3, 1, NE), jnp.int32),
            pltpu.VMEM((2 * DEV, NE), bf16),
            pltpu.VMEM((BLOCKS, NM, NE), f32),
            pltpu.VMEM((DEV, BLOCKS * 8, 128), f32),
            pltpu.SemaphoreType.DMA((7,)),
            pltpu.SemaphoreType.DMA((BLOCKS,)),
            pltpu.SemaphoreType.DMA((BLOCKS,)),
        ],
        hbm=tuple(range(9)),
        hbm_out=(0,),
        limit=63,
    )


def select_slots(pick, slots):
    parts = jnp.concatenate(split3(slots), axis=0)
    picks = jnp.concatenate([pick, pick, pick], axis=1)
    placed = lax.dot_general(picks, parts, (((1,), (0,)), ((), ())), preferred_element_type=f32)
    return jnp.transpose(placed)


def gather_elements(pick, got_ref, row):
    tiles = jnp.swapaxes(got_ref[:, row : row + 8, :].reshape(DEV // 8, 8, 8, 128), 1, 2)
    rows = [tiles[:, n].reshape(DEV, 128) for n in range(8)]
    slots = [jnp.concatenate(rows[4 * r : 4 * r + 4], axis=1) for r in range(2)]
    return select_slots(pick, jnp.concatenate(slots, axis=0))


def mode_indices(shape):
    mode = lax.broadcasted_iota(jnp.int32, shape, 0)
    return mode // 64, (mode // 8) % 8, mode % 8


def mask_and_sign(order, orient):
    i, j, k = mode_indices((NM, NE))
    highest = jnp.maximum(jnp.maximum(i, j), k).astype(f32)
    flip_x = (orient == 1.0) | (orient == 3.0)
    flip_y = orient >= 2.0
    sign_x = jnp.where(i % 2 == 1, jnp.where(flip_x, -1.0, 1.0), 1.0)
    sign_y = jnp.where(j % 2 == 1, jnp.where(flip_y, -1.0, 1.0), 1.0)
    return jnp.where(highest <= order, sign_x * sign_y, 0.0)


def odd_device():
    return jnp.full((NP, NE), lax.axis_index("dom"), jnp.int32) % 2 == 1


def face_traces(modes, row):
    low4, low2, even = row < 4, row % 4 < 2, row % 2 == 0
    fours = []
    for j in range(4):
        first, second = modes[j], modes[j + 4]
        other = jnp.where(low4, second, first)
        fours.append(jnp.where(low4, first, second) + pltpu.roll(other, 4, 0))
    twos = []
    for j in range(2):
        first, second = fours[j], fours[j + 2]
        twos.append(
            jnp.where(low2, first + pltpu.roll(first, 6, 0), second + pltpu.roll(second, 2, 0))
        )
    first, second = twos
    next_first, next_second = pltpu.roll(first, 7, 0), pltpu.roll(second, 1, 0)
    upper = jnp.where(even, first + next_first, second + next_second)
    lower = jnp.where(even, first - next_first, next_second - second)
    return upper, lower


def place_kernel(
    meta_ref, got_ref, adj_ref, wave_ref, cross_ref, paired_ref, rows_ref, pick_ref, frame_ref
):
    keep = meta_ref[6:7, :] > 0.5
    odd = odd_device()
    lane = lax.broadcasted_iota(jnp.int32, (DEV, NE), 1)
    columns = []
    for r in range(2):
        column = jnp.zeros((DEV, NE), f32)
        for n in range(SNAPS):
            value = got_ref[:, (FIELDS + n) * 8 + r * 4, 0:1]
            column = jnp.where(lane == n, value, column)
        columns.append(column)
        chosen = jnp.where(column[:, 5:6] == lane.astype(f32) + 1.0, 1.0, 0.0)
        pick_ref[:, r * DEV : (r + 1) * DEV] = jnp.transpose(chosen).astype(bf16)
    arrived = select_slots(pick_ref[...], jnp.concatenate(columns, axis=0))
    meta = jnp.where(keep, meta_ref[...], arrived[0:8])
    density, lam, mu = meta[0:1], meta[1:2], meta[2:3]
    order, orient = meta[3:4], meta[4:5]
    rows_ref[0:1, :] = 1.0 / density
    rows_ref[1:2, :] = lam
    rows_ref[2:3, :] = mu
    rows_ref[3:4, :] = jnp.sqrt((lam + 2.0 * mu) / density)
    rows_ref[4:5, :] = order
    rows_ref[5:6, :] = orient
    rows_ref[6:8, :] = jnp.zeros((2, NE), f32)
    frame_ref[...] = mask_and_sign(order, orient)

    row = lax.broadcasted_iota(jnp.int32, (NP, NE), 0)
    for f in range(FIELDS):
        block = gather_elements(pick_ref[...], got_ref, f * 8)
        wave = jnp.where(keep, adj_ref[f], block) * frame_ref[...]
        wave = wave.reshape(64, NP, NE)
        wave_ref[f] = wave
        for i in range(NP):
            upper, lower = face_traces([wave[i * NP + j] for j in range(NP)], row)
            cross_ref[f, i * NP : (i + 1) * NP, :] = jnp.where(odd, upper, lower)
            paired_ref[f, i * NP : (i + 1) * NP, :] = jnp.where(odd, lower, upper)


def place(meta, got, adjoint):
    return call(
        place_kernel,
        (meta, got, adjoint),
        [
            array(FIELDS, 64, NP, NE),
            array(FIELDS, 64, NE),
            array(FIELDS, 64, NE),
            array(8, NE),
            array(NE, 2 * DEV, dtype=bf16),
            array(NM, NE),
        ],
    )


def materials(rows_ref):
    full = lambda r: jnp.broadcast_to(rows_ref[r : r + 1, :], (NP, NE))
    return full(0), full(1), full(2), full(3)


def apply_b(values, direction, rinv, lam, mu):
    out = [None] * FIELDS
    for c in range(3):
        out[c] = values[VOIGT[c][direction]] * rinv
    spread = lam * values[direction]
    for b in range(3):
        out[3 + b] = spread
    out[3 + direction] = spread + 2.0 * mu * values[direction]
    for c in range(3):
        if c != direction:
            out[VOIGT[c][direction]] = mu * values[c]
    return out


def face_flux(total, difference, direction, rinv, lam, mu, speed):
    even_b = apply_b(difference, direction, rinv, lam, mu)
    odd_b = apply_b(total, direction, rinv, lam, mu)
    even, odd = [], []
    for f in range(FIELDS):
        pen_even, pen_odd = speed * total[f], speed * difference[f]
        if even_b[f] is not None:
            pen_even, pen_odd = pen_even + even_b[f], pen_odd + odd_b[f]
        even.append(-0.25 * pen_even)
        odd.append(-0.25 * pen_odd)
    return even, odd


def local_flux(evens, odds, direction, offset, keep_up, keep_down, rinv, lam, mu, speed):
    total, difference = [], []
    for f in range(FIELDS):
        upper, lower = evens[f] + odds[f], evens[f] - odds[f]
        above = pltpu.roll(lower, NE - offset, 1) * keep_up
        below = pltpu.roll(upper, offset, 1) * keep_down
        total.append((upper - above) + (lower - below))
        difference.append((upper - above) - (lower - below))
    return face_flux(total, difference, direction, rinv, lam, mu, speed)


def lane_keeps():
    lane = lax.broadcasted_iota(jnp.int32, (NP, NE), 1)
    one = lambda cond: jnp.where(cond, 1.0, 0.0)
    column = lane % EX
    return (
        (one(column != EX - 1), one(column != 0)),
        (one(lane < NE - EX), one(lane >= EX)),
    )


def mode_rows():
    k = lax.broadcasted_iota(jnp.int32, (NP, NE), 0)
    one = lambda cond: jnp.where(cond, 1.0, 0.0)
    return one(k < 7), one(k < 6), one(k < 4), (2 * k + 1).astype(f32)


def sums_above(x, keep1, keep2, keep4):
    x = pltpu.roll(x, 7, 0) * keep1
    x = x + pltpu.roll(x, 6, 0) * keep2
    return x + pltpu.roll(x, 4, 0) * keep4


def inner_kernel(step, *refs):
    if step is None:
        wave_ref, rows_ref, out_ref, flux_ref, run_ref, fluxy_ref = refs
    else:
        (begun_ref, fluxz_ref, rows_ref, wave_ref, out_ref, flux_ref, run_ref,
         fluxy_ref) = refs
        order = jnp.broadcast_to(rows_ref[4:5, :], (NP, NE))
        k = lax.broadcasted_iota(jnp.int32, (NP, NE), 0)
    rinv, lam, mu, speed = materials(rows_ref)
    keeps_x, keeps_y = lane_keeps()
    keep1, keep2, keep4, factor_z = mode_rows()
    run_ref[...] = jnp.zeros_like(run_ref)

    @pl.loop(0, NP)
    def _(g):
        i = NP - 1 - g
        parity = lax.rem(i, 2)
        factor_x = (2 * i + 1).astype(f32)

        if step is not None:
            at = pl.multiple_of(i * NP, NP)
            scales = [factor_z * mask for mask in order_masks(order, k, i, step)]
            for f in range(FIELDS):
                for j in range(NP):
                    lifted = lifted_row(fluxz_ref, f, at + j, k)
                    wave_ref[f, at + j] = begun_ref[f, at + j] + scales[j] * lifted

        evens, odds = [], []
        for f in range(FIELDS):
            col = [wave_ref[f, i * NP + j] for j in range(NP)]
            evens.append((col[0] + col[2]) + (col[4] + col[6]))
            odds.append((col[1] + col[3]) + (col[5] + col[7]))
        even, odd = local_flux(evens, odds, 1, EX, *keeps_y, rinv, lam, mu, speed)
        for f in range(FIELDS):
            fluxy_ref[0, f] = even[f]
            fluxy_ref[1, f] = odd[f]

        sums_y = {f: [None, None] for f in ACTIVE[1]}
        for j in range(NP - 1, -1, -1):
            here = [wave_ref[f, i * NP + j] for f in range(FIELDS)]
            slope = [{}, {}, {}]
            for f in ACTIVE[0]:
                slope[0][f] = factor_x * run_ref[parity, f, j]
            for f in ACTIVE[1]:
                if sums_y[f][j % 2] is not None:
                    slope[1][f] = (2.0 * j + 1.0) * sums_y[f][j % 2]
            for f in ACTIVE[2]:
                slope[2][f] = factor_z * sums_above(here[f], keep1, keep2, keep4)

            def total(pairs):
                found = [slope[a][f] for a, f in pairs if f in slope[a]]
                result = found[0]
                for item in found[1:]:
                    result = result + item
                return result

            result = [None] * FIELDS
            for c in range(3):
                result[c] = rinv * total([(a, VOIGT[c][a]) for a in range(3)])
            spread = lam * total([(a, a) for a in range(3)])
            for b in range(3):
                if b in slope[b]:
                    result[3 + b] = spread + 2.0 * mu * slope[b][b]
                else:
                    result[3 + b] = spread
            for b, c in ((1, 2), (0, 2), (0, 1)):
                result[VOIGT[b][c]] = mu * total([(b, c), (c, b)])
            for f in range(FIELDS):
                out_ref[f, i * NP + j] = result[f] + (2.0 * j + 1.0) * fluxy_ref[j % 2, f]

            for f in ACTIVE[1]:
                before = sums_y[f][1 - j % 2]
                sums_y[f][1 - j % 2] = here[f] if before is None else before + here[f]
            for f in range(FIELDS):
                run_ref[1 - parity, f, j] += here[f]

    @pl.loop(0, NP)
    def _(j):
        even_x, odd_x = local_flux(
            [run_ref[1, f, j] for f in range(FIELDS)],
            [run_ref[0, f, j] for f in range(FIELDS)],
            0, 1, *keeps_x, rinv, lam, mu, speed,
        )
        for f in range(FIELDS):
            flux_ref[0, f, j] = even_x[f]
            flux_ref[1, f, j] = odd_x[f]


def inner(wave, rows):
    return call(
        lambda *refs: inner_kernel(None, *refs),
        (wave, rows),
        [array(FIELDS, 64, NP, NE), array(2, FIELDS, NP, NP, NE)],
        [pltpu.VMEM((2, FIELDS, NP, NP, NE), f32), pltpu.VMEM((2, FIELDS, NP, NE), f32)],
    )


def complete(begun, fluxz, rows, step):
    return call(
        lambda *refs: inner_kernel(step, *refs),
        (begun, fluxz, rows),
        [
            array(FIELDS, 64, NP, NE),
            array(FIELDS, 64, NP, NE),
            array(2, FIELDS, NP, NP, NE),
        ],
        [pltpu.VMEM((2, FIELDS, NP, NP, NE), f32), pltpu.VMEM((2, FIELDS, NP, NE), f32)],
    )


def order_masks(order, k, i, step):
    highest = [jnp.maximum(k, jnp.maximum(i, j)).astype(f32) for j in range(NP)]
    return [jnp.where(h <= order, step, 0.0) for h in highest]


def lifted_row(fluxz_ref, f, at, k):
    return jnp.where(
        k % 2 == 0,
        jnp.broadcast_to(fluxz_ref[0, f, pl.ds(at, 1), :], (NP, NE)),
        jnp.broadcast_to(fluxz_ref[1, f, pl.ds(at, 1), :], (NP, NE)),
    )


def begin_kernel(half, *refs):
    refs = list(refs)
    base_ref = refs.pop(0) if half else None
    wave_ref, part_ref, flux_ref, rows_ref, out_ref, cross_ref, paired_ref = refs
    order = jnp.broadcast_to(rows_ref[4:5, :], (NP, NE))
    odd = odd_device()
    k = lax.broadcasted_iota(jnp.int32, (NP, NE), 0)

    @pl.loop(0, NP)
    def _(i):
        parity = lax.rem(i, 2)
        factor_x = (2 * i + 1).astype(f32)
        at = pl.multiple_of(i * NP, NP)
        rows = pl.ds(at, NP)
        masks = order_masks(order, k, i, 0.5 * DT if half else DT)
        for f in range(FIELDS):
            fresh = []
            for j in range(NP):
                slope = part_ref[f, at + j] + factor_x * flux_ref[parity, f, j]
                start = wave_ref[f, at + j]
                if half:
                    start = 0.5 * (base_ref[f, at + j] + start)
                new = start + masks[j] * slope
                out_ref[f, at + j] = new
                fresh.append(new)
            upper, lower = face_traces(fresh, k)
            cross_ref[f, rows] = jnp.where(odd, upper, lower)
            paired_ref[f, rows] = jnp.where(odd, lower, upper)


def begin(base, wave, part, flux, rows):
    half = base is not None
    return call(
        lambda *refs: begin_kernel(half, *refs),
        ([base] if half else []) + [wave, part, flux, rows],
        [array(FIELDS, 64, NP, NE), array(FIELDS, 64, NE), array(FIELDS, 64, NE)],
    )


def outer_kernel(
    step, cross_ref, paired_ref, got_cross_ref, got_paired_ref, begun_cross_ref,
    begun_paired_ref, rows_ref, fluxz_ref, out_cross_ref, out_paired_ref,
):
    rinv, lam, mu, speed = materials(rows_ref)
    order = jnp.broadcast_to(rows_ref[4:5, :], (NP, NE))
    side = jnp.where(odd_device(), 1.0, -1.0)
    j = lax.broadcasted_iota(jnp.int32, (NP, NE), 0)

    def factors(first):
        total = jnp.zeros((NP, NE), f32)
        for n in range(first, NP, 2):
            total = total + jnp.where(order >= float(n), 2.0 * n + 1.0, 0.0)
        return step * total

    factor_even, factor_odd = factors(0), side * factors(1)

    @pl.loop(0, NP)
    def _(i):
        rows = pl.ds(pl.multiple_of(i * NP, NP), NP)
        total, difference = [], []
        for f in range(FIELDS):
            jump_cross = cross_ref[f, rows] - got_cross_ref[f, rows]
            jump_paired = paired_ref[f, rows] - got_paired_ref[f, rows]
            total.append(jump_cross + jump_paired)
            difference.append(side * (jump_cross - jump_paired))
        even, odds = face_flux(total, difference, 2, rinv, lam, mu, speed)
        allowed = jnp.where(jnp.maximum(j, i).astype(f32) <= order, 1.0, 0.0)
        scale_even, scale_odd = allowed * factor_even, allowed * factor_odd
        for f in range(FIELDS):
            fluxz_ref[0, f, rows] = even[f]
            fluxz_ref[1, f, rows] = odds[f]
            from_even, from_odd = scale_even * even[f], scale_odd * odds[f]
            out_cross_ref[f, rows] = begun_cross_ref[f, rows] + (from_even + from_odd)
            out_paired_ref[f, rows] = begun_paired_ref[f, rows] + (from_even - from_odd)


def outer(traces, got, begun_traces, rows, step):
    trace = array(FIELDS, 64, NE)
    return call(
        lambda *refs: outer_kernel(step, *refs),
        [*traces, *got, *begun_traces, rows],
        [array(2, FIELDS, 64, NE), trace, trace],
    )


def finish_kernel(
    base_ref, wave_ref, part_ref, flux_ref, cross_ref, paired_ref, got_cross_ref,
    got_paired_ref, rows_ref, strain_ref, first_ref, out_hbm, gradient_ref,
    out_ref, fluxz_ref, sums_ref, out_sem,
):
    rinv, lam, mu, speed = materials(rows_ref)
    order = jnp.broadcast_to(rows_ref[4:5, :], (NP, NE))
    orient = jnp.broadcast_to(rows_ref[5:6, :], (NP, NE))
    side = jnp.where(odd_device(), 1.0, -1.0)
    k = lax.broadcasted_iota(jnp.int32, (NP, NE), 0)
    factor_z = (2 * k + 1).astype(f32)
    sums_ref[...] = jnp.zeros_like(sums_ref)

    def leave(i):
        rows = pl.ds(pl.multiple_of(i * NP, NP), NP)
        return pltpu.make_async_copy(out_ref.at[:, rows], out_hbm.at[:, rows], out_sem.at[i])

    @pl.loop(0, NP)
    def _(i):
        parity = lax.rem(i, 2)
        factor_x = (2 * i + 1).astype(f32)
        at = pl.multiple_of(i * NP, NP)
        rows = pl.ds(at, NP)
        total, difference = [], []
        for f in range(FIELDS):
            jump_cross = cross_ref[f, rows] - got_cross_ref[f, rows]
            jump_paired = paired_ref[f, rows] - got_paired_ref[f, rows]
            total.append(jump_cross + jump_paired)
            difference.append(side * (jump_cross - jump_paired))
        even, odds = face_flux(total, difference, 2, rinv, lam, mu, speed)
        for f in range(FIELDS):
            fluxz_ref[0, f] = even[f]
            fluxz_ref[1, f] = odds[f]

        masks = order_masks(order, k, i, 0.5 * DT)
        flip_x = ((orient == 1.0) | (orient == 3.0)) & (parity == 1)
        sign_x = jnp.where(flip_x, -1.0, 1.0)
        sign_y = jnp.where(orient >= 2.0, -1.0, 1.0)
        signs = [sign_x, sign_x * sign_y]
        stresses = [[] for _ in range(NP)]
        for f in range(FIELDS):
            for j in range(NP):
                lifted = lifted_row(fluxz_ref, f, j, k)
                slope = part_ref[f, at + j] + factor_x * flux_ref[parity, f, j] + factor_z * lifted
                start = 0.5 * (base_ref[f, at + j] + wave_ref[f, at + j])
                new = start + masks[j] * slope
                out_ref[f, at + j] = new * signs[j % 2]
                if f >= 3:
                    stresses[j].append(new)
        leave(i).start()
        for j in range(NP):
            add_gradient(sums_ref, stresses[j], [strain_ref[f, at + j] for f in range(6)])

    gradient_ref[...] = first_ref[...] + gradient_rows(sums_ref)
    for i in range(NP):
        leave(i).wait()


def finish(base, wave, part, flux, traces, got, rows, strain, first):
    return call(
        finish_kernel,
        [base, wave, part, flux, *traces, *got, rows, strain, first],
        [array(FIELDS, 64, NP, NE), array(2, NE)],
        [
            pltpu.VMEM((FIELDS, 64, NP, NE), f32),
            pltpu.VMEM((2, FIELDS, NP, NE), f32),
            pltpu.VMEM((2, NP, NE), f32),
            pltpu.SemaphoreType.DMA((NP,)),
        ],
        hbm_out=(0,),
    )


def add_gradient(sums_ref, stress, strain):
    normal = (stress[0] + stress[1]) + stress[2]
    sums_ref[0] += normal * ((strain[0] + strain[1]) + strain[2])
    shear = stress[0] * strain[0]
    for f in range(1, 6):
        shear = shear + stress[f] * strain[f]
    sums_ref[1] += shear


def gradient_rows(sums_ref):
    first = (0.5 * DT) * jnp.sum(sums_ref[0], axis=0, keepdims=True)
    second = DT * jnp.sum(sums_ref[1], axis=0, keepdims=True)
    return jnp.concatenate([first, second], axis=0)


def velocity_kernel(second, meta_ref, pick_ref, frame_ref, *refs):
    if second:
        snap_ref, got_ref, strain_ref, *rest = refs
    else:
        wave_ref, snap_ref, got_ref, gradient_ref, *rest = refs
    vel_ref, run_ref, sums_ref = rest
    start = 3 if second else 0
    keep = meta_ref[6:7, :] > 0.5
    row = lax.broadcasted_iota(jnp.int32, (8, NE), 0)
    keep1, keep2, keep4, factor_z = mode_rows()
    weight_z = 2.0 / factor_z
    sums_ref[...] = jnp.zeros_like(sums_ref)

    def settle(c):
        block = gather_elements(pick_ref[...], got_ref, (FIELDS + start + c) * 8)
        block = jnp.concatenate([jnp.where(row == 0, 0.0, block[0:8]), block[8:]], axis=0)
        velocity = jnp.where(keep, snap_ref[start + c], block) * frame_ref[...]
        vel_ref[c] = velocity.reshape(64, NP, NE)

    def strains(use):
        run_ref[...] = jnp.zeros_like(run_ref)

        @pl.loop(0, NP)
        def _(g):
            i = NP - 1 - g
            parity = lax.rem(i, 2)
            at = pl.multiple_of(i * NP, NP)
            weight_x = 2.0 / jnp.full((NP, NE), 2 * i + 1, jnp.int32).astype(f32)
            weight_xz = 2.0 * weight_x * weight_z
            zero = jnp.zeros((NP, NE), f32)
            run_y = [[zero, zero] for _ in range(3)]
            for j in range(NP - 1, -1, -1):
                weight_y = 2.0 / (2.0 * j + 1.0)
                slopes = []
                for c in range(3):
                    here = vel_ref[c, at + j]
                    slopes.append([
                        (2.0 * weight_y) * (weight_z * run_ref[parity, c, j]),
                        weight_xz * run_y[c][j % 2],
                        (2.0 * weight_y) * (weight_x * sums_above(here, keep1, keep2, keep4)),
                    ])
                    run_y[c][1 - j % 2] = run_y[c][1 - j % 2] + here
                    run_ref[1 - parity, c, j] += here
                use(at + j, [
                    2.0 * slopes[0][0], 2.0 * slopes[1][1], 2.0 * slopes[2][2],
                    slopes[2][1] + slopes[1][2], slopes[2][0] + slopes[0][2],
                    slopes[1][0] + slopes[0][1],
                ])

    for c in range(3):
        settle(c)
    if second:

        def keep_strains(at, strain):
            for f in range(6):
                strain_ref[f, at] = strain[f]

        strains(keep_strains)
    else:
        strains(
            lambda at, strain: add_gradient(
                sums_ref, [wave_ref[3 + f, at] for f in range(6)], strain
            )
        )
        gradient_ref[...] = gradient_rows(sums_ref)


def velocities(meta, pick, frame, wave, snaps, got):
    second = wave is None
    operands = [meta, pick, frame] + ([] if second else [wave]) + [snaps, got]

    def kernel(*refs):
        velocity_kernel(second, *refs)

    (result,) = call(
        kernel,
        operands,
        [array(6, 64, NP, NE) if second else array(2, NE)],
        [
            pltpu.VMEM((3, 64, NP, NE), f32),
            pltpu.VMEM((2, 3, NP, NP, NE), f32),
            pltpu.VMEM((2, NP, NE), f32),
        ],
    )
    return result


def exchange(send):
    return lax.all_to_all(send, "dom", split_axis=0, concat_axis=0, tiled=True)


def swap_traces(cross, paired):
    ups = [(d, d + 1) for d in range(1, DEV - 1, 2)]
    pairs = [(d, d + 1) for d in range(0, DEV, 2)]
    both = lambda steps: steps + [(b, a) for a, b in steps]
    return lax.ppermute(cross, "dom", both(ups)), lax.ppermute(paired, "dom", both(pairs))


def body(
    adjoint, snapshots, density, lame_lambda, lame_mu, element_order, orient, new_owner, new_slot
):
    rows = [
        x.reshape(1, NE)
        for x in (new_owner, density, lame_lambda, lame_mu, element_order, orient, new_slot)
    ]
    snaps = snapshots.reshape(SNAPS, NM, NE)
    send, meta = pack(rows, adjoint, snaps)
    got = lax.all_to_all(send, "dom", split_axis=0, concat_axis=0, tiled=True)
    wave, *traces, rows, pick, frame = place(meta, got, adjoint)
    part, flux = inner(wave, rows)
    start, base = wave, None
    for stage in range(2 * STEPS - 1):
        got_traces = swap_traces(*traces)
        step = DT if base is None else 0.5 * DT
        begun, *begun_traces = begin(base, wave, part, flux, rows)
        if stage == 2:
            strain = velocities(meta, pick, frame, None, snaps, got)
            begun_traces[0], strain = lax.optimization_barrier((begun_traces[0], strain))
        fluxz, *traces = outer(traces, got_traces, begun_traces, rows, step)
        wave, part, flux = complete(begun, fluxz, rows, step)
        if base is None:
            base = start
        else:
            start, base = wave, None
    first = velocities(meta, pick, frame, start, snaps, got)
    got_traces = swap_traces(*traces)
    signed, gradients = finish(
        base, wave, part, flux, traces, got_traces, rows, strain, first
    )
    return signed.reshape(FIELDS, NM, NE), gradients


def solution(mesh):
    shard = P("dom")
    in_specs = (P(None, None, "dom"), P(None, None, None, "dom")) + (shard,) * 7
    out_specs = (P(None, None, "dom"), P(None, "dom"))
    return jax.shard_map(body, mesh=mesh, in_specs=in_specs, out_specs=out_specs, check_vma=False)
```

```python
import jax
import jax.numpy as jnp
from jax import lax
from jax.experimental import pallas as pl
from jax.experimental.pallas import tpu as pltpu
from jax.sharding import PartitionSpec as P

NP = 8
NM = 512
EX = 8
NE = 128
STEPS = 2
DEV = 128
FIELDS = 9
SNAPS = 6
BLOCKS = FIELDS + SNAPS
DT = 0.01
f32 = jnp.float32
bf16 = jnp.bfloat16

VOIGT = ((3, 8, 7), (8, 4, 6), (7, 6, 5))
ACTIVE = tuple((0, 1, 2) + VOIGT[a] for a in range(3))


def split3(x):
    high = x.astype(bf16)
    rest = x - high.astype(f32)
    middle = rest.astype(bf16)
    low = (rest - middle.astype(f32)).astype(bf16)
    return high, middle, low


def call(kernel, operands, out_shape, scratch_shapes=(), hbm=(), hbm_out=(), limit=16):
    def space(position, x):
        return pltpu.HBM if position in hbm else pltpu.VMEM

    return pl.pallas_call(
        kernel,
        in_specs=[pl.BlockSpec(memory_space=space(n, x)) for n, x in enumerate(operands)],
        out_specs=[
            pl.BlockSpec(memory_space=pltpu.HBM if n in hbm_out else pltpu.VMEM)
            for n in range(len(out_shape))
        ],
        out_shape=out_shape,
        scratch_shapes=list(scratch_shapes),
        compiler_params=pltpu.CompilerParams(vmem_limit_bytes=limit * 1024 * 1024),
        cost_estimate=pl.CostEstimate(flops=0, bytes_accessed=0, transcendentals=0),
    )(*operands)


def array(*shape, dtype=f32):
    return jax.ShapeDtypeStruct(shape, dtype)


def scatter_rows(hot, x, out_ref, row):
    parts = jnp.concatenate(split3(x), axis=1)
    hots = jnp.concatenate([hot, hot, hot], axis=1)
    rows = lax.dot_general(hots, parts, (((1,), (1,)), ((), ())), preferred_element_type=f32)
    groups = [
        rows[r * DEV : (r + 1) * DEV, q * 128 : (q + 1) * 128].reshape(DEV // 8, 8, 128)
        for r in range(2)
        for q in range(4)
    ]
    tiles = jnp.swapaxes(jnp.stack(groups, axis=1), 1, 2)
    out_ref[:, row : row + 8, :] = tiles.reshape(DEV, 8, 128)


def pack_kernel(*refs):
    (owner_hbm, density_hbm, lambda_hbm, mu_hbm, order_hbm, orient_hbm, slot_hbm, adj_hbm,
     snap_hbm, out_hbm, meta_ref, owner_ref, floats_ref, ints_ref, hot_ref, block_ref, out_ref,
     row_sem, in_sem, out_sem) = refs
    small = [pltpu.make_async_copy(owner_hbm, owner_ref, row_sem.at[0])]
    for n, source in enumerate((density_hbm, lambda_hbm, mu_hbm)):
        small.append(pltpu.make_async_copy(source, floats_ref.at[n], row_sem.at[1 + n]))
    for n, source in enumerate((order_hbm, orient_hbm, slot_hbm)):
        small.append(pltpu.make_async_copy(source, ints_ref.at[n], row_sem.at[4 + n]))
    arrive = []
    for b in range(BLOCKS):
        source = adj_hbm.at[b] if b < FIELDS else snap_hbm.at[b - FIELDS]
        arrive.append(pltpu.make_async_copy(source, block_ref.at[b], in_sem.at[b]))
    for copy in small + arrive:
        copy.start()
    for copy in small:
        copy.wait()
    for n in range(3):
        meta_ref[n : n + 1, :] = floats_ref[n]
        meta_ref[3 + n : 4 + n, :] = ints_ref[n].astype(f32)
    meta_ref[5:6, :] += 1.0
    meta_ref[6:7, :] = jnp.where(owner_ref[...] == lax.axis_index("dom"), 1.0, 0.0)
    meta_ref[7:8, :] = jnp.zeros((1, NE), f32)
    owner_row = owner_ref[...]
    owner_all = jnp.broadcast_to(owner_row, (NE, NE))
    owner_col = jnp.transpose(owner_all)
    at0 = lax.broadcasted_iota(jnp.int32, (NE, NE), 0)
    at1 = lax.broadcasted_iota(jnp.int32, (NE, NE), 1)
    earlier = jnp.where((owner_col == owner_all) & (at0 < at1), 1.0, 0.0)
    rank = jnp.sum(earlier, axis=0, keepdims=True)
    dest = jnp.where(owner_row != lax.axis_index("dom"), owner_row, -1)
    for r in range(2):
        chosen = (at0 == dest) & (rank == float(r))
        hot_ref[r * DEV : (r + 1) * DEV, :] = jnp.where(chosen, 1.0, 0.0).astype(bf16)

    first_row = lax.broadcasted_iota(jnp.int32, (8, NE), 0) == 0
    leave = []
    for b in range(BLOCKS):
        arrive[b].wait()
        block = block_ref[b]
        if b >= FIELDS:
            n = b - FIELDS
            row = jnp.broadcast_to(meta_ref[n : n + 1, :], (8, NE))
            block = jnp.concatenate([jnp.where(first_row, row, block[0:8]), block[8:]], axis=0)
        scatter_rows(hot_ref[...], block, out_ref, b * 8)
        rows = pl.ds(b * 8, 8)
        leave.append(
            pltpu.make_async_copy(out_ref.at[:, rows, :], out_hbm.at[:, rows, :], out_sem.at[b])
        )
        leave[b].start()
    for copy in leave:
        copy.wait()


def pack(rows, adjoint, snaps):
    return call(
        pack_kernel,
        (*rows, adjoint, snaps),
        [array(DEV, BLOCKS * 8, 128), array(8, NE)],
        [
            pltpu.VMEM((1, NE), jnp.int32),
            pltpu.VMEM((3, 1, NE), f32),
            pltpu.VMEM((3, 1, NE), jnp.int32),
            pltpu.VMEM((2 * DEV, NE), bf16),
            pltpu.VMEM((BLOCKS, NM, NE), f32),
            pltpu.VMEM((DEV, BLOCKS * 8, 128), f32),
            pltpu.SemaphoreType.DMA((7,)),
            pltpu.SemaphoreType.DMA((BLOCKS,)),
            pltpu.SemaphoreType.DMA((BLOCKS,)),
        ],
        hbm=tuple(range(9)),
        hbm_out=(0,),
        limit=63,
    )


def select_slots(pick, slots):
    parts = jnp.concatenate(split3(slots), axis=0)
    picks = jnp.concatenate([pick, pick, pick], axis=1)
    placed = lax.dot_general(picks, parts, (((1,), (0,)), ((), ())), preferred_element_type=f32)
    return jnp.transpose(placed)


def gather_elements(pick, got_ref, row):
    tiles = jnp.swapaxes(got_ref[:, row : row + 8, :].reshape(DEV // 8, 8, 8, 128), 1, 2)
    rows = [tiles[:, n].reshape(DEV, 128) for n in range(8)]
    slots = [jnp.concatenate(rows[4 * r : 4 * r + 4], axis=1) for r in range(2)]
    return select_slots(pick, jnp.concatenate(slots, axis=0))


def mode_indices(shape):
    mode = lax.broadcasted_iota(jnp.int32, shape, 0)
    return mode // 64, (mode // 8) % 8, mode % 8


def mask_and_sign(order, orient):
    i, j, k = mode_indices((NM, NE))
    highest = jnp.maximum(jnp.maximum(i, j), k).astype(f32)
    flip_x = (orient == 1.0) | (orient == 3.0)
    flip_y = orient >= 2.0
    sign_x = jnp.where(i % 2 == 1, jnp.where(flip_x, -1.0, 1.0), 1.0)
    sign_y = jnp.where(j % 2 == 1, jnp.where(flip_y, -1.0, 1.0), 1.0)
    return jnp.where(highest <= order, sign_x * sign_y, 0.0)


def odd_device():
    return jnp.full((NP, NE), lax.axis_index("dom"), jnp.int32) % 2 == 1


def face_traces(modes, row):
    low4, low2, even = row < 4, row % 4 < 2, row % 2 == 0
    fours = []
    for j in range(4):
        first, second = modes[j], modes[j + 4]
        other = jnp.where(low4, second, first)
        fours.append(jnp.where(low4, first, second) + pltpu.roll(other, 4, 0))
    twos = []
    for j in range(2):
        first, second = fours[j], fours[j + 2]
        twos.append(
            jnp.where(low2, first + pltpu.roll(first, 6, 0), second + pltpu.roll(second, 2, 0))
        )
    first, second = twos
    next_first, next_second = pltpu.roll(first, 7, 0), pltpu.roll(second, 1, 0)
    upper = jnp.where(even, first + next_first, second + next_second)
    lower = jnp.where(even, first - next_first, next_second - second)
    return upper, lower


def place_kernel(
    meta_ref, got_ref, adj_ref, wave_ref, cross_ref, paired_ref, rows_ref, pick_ref, frame_ref
):
    keep = meta_ref[6:7, :] > 0.5
    odd = odd_device()
    lane = lax.broadcasted_iota(jnp.int32, (DEV, NE), 1)
    columns = []
    for r in range(2):
        column = jnp.zeros((DEV, NE), f32)
        for n in range(SNAPS):
            value = got_ref[:, (FIELDS + n) * 8 + r * 4, 0:1]
            column = jnp.where(lane == n, value, column)
        columns.append(column)
        chosen = jnp.where(column[:, 5:6] == lane.astype(f32) + 1.0, 1.0, 0.0)
        pick_ref[:, r * DEV : (r + 1) * DEV] = jnp.transpose(chosen).astype(bf16)
    arrived = select_slots(pick_ref[...], jnp.concatenate(columns, axis=0))
    meta = jnp.where(keep, meta_ref[...], arrived[0:8])
    density, lam, mu = meta[0:1], meta[1:2], meta[2:3]
    order, orient = meta[3:4], meta[4:5]
    rows_ref[0:1, :] = 1.0 / density
    rows_ref[1:2, :] = lam
    rows_ref[2:3, :] = mu
    rows_ref[3:4, :] = jnp.sqrt((lam + 2.0 * mu) / density)
    rows_ref[4:5, :] = order
    rows_ref[5:6, :] = orient
    rows_ref[6:8, :] = jnp.zeros((2, NE), f32)
    frame_ref[...] = mask_and_sign(order, orient)

    row = lax.broadcasted_iota(jnp.int32, (NP, NE), 0)
    for f in range(FIELDS):
        block = gather_elements(pick_ref[...], got_ref, f * 8)
        wave = jnp.where(keep, adj_ref[f], block) * frame_ref[...]
        wave = wave.reshape(64, NP, NE)
        wave_ref[f] = wave
        for i in range(NP):
            upper, lower = face_traces([wave[i * NP + j] for j in range(NP)], row)
            cross_ref[f, i * NP : (i + 1) * NP, :] = jnp.where(odd, upper, lower)
            paired_ref[f, i * NP : (i + 1) * NP, :] = jnp.where(odd, lower, upper)


def place(meta, got, adjoint):
    return call(
        place_kernel,
        (meta, got, adjoint),
        [
            array(FIELDS, 64, NP, NE),
            array(FIELDS, 64, NE),
            array(FIELDS, 64, NE),
            array(8, NE),
            array(NE, 2 * DEV, dtype=bf16),
            array(NM, NE),
        ],
    )


def materials(rows_ref):
    full = lambda r: jnp.broadcast_to(rows_ref[r : r + 1, :], (NP, NE))
    return full(0), full(1), full(2), full(3)


def apply_b(values, direction, rinv, lam, mu):
    out = [None] * FIELDS
    for c in range(3):
        out[c] = values[VOIGT[c][direction]] * rinv
    spread = lam * values[direction]
    for b in range(3):
        out[3 + b] = spread
    out[3 + direction] = spread + 2.0 * mu * values[direction]
    for c in range(3):
        if c != direction:
            out[VOIGT[c][direction]] = mu * values[c]
    return out


def face_flux(total, difference, direction, rinv, lam, mu, speed):
    even_b = apply_b(difference, direction, rinv, lam, mu)
    odd_b = apply_b(total, direction, rinv, lam, mu)
    even, odd = [], []
    for f in range(FIELDS):
        pen_even, pen_odd = speed * total[f], speed * difference[f]
        if even_b[f] is not None:
            pen_even, pen_odd = pen_even + even_b[f], pen_odd + odd_b[f]
        even.append(-0.25 * pen_even)
        odd.append(-0.25 * pen_odd)
    return even, odd


def local_flux(evens, odds, direction, offset, keep_up, keep_down, rinv, lam, mu, speed):
    total, difference = [], []
    for f in range(FIELDS):
        upper, lower = evens[f] + odds[f], evens[f] - odds[f]
        above = pltpu.roll(lower, NE - offset, 1) * keep_up
        below = pltpu.roll(upper, offset, 1) * keep_down
        total.append((upper - above) + (lower - below))
        difference.append((upper - above) - (lower - below))
    return face_flux(total, difference, direction, rinv, lam, mu, speed)


def lane_keeps():
    lane = lax.broadcasted_iota(jnp.int32, (NP, NE), 1)
    one = lambda cond: jnp.where(cond, 1.0, 0.0)
    column = lane % EX
    return (
        (one(column != EX - 1), one(column != 0)),
        (one(lane < NE - EX), one(lane >= EX)),
    )


def mode_rows():
    k = lax.broadcasted_iota(jnp.int32, (NP, NE), 0)
    one = lambda cond: jnp.where(cond, 1.0, 0.0)
    return one(k < 7), one(k < 6), one(k < 4), (2 * k + 1).astype(f32)


def sums_above(x, keep1, keep2, keep4):
    x = pltpu.roll(x, 7, 0) * keep1
    x = x + pltpu.roll(x, 6, 0) * keep2
    return x + pltpu.roll(x, 4, 0) * keep4


def inner_kernel(step, *refs):
    if step is None:
        wave_ref, rows_ref, out_ref, flux_ref, run_ref, fluxy_ref = refs
    else:
        (begun_ref, fluxz_ref, rows_ref, wave_ref, out_ref, flux_ref, run_ref,
         fluxy_ref) = refs
        order = jnp.broadcast_to(rows_ref[4:5, :], (NP, NE))
        k = lax.broadcasted_iota(jnp.int32, (NP, NE), 0)
    rinv, lam, mu, speed = materials(rows_ref)
    keeps_x, keeps_y = lane_keeps()
    keep1, keep2, keep4, factor_z = mode_rows()
    run_ref[...] = jnp.zeros_like(run_ref)

    @pl.loop(0, NP)
    def _(g):
        i = NP - 1 - g
        parity = lax.rem(i, 2)
        factor_x = (2 * i + 1).astype(f32)

        if step is not None:
            at = pl.multiple_of(i * NP, NP)
            scales = [factor_z * mask for mask in order_masks(order, k, i, step)]
            for f in range(FIELDS):
                for j in range(NP):
                    lifted = lifted_row(fluxz_ref, f, at + j, k)
                    wave_ref[f, at + j] = begun_ref[f, at + j] + scales[j] * lifted

        evens, odds = [], []
        for f in range(FIELDS):
            col = [wave_ref[f, i * NP + j] for j in range(NP)]
            evens.append((col[0] + col[2]) + (col[4] + col[6]))
            odds.append((col[1] + col[3]) + (col[5] + col[7]))
        even, odd = local_flux(evens, odds, 1, EX, *keeps_y, rinv, lam, mu, speed)
        for f in range(FIELDS):
            fluxy_ref[0, f] = even[f]
            fluxy_ref[1, f] = odd[f]

        sums_y = {f: [None, None] for f in ACTIVE[1]}
        for j in range(NP - 1, -1, -1):
            here = [wave_ref[f, i * NP + j] for f in range(FIELDS)]
            slope = [{}, {}, {}]
            for f in ACTIVE[0]:
                slope[0][f] = factor_x * run_ref[parity, f, j]
            for f in ACTIVE[1]:
                if sums_y[f][j % 2] is not None:
                    slope[1][f] = (2.0 * j + 1.0) * sums_y[f][j % 2]
            for f in ACTIVE[2]:
                slope[2][f] = factor_z * sums_above(here[f], keep1, keep2, keep4)

            def total(pairs):
                found = [slope[a][f] for a, f in pairs if f in slope[a]]
                result = found[0]
                for item in found[1:]:
                    result = result + item
                return result

            result = [None] * FIELDS
            for c in range(3):
                result[c] = rinv * total([(a, VOIGT[c][a]) for a in range(3)])
            spread = lam * total([(a, a) for a in range(3)])
            for b in range(3):
                if b in slope[b]:
                    result[3 + b] = spread + 2.0 * mu * slope[b][b]
                else:
                    result[3 + b] = spread
            for b, c in ((1, 2), (0, 2), (0, 1)):
                result[VOIGT[b][c]] = mu * total([(b, c), (c, b)])
            for f in range(FIELDS):
                out_ref[f, i * NP + j] = result[f] + (2.0 * j + 1.0) * fluxy_ref[j % 2, f]

            for f in ACTIVE[1]:
                before = sums_y[f][1 - j % 2]
                sums_y[f][1 - j % 2] = here[f] if before is None else before + here[f]
            for f in range(FIELDS):
                run_ref[1 - parity, f, j] += here[f]

    @pl.loop(0, NP)
    def _(j):
        even_x, odd_x = local_flux(
            [run_ref[1, f, j] for f in range(FIELDS)],
            [run_ref[0, f, j] for f in range(FIELDS)],
            0, 1, *keeps_x, rinv, lam, mu, speed,
        )
        for f in range(FIELDS):
            flux_ref[0, f, j] = even_x[f]
            flux_ref[1, f, j] = odd_x[f]


def inner(wave, rows):
    return call(
        lambda *refs: inner_kernel(None, *refs),
        (wave, rows),
        [array(FIELDS, 64, NP, NE), array(2, FIELDS, NP, NP, NE)],
        [pltpu.VMEM((2, FIELDS, NP, NP, NE), f32), pltpu.VMEM((2, FIELDS, NP, NE), f32)],
    )


def complete(begun, fluxz, rows, step):
    return call(
        lambda *refs: inner_kernel(step, *refs),
        (begun, fluxz, rows),
        [
            array(FIELDS, 64, NP, NE),
            array(FIELDS, 64, NP, NE),
            array(2, FIELDS, NP, NP, NE),
        ],
        [pltpu.VMEM((2, FIELDS, NP, NP, NE), f32), pltpu.VMEM((2, FIELDS, NP, NE), f32)],
    )


def order_masks(order, k, i, step):
    highest = [jnp.maximum(k, jnp.maximum(i, j)).astype(f32) for j in range(NP)]
    return [jnp.where(h <= order, step, 0.0) for h in highest]


def lifted_row(fluxz_ref, f, at, k):
    return jnp.where(
        k % 2 == 0,
        jnp.broadcast_to(fluxz_ref[0, f, pl.ds(at, 1), :], (NP, NE)),
        jnp.broadcast_to(fluxz_ref[1, f, pl.ds(at, 1), :], (NP, NE)),
    )


def begin_kernel(half, *refs):
    refs = list(refs)
    base_ref = refs.pop(0) if half else None
    wave_ref, part_ref, flux_ref, rows_ref, out_ref, cross_ref, paired_ref = refs
    order = jnp.broadcast_to(rows_ref[4:5, :], (NP, NE))
    odd = odd_device()
    k = lax.broadcasted_iota(jnp.int32, (NP, NE), 0)

    @pl.loop(0, NP)
    def _(i):
        parity = lax.rem(i, 2)
        factor_x = (2 * i + 1).astype(f32)
        at = pl.multiple_of(i * NP, NP)
        rows = pl.ds(at, NP)
        masks = order_masks(order, k, i, 0.5 * DT if half else DT)
        for f in range(FIELDS):
            fresh = []
            for j in range(NP):
                slope = part_ref[f, at + j] + factor_x * flux_ref[parity, f, j]
                start = wave_ref[f, at + j]
                if half:
                    start = 0.5 * (base_ref[f, at + j] + start)
                new = start + masks[j] * slope
                out_ref[f, at + j] = new
                fresh.append(new)
            upper, lower = face_traces(fresh, k)
            cross_ref[f, rows] = jnp.where(odd, upper, lower)
            paired_ref[f, rows] = jnp.where(odd, lower, upper)


def begin(base, wave, part, flux, rows):
    half = base is not None
    return call(
        lambda *refs: begin_kernel(half, *refs),
        ([base] if half else []) + [wave, part, flux, rows],
        [array(FIELDS, 64, NP, NE), array(FIELDS, 64, NE), array(FIELDS, 64, NE)],
    )


def outer_kernel(
    step, cross_ref, paired_ref, got_cross_ref, got_paired_ref, begun_cross_ref,
    begun_paired_ref, rows_ref, fluxz_ref, out_cross_ref, out_paired_ref,
):
    rinv, lam, mu, speed = materials(rows_ref)
    order = jnp.broadcast_to(rows_ref[4:5, :], (NP, NE))
    side = jnp.where(odd_device(), 1.0, -1.0)
    j = lax.broadcasted_iota(jnp.int32, (NP, NE), 0)

    def factors(first):
        total = jnp.zeros((NP, NE), f32)
        for n in range(first, NP, 2):
            total = total + jnp.where(order >= float(n), 2.0 * n + 1.0, 0.0)
        return step * total

    factor_even, factor_odd = factors(0), side * factors(1)

    @pl.loop(0, NP)
    def _(i):
        rows = pl.ds(pl.multiple_of(i * NP, NP), NP)
        total, difference = [], []
        for f in range(FIELDS):
            jump_cross = cross_ref[f, rows] - got_cross_ref[f, rows]
            jump_paired = paired_ref[f, rows] - got_paired_ref[f, rows]
            total.append(jump_cross + jump_paired)
            difference.append(side * (jump_cross - jump_paired))
        even, odds = face_flux(total, difference, 2, rinv, lam, mu, speed)
        allowed = jnp.where(jnp.maximum(j, i).astype(f32) <= order, 1.0, 0.0)
        scale_even, scale_odd = allowed * factor_even, allowed * factor_odd
        for f in range(FIELDS):
            fluxz_ref[0, f, rows] = even[f]
            fluxz_ref[1, f, rows] = odds[f]
            from_even, from_odd = scale_even * even[f], scale_odd * odds[f]
            out_cross_ref[f, rows] = begun_cross_ref[f, rows] + (from_even + from_odd)
            out_paired_ref[f, rows] = begun_paired_ref[f, rows] + (from_even - from_odd)


def outer(traces, got, begun_traces, rows, step):
    trace = array(FIELDS, 64, NE)
    return call(
        lambda *refs: outer_kernel(step, *refs),
        [*traces, *got, *begun_traces, rows],
        [array(2, FIELDS, 64, NE), trace, trace],
    )


def finish_kernel(
    begun_ref, cross_ref, paired_ref, got_cross_ref, got_paired_ref, rows_ref, strain_ref,
    first_ref, out_hbm, gradient_ref, out_ref, fluxz_ref, sums_ref, out_sem,
):
    rinv, lam, mu, speed = materials(rows_ref)
    order = jnp.broadcast_to(rows_ref[4:5, :], (NP, NE))
    orient = jnp.broadcast_to(rows_ref[5:6, :], (NP, NE))
    side = jnp.where(odd_device(), 1.0, -1.0)
    k = lax.broadcasted_iota(jnp.int32, (NP, NE), 0)
    factor_z = (2 * k + 1).astype(f32)
    sums_ref[...] = jnp.zeros_like(sums_ref)

    def leave(i):
        rows = pl.ds(pl.multiple_of(i * NP, NP), NP)
        return pltpu.make_async_copy(out_ref.at[:, rows], out_hbm.at[:, rows], out_sem.at[i])

    @pl.loop(0, NP)
    def _(i):
        at = pl.multiple_of(i * NP, NP)
        rows = pl.ds(at, NP)
        total, difference = [], []
        for f in range(FIELDS):
            jump_cross = cross_ref[f, rows] - got_cross_ref[f, rows]
            jump_paired = paired_ref[f, rows] - got_paired_ref[f, rows]
            total.append(jump_cross + jump_paired)
            difference.append(side * (jump_cross - jump_paired))
        even, odds = face_flux(total, difference, 2, rinv, lam, mu, speed)
        for f in range(FIELDS):
            fluxz_ref[0, f] = even[f]
            fluxz_ref[1, f] = odds[f]

        scales = [factor_z * mask for mask in order_masks(order, k, i, 0.5 * DT)]
        flip_x = ((orient == 1.0) | (orient == 3.0)) & (lax.rem(i, 2) == 1)
        sign_x = jnp.where(flip_x, -1.0, 1.0)
        sign_y = jnp.where(orient >= 2.0, -1.0, 1.0)
        signs = [sign_x, sign_x * sign_y]
        stresses = [[] for _ in range(NP)]
        for f in range(FIELDS):
            for j in range(NP):
                lifted = lifted_row(fluxz_ref, f, j, k)
                new = begun_ref[f, at + j] + scales[j] * lifted
                out_ref[f, at + j] = new * signs[j % 2]
                if f >= 3:
                    stresses[j].append(new)
        leave(i).start()
        for j in range(NP):
            add_gradient(sums_ref, stresses[j], [strain_ref[f, at + j] for f in range(6)])

    gradient_ref[...] = first_ref[...] + gradient_rows(sums_ref)
    for i in range(NP):
        leave(i).wait()


def finish(begun, traces, got, rows, strain, first):
    return call(
        finish_kernel,
        [begun, *traces, *got, rows, strain, first],
        [array(FIELDS, 64, NP, NE), array(2, NE)],
        [
            pltpu.VMEM((FIELDS, 64, NP, NE), f32),
            pltpu.VMEM((2, FIELDS, NP, NE), f32),
            pltpu.VMEM((2, NP, NE), f32),
            pltpu.SemaphoreType.DMA((NP,)),
        ],
        hbm_out=(0,),
    )


def add_gradient(sums_ref, stress, strain):
    normal = (stress[0] + stress[1]) + stress[2]
    sums_ref[0] += normal * ((strain[0] + strain[1]) + strain[2])
    shear = stress[0] * strain[0]
    for f in range(1, 6):
        shear = shear + stress[f] * strain[f]
    sums_ref[1] += shear


def gradient_rows(sums_ref):
    first = (0.5 * DT) * jnp.sum(sums_ref[0], axis=0, keepdims=True)
    second = DT * jnp.sum(sums_ref[1], axis=0, keepdims=True)
    return jnp.concatenate([first, second], axis=0)


def velocity_kernel(second, meta_ref, pick_ref, frame_ref, *refs):
    if second:
        snap_ref, got_ref, strain_ref, *rest = refs
    else:
        wave_ref, snap_ref, got_ref, gradient_ref, *rest = refs
    vel_ref, run_ref, sums_ref = rest
    start = 3 if second else 0
    keep = meta_ref[6:7, :] > 0.5
    row = lax.broadcasted_iota(jnp.int32, (8, NE), 0)
    keep1, keep2, keep4, factor_z = mode_rows()
    weight_z = 2.0 / factor_z
    sums_ref[...] = jnp.zeros_like(sums_ref)

    def settle(c):
        block = gather_elements(pick_ref[...], got_ref, (FIELDS + start + c) * 8)
        block = jnp.concatenate([jnp.where(row == 0, 0.0, block[0:8]), block[8:]], axis=0)
        velocity = jnp.where(keep, snap_ref[start + c], block) * frame_ref[...]
        vel_ref[c] = velocity.reshape(64, NP, NE)

    def strains(use):
        run_ref[...] = jnp.zeros_like(run_ref)

        @pl.loop(0, NP)
        def _(g):
            i = NP - 1 - g
            parity = lax.rem(i, 2)
            at = pl.multiple_of(i * NP, NP)
            weight_x = 2.0 / jnp.full((NP, NE), 2 * i + 1, jnp.int32).astype(f32)
            weight_xz = 2.0 * weight_x * weight_z
            zero = jnp.zeros((NP, NE), f32)
            run_y = [[zero, zero] for _ in range(3)]
            for j in range(NP - 1, -1, -1):
                weight_y = 2.0 / (2.0 * j + 1.0)
                slopes = []
                for c in range(3):
                    here = vel_ref[c, at + j]
                    slopes.append([
                        (2.0 * weight_y) * (weight_z * run_ref[parity, c, j]),
                        weight_xz * run_y[c][j % 2],
                        (2.0 * weight_y) * (weight_x * sums_above(here, keep1, keep2, keep4)),
                    ])
                    run_y[c][1 - j % 2] = run_y[c][1 - j % 2] + here
                    run_ref[1 - parity, c, j] += here
                use(at + j, [
                    2.0 * slopes[0][0], 2.0 * slopes[1][1], 2.0 * slopes[2][2],
                    slopes[2][1] + slopes[1][2], slopes[2][0] + slopes[0][2],
                    slopes[1][0] + slopes[0][1],
                ])

    for c in range(3):
        settle(c)
    if second:

        def keep_strains(at, strain):
            for f in range(6):
                strain_ref[f, at] = strain[f]

        strains(keep_strains)
    else:
        strains(
            lambda at, strain: add_gradient(
                sums_ref, [wave_ref[3 + f, at] for f in range(6)], strain
            )
        )
        gradient_ref[...] = gradient_rows(sums_ref)


def velocities(meta, pick, frame, wave, snaps, got):
    second = wave is None
    operands = [meta, pick, frame] + ([] if second else [wave]) + [snaps, got]

    def kernel(*refs):
        velocity_kernel(second, *refs)

    (result,) = call(
        kernel,
        operands,
        [array(6, 64, NP, NE) if second else array(2, NE)],
        [
            pltpu.VMEM((3, 64, NP, NE), f32),
            pltpu.VMEM((2, 3, NP, NP, NE), f32),
            pltpu.VMEM((2, NP, NE), f32),
        ],
    )
    return result


def exchange(send):
    return lax.all_to_all(send, "dom", split_axis=0, concat_axis=0, tiled=True)


def swap_traces(cross, paired):
    ups = [(d, d + 1) for d in range(1, DEV - 1, 2)]
    pairs = [(d, d + 1) for d in range(0, DEV, 2)]
    both = lambda steps: steps + [(b, a) for a, b in steps]
    return lax.ppermute(cross, "dom", both(ups)), lax.ppermute(paired, "dom", both(pairs))


def body(
    adjoint, snapshots, density, lame_lambda, lame_mu, element_order, orient, new_owner, new_slot
):
    rows = [
        x.reshape(1, NE)
        for x in (new_owner, density, lame_lambda, lame_mu, element_order, orient, new_slot)
    ]
    snaps = snapshots.reshape(SNAPS, NM, NE)
    send, meta = pack(rows, adjoint, snaps)
    got = lax.all_to_all(send, "dom", split_axis=0, concat_axis=0, tiled=True)
    wave, *traces, rows, pick, frame = place(meta, got, adjoint)
    part, flux = inner(wave, rows)
    start, base = wave, None
    for stage in range(2 * STEPS - 1):
        got_traces = swap_traces(*traces)
        step = DT if base is None else 0.5 * DT
        begun, *begun_traces = begin(base, wave, part, flux, rows)
        if stage == 2:
            strain = velocities(meta, pick, frame, None, snaps, got)
            begun_traces[0], strain = lax.optimization_barrier((begun_traces[0], strain))
        fluxz, *traces = outer(traces, got_traces, begun_traces, rows, step)
        wave, part, flux = complete(begun, fluxz, rows, step)
        if base is None:
            base = start
        else:
            start, base = wave, None
    first = velocities(meta, pick, frame, start, snaps, got)
    got_traces = swap_traces(*traces)
    begun, *_ = begin(base, wave, part, flux, rows)
    signed, gradients = finish(begun, traces, got_traces, rows, strain, first)
    return signed.reshape(FIELDS, NM, NE), gradients


def solution(mesh):
    shard = P("dom")
    in_specs = (P(None, None, "dom"), P(None, None, None, "dom")) + (shard,) * 7
    out_specs = (P(None, None, "dom"), P(None, "dom"))
    return jax.shard_map(body, mesh=mesh, in_specs=in_specs, out_specs=out_specs, check_vma=False)
```

```python
import jax
import jax.numpy as jnp
from jax import lax
from jax.experimental import pallas as pl
from jax.experimental.pallas import tpu as pltpu
from jax.sharding import PartitionSpec as P

NP = 8
NM = 512
EX = 8
NE = 128
STEPS = 2
DEV = 128
FIELDS = 9
SNAPS = 6
BLOCKS = FIELDS + SNAPS
DT = 0.01
f32 = jnp.float32
bf16 = jnp.bfloat16

VOIGT = ((3, 8, 7), (8, 4, 6), (7, 6, 5))
ACTIVE = tuple((0, 1, 2) + VOIGT[a] for a in range(3))


def split3(x):
    high = x.astype(bf16)
    rest = x - high.astype(f32)
    middle = rest.astype(bf16)
    low = (rest - middle.astype(f32)).astype(bf16)
    return high, middle, low


def call(kernel, operands, out_shape, scratch_shapes=(), hbm=(), hbm_out=(), limit=16):
    def space(position, x):
        return pltpu.HBM if position in hbm else pltpu.VMEM

    return pl.pallas_call(
        kernel,
        in_specs=[pl.BlockSpec(memory_space=space(n, x)) for n, x in enumerate(operands)],
        out_specs=[
            pl.BlockSpec(memory_space=pltpu.HBM if n in hbm_out else pltpu.VMEM)
            for n in range(len(out_shape))
        ],
        out_shape=out_shape,
        scratch_shapes=list(scratch_shapes),
        compiler_params=pltpu.CompilerParams(vmem_limit_bytes=limit * 1024 * 1024),
        cost_estimate=pl.CostEstimate(flops=0, bytes_accessed=0, transcendentals=0),
    )(*operands)


def array(*shape, dtype=f32):
    return jax.ShapeDtypeStruct(shape, dtype)


def scatter_rows(hot, blocks, out_ref, row):
    parts = jnp.concatenate(split3(jnp.concatenate(blocks, axis=0)), axis=1)
    hots = jnp.concatenate([hot, hot, hot], axis=1)
    rows = lax.dot_general(hots, parts, (((1,), (1,)), ((), ())), preferred_element_type=f32)
    for b in range(len(blocks)):
        store_block(rows[:, b * NM : (b + 1) * NM], out_ref, row + 8 * b)


def store_block(rows, out_ref, row):
    groups = [
        rows[r * DEV : (r + 1) * DEV, q * 128 : (q + 1) * 128].reshape(DEV // 8, 8, 128)
        for r in range(2)
        for q in range(4)
    ]
    tiles = jnp.swapaxes(jnp.stack(groups, axis=1), 1, 2)
    out_ref[:, row : row + 8, :] = tiles.reshape(DEV, 8, 128)


def pack_kernel(*refs):
    (owner_hbm, density_hbm, lambda_hbm, mu_hbm, order_hbm, orient_hbm, slot_hbm, adj_hbm,
     snap_hbm, out_hbm, meta_ref, owner_ref, floats_ref, ints_ref, hot_ref, block_ref, out_ref,
     row_sem, in_sem, out_sem) = refs
    small = [pltpu.make_async_copy(owner_hbm, owner_ref, row_sem.at[0])]
    for n, source in enumerate((density_hbm, lambda_hbm, mu_hbm)):
        small.append(pltpu.make_async_copy(source, floats_ref.at[n], row_sem.at[1 + n]))
    for n, source in enumerate((order_hbm, orient_hbm, slot_hbm)):
        small.append(pltpu.make_async_copy(source, ints_ref.at[n], row_sem.at[4 + n]))
    arrive = []
    for b in range(BLOCKS):
        source = adj_hbm.at[b] if b < FIELDS else snap_hbm.at[b - FIELDS]
        arrive.append(pltpu.make_async_copy(source, block_ref.at[b], in_sem.at[b]))
    for copy in small + arrive:
        copy.start()
    for copy in small:
        copy.wait()
    for n in range(3):
        meta_ref[n : n + 1, :] = floats_ref[n]
        meta_ref[3 + n : 4 + n, :] = ints_ref[n].astype(f32)
    meta_ref[5:6, :] += 1.0
    meta_ref[6:7, :] = jnp.where(owner_ref[...] == lax.axis_index("dom"), 1.0, 0.0)
    meta_ref[7:8, :] = jnp.zeros((1, NE), f32)
    owner_row = owner_ref[...]
    owner_all = jnp.broadcast_to(owner_row, (NE, NE))
    owner_col = jnp.transpose(owner_all)
    at0 = lax.broadcasted_iota(jnp.int32, (NE, NE), 0)
    at1 = lax.broadcasted_iota(jnp.int32, (NE, NE), 1)
    earlier = jnp.where((owner_col == owner_all) & (at0 < at1), 1.0, 0.0)
    rank = jnp.sum(earlier, axis=0, keepdims=True)
    dest = jnp.where(owner_row != lax.axis_index("dom"), owner_row, -1)
    for r in range(2):
        chosen = (at0 == dest) & (rank == float(r))
        hot_ref[r * DEV : (r + 1) * DEV, :] = jnp.where(chosen, 1.0, 0.0).astype(bf16)

    first_row = lax.broadcasted_iota(jnp.int32, (8, NE), 0) == 0
    def load(b):
        arrive[b].wait()
        block = block_ref[b]
        if b < FIELDS:
            return block
        n = b - FIELDS
        row = jnp.broadcast_to(meta_ref[n : n + 1, :], (8, NE))
        return jnp.concatenate([jnp.where(first_row, row, block[0:8]), block[8:]], axis=0)

    leave, b = [], 0
    for count in (3, 3, 3, 3, 2, 1):
        scatter_rows(hot_ref[...], [load(b + n) for n in range(count)], out_ref, b * 8)
        rows = pl.ds(b * 8, count * 8)
        leave.append(
            pltpu.make_async_copy(out_ref.at[:, rows, :], out_hbm.at[:, rows, :], out_sem.at[b])
        )
        leave[-1].start()
        b += count
    for copy in leave:
        copy.wait()


def pack(rows, adjoint, snaps):
    return call(
        pack_kernel,
        (*rows, adjoint, snaps),
        [array(DEV, BLOCKS * 8, 128), array(8, NE)],
        [
            pltpu.VMEM((1, NE), jnp.int32),
            pltpu.VMEM((3, 1, NE), f32),
            pltpu.VMEM((3, 1, NE), jnp.int32),
            pltpu.VMEM((2 * DEV, NE), bf16),
            pltpu.VMEM((BLOCKS, NM, NE), f32),
            pltpu.VMEM((DEV, BLOCKS * 8, 128), f32),
            pltpu.SemaphoreType.DMA((7,)),
            pltpu.SemaphoreType.DMA((BLOCKS,)),
            pltpu.SemaphoreType.DMA((BLOCKS,)),
        ],
        hbm=tuple(range(9)),
        hbm_out=(0,),
        limit=63,
    )


def select_slots(pick, slots):
    parts = jnp.concatenate(split3(slots), axis=0)
    picks = jnp.concatenate([pick, pick, pick], axis=1)
    placed = lax.dot_general(picks, parts, (((1,), (0,)), ((), ())), preferred_element_type=f32)
    return jnp.transpose(placed)


def gather_elements(pick, got_ref, row):
    tiles = jnp.swapaxes(got_ref[:, row : row + 8, :].reshape(DEV // 8, 8, 8, 128), 1, 2)
    rows = [tiles[:, n].reshape(DEV, 128) for n in range(8)]
    slots = [jnp.concatenate(rows[4 * r : 4 * r + 4], axis=1) for r in range(2)]
    return select_slots(pick, jnp.concatenate(slots, axis=0))


def mode_indices(shape):
    mode = lax.broadcasted_iota(jnp.int32, shape, 0)
    return mode // 64, (mode // 8) % 8, mode % 8


def mask_and_sign(order, orient):
    i, j, k = mode_indices((NM, NE))
    highest = jnp.maximum(jnp.maximum(i, j), k).astype(f32)
    flip_x = (orient == 1.0) | (orient == 3.0)
    flip_y = orient >= 2.0
    sign_x = jnp.where(i % 2 == 1, jnp.where(flip_x, -1.0, 1.0), 1.0)
    sign_y = jnp.where(j % 2 == 1, jnp.where(flip_y, -1.0, 1.0), 1.0)
    return jnp.where(highest <= order, sign_x * sign_y, 0.0)


def odd_device():
    return jnp.full((NP, NE), lax.axis_index("dom"), jnp.int32) % 2 == 1


def face_traces(modes, row):
    low4, low2, even = row < 4, row % 4 < 2, row % 2 == 0
    fours = []
    for j in range(4):
        first, second = modes[j], modes[j + 4]
        other = jnp.where(low4, second, first)
        fours.append(jnp.where(low4, first, second) + pltpu.roll(other, 4, 0))
    twos = []
    for j in range(2):
        first, second = fours[j], fours[j + 2]
        twos.append(
            jnp.where(low2, first + pltpu.roll(first, 6, 0), second + pltpu.roll(second, 2, 0))
        )
    first, second = twos
    next_first, next_second = pltpu.roll(first, 7, 0), pltpu.roll(second, 1, 0)
    upper = jnp.where(even, first + next_first, second + next_second)
    lower = jnp.where(even, first - next_first, next_second - second)
    return upper, lower


def place_kernel(
    meta_ref, got_ref, adj_ref, wave_ref, cross_ref, paired_ref, rows_ref, pick_ref, frame_ref
):
    keep = meta_ref[6:7, :] > 0.5
    odd = odd_device()
    lane = lax.broadcasted_iota(jnp.int32, (DEV, NE), 1)
    columns = []
    for r in range(2):
        column = jnp.zeros((DEV, NE), f32)
        for n in range(SNAPS):
            value = got_ref[:, (FIELDS + n) * 8 + r * 4, 0:1]
            column = jnp.where(lane == n, value, column)
        columns.append(column)
        chosen = jnp.where(column[:, 5:6] == lane.astype(f32) + 1.0, 1.0, 0.0)
        pick_ref[:, r * DEV : (r + 1) * DEV] = jnp.transpose(chosen).astype(bf16)
    arrived = select_slots(pick_ref[...], jnp.concatenate(columns, axis=0))
    meta = jnp.where(keep, meta_ref[...], arrived[0:8])
    density, lam, mu = meta[0:1], meta[1:2], meta[2:3]
    order, orient = meta[3:4], meta[4:5]
    rows_ref[0:1, :] = 1.0 / density
    rows_ref[1:2, :] = lam
    rows_ref[2:3, :] = mu
    rows_ref[3:4, :] = jnp.sqrt((lam + 2.0 * mu) / density)
    rows_ref[4:5, :] = order
    rows_ref[5:6, :] = orient
    rows_ref[6:8, :] = jnp.zeros((2, NE), f32)
    frame_ref[...] = mask_and_sign(order, orient)

    row = lax.broadcasted_iota(jnp.int32, (NP, NE), 0)
    for f in range(FIELDS):
        block = gather_elements(pick_ref[...], got_ref, f * 8)
        wave = jnp.where(keep, adj_ref[f], block) * frame_ref[...]
        wave = wave.reshape(64, NP, NE)
        wave_ref[f] = wave
        for i in range(NP):
            upper, lower = face_traces([wave[i * NP + j] for j in range(NP)], row)
            cross_ref[f, i * NP : (i + 1) * NP, :] = jnp.where(odd, upper, lower)
            paired_ref[f, i * NP : (i + 1) * NP, :] = jnp.where(odd, lower, upper)


def place(meta, got, adjoint):
    return call(
        place_kernel,
        (meta, got, adjoint),
        [
            array(FIELDS, 64, NP, NE),
            array(FIELDS, 64, NE),
            array(FIELDS, 64, NE),
            array(8, NE),
            array(NE, 2 * DEV, dtype=bf16),
            array(NM, NE),
        ],
    )


def materials(rows_ref):
    full = lambda r: jnp.broadcast_to(rows_ref[r : r + 1, :], (NP, NE))
    return full(0), full(1), full(2), full(3)


def apply_b(values, direction, rinv, lam, mu):
    out = [None] * FIELDS
    for c in range(3):
        out[c] = values[VOIGT[c][direction]] * rinv
    spread = lam * values[direction]
    for b in range(3):
        out[3 + b] = spread
    out[3 + direction] = spread + 2.0 * mu * values[direction]
    for c in range(3):
        if c != direction:
            out[VOIGT[c][direction]] = mu * values[c]
    return out


def face_flux(total, difference, direction, rinv, lam, mu, speed):
    even_b = apply_b(difference, direction, rinv, lam, mu)
    odd_b = apply_b(total, direction, rinv, lam, mu)
    even, odd = [], []
    for f in range(FIELDS):
        pen_even, pen_odd = speed * total[f], speed * difference[f]
        if even_b[f] is not None:
            pen_even, pen_odd = pen_even + even_b[f], pen_odd + odd_b[f]
        even.append(-0.25 * pen_even)
        odd.append(-0.25 * pen_odd)
    return even, odd


def local_flux(evens, odds, direction, offset, keep_up, keep_down, rinv, lam, mu, speed):
    total, difference = [], []
    for f in range(FIELDS):
        upper, lower = evens[f] + odds[f], evens[f] - odds[f]
        above = pltpu.roll(lower, NE - offset, 1) * keep_up
        below = pltpu.roll(upper, offset, 1) * keep_down
        total.append((upper - above) + (lower - below))
        difference.append((upper - above) - (lower - below))
    return face_flux(total, difference, direction, rinv, lam, mu, speed)


def lane_keeps():
    lane = lax.broadcasted_iota(jnp.int32, (NP, NE), 1)
    one = lambda cond: jnp.where(cond, 1.0, 0.0)
    column = lane % EX
    return (
        (one(column != EX - 1), one(column != 0)),
        (one(lane < NE - EX), one(lane >= EX)),
    )


def mode_rows():
    k = lax.broadcasted_iota(jnp.int32, (NP, NE), 0)
    one = lambda cond: jnp.where(cond, 1.0, 0.0)
    return one(k < 7), one(k < 6), one(k < 4), (2 * k + 1).astype(f32)


def sums_above(x, keep1, keep2, keep4):
    x = pltpu.roll(x, 7, 0) * keep1
    x = x + pltpu.roll(x, 6, 0) * keep2
    return x + pltpu.roll(x, 4, 0) * keep4


def inner_kernel(step, *refs):
    if step is None:
        wave_ref, rows_ref, out_ref, flux_ref, run_ref, fluxy_ref = refs
    else:
        (begun_ref, fluxz_ref, rows_ref, wave_ref, out_ref, flux_ref, run_ref,
         fluxy_ref) = refs
        order = jnp.broadcast_to(rows_ref[4:5, :], (NP, NE))
        k = lax.broadcasted_iota(jnp.int32, (NP, NE), 0)
    rinv, lam, mu, speed = materials(rows_ref)
    keeps_x, keeps_y = lane_keeps()
    keep1, keep2, keep4, factor_z = mode_rows()
    run_ref[...] = jnp.zeros_like(run_ref)

    @pl.loop(0, NP)
    def _(g):
        i = NP - 1 - g
        parity = lax.rem(i, 2)
        factor_x = (2 * i + 1).astype(f32)

        if step is not None:
            at = pl.multiple_of(i * NP, NP)
            scales = [factor_z * mask for mask in order_masks(order, k, i, step)]
            for f in range(FIELDS):
                for j in range(NP):
                    lifted = lifted_row(fluxz_ref, f, at + j, k)
                    wave_ref[f, at + j] = begun_ref[f, at + j] + scales[j] * lifted

        evens, odds = [], []
        for f in range(FIELDS):
            col = [wave_ref[f, i * NP + j] for j in range(NP)]
            evens.append((col[0] + col[2]) + (col[4] + col[6]))
            odds.append((col[1] + col[3]) + (col[5] + col[7]))
        even, odd = local_flux(evens, odds, 1, EX, *keeps_y, rinv, lam, mu, speed)
        for f in range(FIELDS):
            fluxy_ref[0, f] = even[f]
            fluxy_ref[1, f] = odd[f]

        sums_y = {f: [None, None] for f in ACTIVE[1]}
        for j in range(NP - 1, -1, -1):
            here = [wave_ref[f, i * NP + j] for f in range(FIELDS)]
            slope = [{}, {}, {}]
            for f in ACTIVE[0]:
                slope[0][f] = factor_x * run_ref[parity, f, j]
            for f in ACTIVE[1]:
                if sums_y[f][j % 2] is not None:
                    slope[1][f] = (2.0 * j + 1.0) * sums_y[f][j % 2]
            for f in ACTIVE[2]:
                slope[2][f] = factor_z * sums_above(here[f], keep1, keep2, keep4)

            def total(pairs):
                found = [slope[a][f] for a, f in pairs if f in slope[a]]
                result = found[0]
                for item in found[1:]:
                    result = result + item
                return result

            result = [None] * FIELDS
            for c in range(3):
                result[c] = rinv * total([(a, VOIGT[c][a]) for a in range(3)])
            spread = lam * total([(a, a) for a in range(3)])
            for b in range(3):
                if b in slope[b]:
                    result[3 + b] = spread + 2.0 * mu * slope[b][b]
                else:
                    result[3 + b] = spread
            for b, c in ((1, 2), (0, 2), (0, 1)):
                result[VOIGT[b][c]] = mu * total([(b, c), (c, b)])
            for f in range(FIELDS):
                out_ref[f, i * NP + j] = result[f] + (2.0 * j + 1.0) * fluxy_ref[j % 2, f]

            for f in ACTIVE[1]:
                before = sums_y[f][1 - j % 2]
                sums_y[f][1 - j % 2] = here[f] if before is None else before + here[f]
            for f in range(FIELDS):
                run_ref[1 - parity, f, j] += here[f]

    @pl.loop(0, NP)
    def _(j):
        even_x, odd_x = local_flux(
            [run_ref[1, f, j] for f in range(FIELDS)],
            [run_ref[0, f, j] for f in range(FIELDS)],
            0, 1, *keeps_x, rinv, lam, mu, speed,
        )
        for f in range(FIELDS):
            flux_ref[0, f, j] = even_x[f]
            flux_ref[1, f, j] = odd_x[f]


def inner(wave, rows):
    return call(
        lambda *refs: inner_kernel(None, *refs),
        (wave, rows),
        [array(FIELDS, 64, NP, NE), array(2, FIELDS, NP, NP, NE)],
        [pltpu.VMEM((2, FIELDS, NP, NP, NE), f32), pltpu.VMEM((2, FIELDS, NP, NE), f32)],
    )


def complete(begun, fluxz, rows, step):
    return call(
        lambda *refs: inner_kernel(step, *refs),
        (begun, fluxz, rows),
        [
            array(FIELDS, 64, NP, NE),
            array(FIELDS, 64, NP, NE),
            array(2, FIELDS, NP, NP, NE),
        ],
        [pltpu.VMEM((2, FIELDS, NP, NP, NE), f32), pltpu.VMEM((2, FIELDS, NP, NE), f32)],
    )


def order_masks(order, k, i, step):
    highest = [jnp.maximum(k, jnp.maximum(i, j)).astype(f32) for j in range(NP)]
    return [jnp.where(h <= order, step, 0.0) for h in highest]


def lifted_row(fluxz_ref, f, at, k):
    return jnp.where(
        k % 2 == 0,
        jnp.broadcast_to(fluxz_ref[0, f, pl.ds(at, 1), :], (NP, NE)),
        jnp.broadcast_to(fluxz_ref[1, f, pl.ds(at, 1), :], (NP, NE)),
    )


def begin_kernel(half, *refs):
    refs = list(refs)
    base_ref = refs.pop(0) if half else None
    wave_ref, part_ref, flux_ref, rows_ref, out_ref, cross_ref, paired_ref = refs
    order = jnp.broadcast_to(rows_ref[4:5, :], (NP, NE))
    odd = odd_device()
    k = lax.broadcasted_iota(jnp.int32, (NP, NE), 0)

    @pl.loop(0, NP)
    def _(i):
        parity = lax.rem(i, 2)
        factor_x = (2 * i + 1).astype(f32)
        at = pl.multiple_of(i * NP, NP)
        rows = pl.ds(at, NP)
        masks = order_masks(order, k, i, 0.5 * DT if half else DT)
        for f in range(FIELDS):
            fresh = []
            for j in range(NP):
                slope = part_ref[f, at + j] + factor_x * flux_ref[parity, f, j]
                start = wave_ref[f, at + j]
                if half:
                    start = 0.5 * (base_ref[f, at + j] + start)
                new = start + masks[j] * slope
                out_ref[f, at + j] = new
                fresh.append(new)
            upper, lower = face_traces(fresh, k)
            cross_ref[f, rows] = jnp.where(odd, upper, lower)
            paired_ref[f, rows] = jnp.where(odd, lower, upper)


def begin(base, wave, part, flux, rows):
    half = base is not None
    return call(
        lambda *refs: begin_kernel(half, *refs),
        ([base] if half else []) + [wave, part, flux, rows],
        [array(FIELDS, 64, NP, NE), array(FIELDS, 64, NE), array(FIELDS, 64, NE)],
    )


def outer_kernel(
    step, cross_ref, paired_ref, got_cross_ref, got_paired_ref, begun_cross_ref,
    begun_paired_ref, rows_ref, fluxz_ref, out_cross_ref, out_paired_ref,
):
    rinv, lam, mu, speed = materials(rows_ref)
    order = jnp.broadcast_to(rows_ref[4:5, :], (NP, NE))
    side = jnp.where(odd_device(), 1.0, -1.0)
    j = lax.broadcasted_iota(jnp.int32, (NP, NE), 0)

    def factors(first):
        total = jnp.zeros((NP, NE), f32)
        for n in range(first, NP, 2):
            total = total + jnp.where(order >= float(n), 2.0 * n + 1.0, 0.0)
        return step * total

    factor_even, factor_odd = factors(0), side * factors(1)

    @pl.loop(0, NP)
    def _(i):
        rows = pl.ds(pl.multiple_of(i * NP, NP), NP)
        total, difference = [], []
        for f in range(FIELDS):
            jump_cross = cross_ref[f, rows] - got_cross_ref[f, rows]
            jump_paired = paired_ref[f, rows] - got_paired_ref[f, rows]
            total.append(jump_cross + jump_paired)
            difference.append(side * (jump_cross - jump_paired))
        even, odds = face_flux(total, difference, 2, rinv, lam, mu, speed)
        allowed = jnp.where(jnp.maximum(j, i).astype(f32) <= order, 1.0, 0.0)
        scale_even, scale_odd = allowed * factor_even, allowed * factor_odd
        for f in range(FIELDS):
            fluxz_ref[0, f, rows] = even[f]
            fluxz_ref[1, f, rows] = odds[f]
            from_even, from_odd = scale_even * even[f], scale_odd * odds[f]
            out_cross_ref[f, rows] = begun_cross_ref[f, rows] + (from_even + from_odd)
            out_paired_ref[f, rows] = begun_paired_ref[f, rows] + (from_even - from_odd)


def outer(traces, got, begun_traces, rows, step):
    trace = array(FIELDS, 64, NE)
    return call(
        lambda *refs: outer_kernel(step, *refs),
        [*traces, *got, *begun_traces, rows],
        [array(2, FIELDS, 64, NE), trace, trace],
    )


def finish_kernel(
    base_ref, wave_ref, part_ref, flux_ref, cross_ref, paired_ref, got_cross_ref,
    got_paired_ref, rows_ref, strain_ref, first_ref, out_hbm, gradient_ref,
    out_ref, fluxz_ref, sums_ref, out_sem,
):
    rinv, lam, mu, speed = materials(rows_ref)
    order = jnp.broadcast_to(rows_ref[4:5, :], (NP, NE))
    orient = jnp.broadcast_to(rows_ref[5:6, :], (NP, NE))
    side = jnp.where(odd_device(), 1.0, -1.0)
    k = lax.broadcasted_iota(jnp.int32, (NP, NE), 0)
    factor_z = (2 * k + 1).astype(f32)
    sums_ref[...] = jnp.zeros_like(sums_ref)

    def leave(i):
        rows = pl.ds(pl.multiple_of(i * NP, NP), NP)
        return pltpu.make_async_copy(out_ref.at[:, rows], out_hbm.at[:, rows], out_sem.at[i])

    @pl.loop(0, NP)
    def _(i):
        parity = lax.rem(i, 2)
        factor_x = (2 * i + 1).astype(f32)
        at = pl.multiple_of(i * NP, NP)
        rows = pl.ds(at, NP)
        total, difference = [], []
        for f in range(FIELDS):
            jump_cross = cross_ref[f, rows] - got_cross_ref[f, rows]
            jump_paired = paired_ref[f, rows] - got_paired_ref[f, rows]
            total.append(jump_cross + jump_paired)
            difference.append(side * (jump_cross - jump_paired))
        even, odds = face_flux(total, difference, 2, rinv, lam, mu, speed)
        for f in range(FIELDS):
            fluxz_ref[0, f] = even[f]
            fluxz_ref[1, f] = odds[f]

        masks = order_masks(order, k, i, 0.5 * DT)
        flip_x = ((orient == 1.0) | (orient == 3.0)) & (parity == 1)
        sign_x = jnp.where(flip_x, -1.0, 1.0)
        sign_y = jnp.where(orient >= 2.0, -1.0, 1.0)
        signs = [sign_x, sign_x * sign_y]
        stresses = [[] for _ in range(NP)]
        for f in range(FIELDS):
            for j in range(NP):
                lifted = lifted_row(fluxz_ref, f, j, k)
                slope = part_ref[f, at + j] + factor_x * flux_ref[parity, f, j] + factor_z * lifted
                start = 0.5 * (base_ref[f, at + j] + wave_ref[f, at + j])
                new = start + masks[j] * slope
                out_ref[f, at + j] = new * signs[j % 2]
                if f >= 3:
                    stresses[j].append(new)
        leave(i).start()
        for j in range(NP):
            add_gradient(sums_ref, stresses[j], [strain_ref[f, at + j] for f in range(6)])

    gradient_ref[...] = first_ref[...] + gradient_rows(sums_ref)
    for i in range(NP):
        leave(i).wait()


def finish(base, wave, part, flux, traces, got, rows, strain, first):
    return call(
        finish_kernel,
        [base, wave, part, flux, *traces, *got, rows, strain, first],
        [array(FIELDS, 64, NP, NE), array(2, NE)],
        [
            pltpu.VMEM((FIELDS, 64, NP, NE), f32),
            pltpu.VMEM((2, FIELDS, NP, NE), f32),
            pltpu.VMEM((2, NP, NE), f32),
            pltpu.SemaphoreType.DMA((NP,)),
        ],
        hbm_out=(0,),
    )


def add_gradient(sums_ref, stress, strain):
    normal = (stress[0] + stress[1]) + stress[2]
    sums_ref[0] += normal * ((strain[0] + strain[1]) + strain[2])
    shear = stress[0] * strain[0]
    for f in range(1, 6):
        shear = shear + stress[f] * strain[f]
    sums_ref[1] += shear


def gradient_rows(sums_ref):
    first = (0.5 * DT) * jnp.sum(sums_ref[0], axis=0, keepdims=True)
    second = DT * jnp.sum(sums_ref[1], axis=0, keepdims=True)
    return jnp.concatenate([first, second], axis=0)


def velocity_kernel(second, meta_ref, pick_ref, frame_ref, *refs):
    if second:
        snap_ref, got_ref, strain_ref, *rest = refs
    else:
        wave_ref, snap_ref, got_ref, gradient_ref, *rest = refs
    vel_ref, run_ref, sums_ref = rest
    start = 3 if second else 0
    keep = meta_ref[6:7, :] > 0.5
    row = lax.broadcasted_iota(jnp.int32, (8, NE), 0)
    keep1, keep2, keep4, factor_z = mode_rows()
    weight_z = 2.0 / factor_z
    sums_ref[...] = jnp.zeros_like(sums_ref)

    def settle(c):
        block = gather_elements(pick_ref[...], got_ref, (FIELDS + start + c) * 8)
        block = jnp.concatenate([jnp.where(row == 0, 0.0, block[0:8]), block[8:]], axis=0)
        velocity = jnp.where(keep, snap_ref[start + c], block) * frame_ref[...]
        vel_ref[c] = velocity.reshape(64, NP, NE)

    def strains(use):
        run_ref[...] = jnp.zeros_like(run_ref)

        @pl.loop(0, NP)
        def _(g):
            i = NP - 1 - g
            parity = lax.rem(i, 2)
            at = pl.multiple_of(i * NP, NP)
            weight_x = 2.0 / jnp.full((NP, NE), 2 * i + 1, jnp.int32).astype(f32)
            weight_xz = 2.0 * weight_x * weight_z
            zero = jnp.zeros((NP, NE), f32)
            run_y = [[zero, zero] for _ in range(3)]
            for j in range(NP - 1, -1, -1):
                weight_y = 2.0 / (2.0 * j + 1.0)
                slopes = []
                for c in range(3):
                    here = vel_ref[c, at + j]
                    slopes.append([
                        (2.0 * weight_y) * (weight_z * run_ref[parity, c, j]),
                        weight_xz * run_y[c][j % 2],
                        (2.0 * weight_y) * (weight_x * sums_above(here, keep1, keep2, keep4)),
                    ])
                    run_y[c][1 - j % 2] = run_y[c][1 - j % 2] + here
                    run_ref[1 - parity, c, j] += here
                use(at + j, [
                    2.0 * slopes[0][0], 2.0 * slopes[1][1], 2.0 * slopes[2][2],
                    slopes[2][1] + slopes[1][2], slopes[2][0] + slopes[0][2],
                    slopes[1][0] + slopes[0][1],
                ])

    for c in range(3):
        settle(c)
    if second:

        def keep_strains(at, strain):
            for f in range(6):
                strain_ref[f, at] = strain[f]

        strains(keep_strains)
    else:
        strains(
            lambda at, strain: add_gradient(
                sums_ref, [wave_ref[3 + f, at] for f in range(6)], strain
            )
        )
        gradient_ref[...] = gradient_rows(sums_ref)


def velocities(meta, pick, frame, wave, snaps, got):
    second = wave is None
    operands = [meta, pick, frame] + ([] if second else [wave]) + [snaps, got]

    def kernel(*refs):
        velocity_kernel(second, *refs)

    (result,) = call(
        kernel,
        operands,
        [array(6, 64, NP, NE) if second else array(2, NE)],
        [
            pltpu.VMEM((3, 64, NP, NE), f32),
            pltpu.VMEM((2, 3, NP, NP, NE), f32),
            pltpu.VMEM((2, NP, NE), f32),
        ],
    )
    return result


def exchange(send):
    return lax.all_to_all(send, "dom", split_axis=0, concat_axis=0, tiled=True)


def swap_traces(cross, paired):
    ups = [(d, d + 1) for d in range(1, DEV - 1, 2)]
    pairs = [(d, d + 1) for d in range(0, DEV, 2)]
    both = lambda steps: steps + [(b, a) for a, b in steps]
    return lax.ppermute(cross, "dom", both(ups)), lax.ppermute(paired, "dom", both(pairs))


def body(
    adjoint, snapshots, density, lame_lambda, lame_mu, element_order, orient, new_owner, new_slot
):
    rows = [
        x.reshape(1, NE)
        for x in (new_owner, density, lame_lambda, lame_mu, element_order, orient, new_slot)
    ]
    snaps = snapshots.reshape(SNAPS, NM, NE)
    send, meta = pack(rows, adjoint, snaps)
    got = lax.all_to_all(send, "dom", split_axis=0, concat_axis=0, tiled=True)
    wave, *traces, rows, pick, frame = place(meta, got, adjoint)
    part, flux = inner(wave, rows)
    start, base = wave, None
    for stage in range(2 * STEPS - 1):
        got_traces = swap_traces(*traces)
        step = DT if base is None else 0.5 * DT
        begun, *begun_traces = begin(base, wave, part, flux, rows)
        if stage == 2:
            strain = velocities(meta, pick, frame, None, snaps, got)
            begun_traces[0], strain = lax.optimization_barrier((begun_traces[0], strain))
        fluxz, *traces = outer(traces, got_traces, begun_traces, rows, step)
        wave, part, flux = complete(begun, fluxz, rows, step)
        if base is None:
            base = start
        else:
            start, base = wave, None
    first = velocities(meta, pick, frame, start, snaps, got)
    got_traces = swap_traces(*traces)
    signed, gradients = finish(
        base, wave, part, flux, traces, got_traces, rows, strain, first
    )
    return signed.reshape(FIELDS, NM, NE), gradients


def solution(mesh):
    shard = P("dom")
    in_specs = (P(None, None, "dom"), P(None, None, None, "dom")) + (shard,) * 7
    out_specs = (P(None, None, "dom"), P(None, "dom"))
    return jax.shard_map(body, mesh=mesh, in_specs=in_specs, out_specs=out_specs, check_vma=False)
```

```python
import jax
import jax.numpy as jnp
from jax import lax
from jax.experimental import pallas as pl
from jax.experimental.pallas import tpu as pltpu
from jax.sharding import PartitionSpec as P

NP = 8
NM = 512
EX = 8
NE = 128
STEPS = 2
DEV = 128
FIELDS = 9
SNAPS = 6
BLOCKS = FIELDS + SNAPS
DT = 0.01
f32 = jnp.float32
bf16 = jnp.bfloat16

VOIGT = ((3, 8, 7), (8, 4, 6), (7, 6, 5))
ACTIVE = tuple((0, 1, 2) + VOIGT[a] for a in range(3))


def split3(x):
    high = x.astype(bf16)
    rest = x - high.astype(f32)
    middle = rest.astype(bf16)
    low = (rest - middle.astype(f32)).astype(bf16)
    return high, middle, low


def call(kernel, operands, out_shape, scratch_shapes=(), hbm=(), hbm_out=(), limit=16):
    def space(position, x):
        return pltpu.HBM if position in hbm else pltpu.VMEM

    return pl.pallas_call(
        kernel,
        in_specs=[pl.BlockSpec(memory_space=space(n, x)) for n, x in enumerate(operands)],
        out_specs=[
            pl.BlockSpec(memory_space=pltpu.HBM if n in hbm_out else pltpu.VMEM)
            for n in range(len(out_shape))
        ],
        out_shape=out_shape,
        scratch_shapes=list(scratch_shapes),
        compiler_params=pltpu.CompilerParams(vmem_limit_bytes=limit * 1024 * 1024),
        cost_estimate=pl.CostEstimate(flops=0, bytes_accessed=0, transcendentals=0),
    )(*operands)


def array(*shape, dtype=f32):
    return jax.ShapeDtypeStruct(shape, dtype)


def scatter_rows(hot, blocks, out_ref, row):
    parts = jnp.concatenate(split3(jnp.concatenate(blocks, axis=0)), axis=1)
    hots = jnp.concatenate([hot, hot, hot], axis=1)
    rows = lax.dot_general(hots, parts, (((1,), (1,)), ((), ())), preferred_element_type=f32)
    for b in range(len(blocks)):
        store_block(rows[:, b * NM : (b + 1) * NM], out_ref, row + 8 * b)


def store_block(rows, out_ref, row):
    groups = [
        rows[r * DEV : (r + 1) * DEV, q * 128 : (q + 1) * 128].reshape(DEV // 8, 8, 128)
        for r in range(2)
        for q in range(4)
    ]
    tiles = jnp.swapaxes(jnp.stack(groups, axis=1), 1, 2)
    out_ref[:, row : row + 8, :] = tiles.reshape(DEV, 8, 128)


def pack_kernel(*refs):
    (owner_hbm, density_hbm, lambda_hbm, mu_hbm, order_hbm, orient_hbm, slot_hbm, adj_hbm,
     snap_hbm, out_hbm, meta_ref, owner_ref, floats_ref, ints_ref, hot_ref, block_ref, out_ref,
     row_sem, in_sem, out_sem) = refs
    small = [pltpu.make_async_copy(owner_hbm, owner_ref, row_sem.at[0])]
    for n, source in enumerate((density_hbm, lambda_hbm, mu_hbm)):
        small.append(pltpu.make_async_copy(source, floats_ref.at[n], row_sem.at[1 + n]))
    for n, source in enumerate((order_hbm, orient_hbm, slot_hbm)):
        small.append(pltpu.make_async_copy(source, ints_ref.at[n], row_sem.at[4 + n]))
    arrive = []
    for b in range(BLOCKS):
        source = adj_hbm.at[b] if b < FIELDS else snap_hbm.at[b - FIELDS]
        arrive.append(pltpu.make_async_copy(source, block_ref.at[b], in_sem.at[b]))
    for copy in small + arrive:
        copy.start()
    for copy in small:
        copy.wait()
    for n in range(3):
        meta_ref[n : n + 1, :] = floats_ref[n]
        meta_ref[3 + n : 4 + n, :] = ints_ref[n].astype(f32)
    meta_ref[5:6, :] += 1.0
    meta_ref[6:7, :] = jnp.where(owner_ref[...] == lax.axis_index("dom"), 1.0, 0.0)
    meta_ref[7:8, :] = jnp.zeros((1, NE), f32)
    owner_row = owner_ref[...]
    owner_all = jnp.broadcast_to(owner_row, (NE, NE))
    owner_col = jnp.transpose(owner_all)
    at0 = lax.broadcasted_iota(jnp.int32, (NE, NE), 0)
    at1 = lax.broadcasted_iota(jnp.int32, (NE, NE), 1)
    earlier = jnp.where((owner_col == owner_all) & (at0 < at1), 1.0, 0.0)
    rank = jnp.sum(earlier, axis=0, keepdims=True)
    dest = jnp.where(owner_row != lax.axis_index("dom"), owner_row, -1)
    for r in range(2):
        chosen = (at0 == dest) & (rank == float(r))
        hot_ref[r * DEV : (r + 1) * DEV, :] = jnp.where(chosen, 1.0, 0.0).astype(bf16)

    first_row = lax.broadcasted_iota(jnp.int32, (8, NE), 0) == 0
    def load(b):
        arrive[b].wait()
        block = block_ref[b]
        if b < FIELDS:
            return block
        n = b - FIELDS
        row = jnp.broadcast_to(meta_ref[n : n + 1, :], (8, NE))
        return jnp.concatenate([jnp.where(first_row, row, block[0:8]), block[8:]], axis=0)

    leave, b = [], 0
    for count in (3, 5, 4, 2, 1):
        scatter_rows(hot_ref[...], [load(b + n) for n in range(count)], out_ref, b * 8)
        rows = pl.ds(b * 8, count * 8)
        leave.append(
            pltpu.make_async_copy(out_ref.at[:, rows, :], out_hbm.at[:, rows, :], out_sem.at[b])
        )
        leave[-1].start()
        b += count
    for copy in leave:
        copy.wait()


def pack(rows, adjoint, snaps):
    return call(
        pack_kernel,
        (*rows, adjoint, snaps),
        [array(DEV, BLOCKS * 8, 128), array(8, NE)],
        [
            pltpu.VMEM((1, NE), jnp.int32),
            pltpu.VMEM((3, 1, NE), f32),
            pltpu.VMEM((3, 1, NE), jnp.int32),
            pltpu.VMEM((2 * DEV, NE), bf16),
            pltpu.VMEM((BLOCKS, NM, NE), f32),
            pltpu.VMEM((DEV, BLOCKS * 8, 128), f32),
            pltpu.SemaphoreType.DMA((7,)),
            pltpu.SemaphoreType.DMA((BLOCKS,)),
            pltpu.SemaphoreType.DMA((BLOCKS,)),
        ],
        hbm=tuple(range(9)),
        hbm_out=(0,),
        limit=63,
    )


def select_slots(pick, slots):
    parts = jnp.concatenate(split3(slots), axis=0)
    picks = jnp.concatenate([pick, pick, pick], axis=1)
    placed = lax.dot_general(picks, parts, (((1,), (0,)), ((), ())), preferred_element_type=f32)
    return jnp.transpose(placed)


def gather_elements(pick, got_ref, row):
    tiles = jnp.swapaxes(got_ref[:, row : row + 8, :].reshape(DEV // 8, 8, 8, 128), 1, 2)
    rows = [tiles[:, n].reshape(DEV, 128) for n in range(8)]
    slots = [jnp.concatenate(rows[4 * r : 4 * r + 4], axis=1) for r in range(2)]
    return select_slots(pick, jnp.concatenate(slots, axis=0))


def mode_indices(shape):
    mode = lax.broadcasted_iota(jnp.int32, shape, 0)
    return mode // 64, (mode // 8) % 8, mode % 8


def mask_and_sign(order, orient):
    i, j, k = mode_indices((NM, NE))
    highest = jnp.maximum(jnp.maximum(i, j), k).astype(f32)
    flip_x = (orient == 1.0) | (orient == 3.0)
    flip_y = orient >= 2.0
    sign_x = jnp.where(i % 2 == 1, jnp.where(flip_x, -1.0, 1.0), 1.0)
    sign_y = jnp.where(j % 2 == 1, jnp.where(flip_y, -1.0, 1.0), 1.0)
    return jnp.where(highest <= order, sign_x * sign_y, 0.0)


def odd_device():
    return jnp.full((NP, NE), lax.axis_index("dom"), jnp.int32) % 2 == 1


def face_traces(modes, row):
    low4, low2, even = row < 4, row % 4 < 2, row % 2 == 0
    fours = []
    for j in range(4):
        first, second = modes[j], modes[j + 4]
        other = jnp.where(low4, second, first)
        fours.append(jnp.where(low4, first, second) + pltpu.roll(other, 4, 0))
    twos = []
    for j in range(2):
        first, second = fours[j], fours[j + 2]
        twos.append(
            jnp.where(low2, first + pltpu.roll(first, 6, 0), second + pltpu.roll(second, 2, 0))
        )
    first, second = twos
    next_first, next_second = pltpu.roll(first, 7, 0), pltpu.roll(second, 1, 0)
    upper = jnp.where(even, first + next_first, second + next_second)
    lower = jnp.where(even, first - next_first, next_second - second)
    return upper, lower


def place_kernel(
    meta_ref, got_ref, adj_ref, wave_ref, cross_ref, paired_ref, rows_ref, pick_ref, frame_ref
):
    keep = meta_ref[6:7, :] > 0.5
    odd = odd_device()
    lane = lax.broadcasted_iota(jnp.int32, (DEV, NE), 1)
    columns = []
    for r in range(2):
        column = jnp.zeros((DEV, NE), f32)
        for n in range(SNAPS):
            value = got_ref[:, (FIELDS + n) * 8 + r * 4, 0:1]
            column = jnp.where(lane == n, value, column)
        columns.append(column)
        chosen = jnp.where(column[:, 5:6] == lane.astype(f32) + 1.0, 1.0, 0.0)
        pick_ref[:, r * DEV : (r + 1) * DEV] = jnp.transpose(chosen).astype(bf16)
    arrived = select_slots(pick_ref[...], jnp.concatenate(columns, axis=0))
    meta = jnp.where(keep, meta_ref[...], arrived[0:8])
    density, lam, mu = meta[0:1], meta[1:2], meta[2:3]
    order, orient = meta[3:4], meta[4:5]
    rows_ref[0:1, :] = 1.0 / density
    rows_ref[1:2, :] = lam
    rows_ref[2:3, :] = mu
    rows_ref[3:4, :] = jnp.sqrt((lam + 2.0 * mu) / density)
    rows_ref[4:5, :] = order
    rows_ref[5:6, :] = orient
    rows_ref[6:8, :] = jnp.zeros((2, NE), f32)
    frame_ref[...] = mask_and_sign(order, orient)

    row = lax.broadcasted_iota(jnp.int32, (NP, NE), 0)
    for f in range(FIELDS):
        block = gather_elements(pick_ref[...], got_ref, f * 8)
        wave = jnp.where(keep, adj_ref[f], block) * frame_ref[...]
        wave = wave.reshape(64, NP, NE)
        wave_ref[f] = wave
        for i in range(NP):
            upper, lower = face_traces([wave[i * NP + j] for j in range(NP)], row)
            cross_ref[f, i * NP : (i + 1) * NP, :] = jnp.where(odd, upper, lower)
            paired_ref[f, i * NP : (i + 1) * NP, :] = jnp.where(odd, lower, upper)


def place(meta, got, adjoint):
    return call(
        place_kernel,
        (meta, got, adjoint),
        [
            array(FIELDS, 64, NP, NE),
            array(FIELDS, 64, NE),
            array(FIELDS, 64, NE),
            array(8, NE),
            array(NE, 2 * DEV, dtype=bf16),
            array(NM, NE),
        ],
    )


def materials(rows_ref):
    full = lambda r: jnp.broadcast_to(rows_ref[r : r + 1, :], (NP, NE))
    return full(0), full(1), full(2), full(3)


def apply_b(values, direction, rinv, lam, mu):
    out = [None] * FIELDS
    for c in range(3):
        out[c] = values[VOIGT[c][direction]] * rinv
    spread = lam * values[direction]
    for b in range(3):
        out[3 + b] = spread
    out[3 + direction] = spread + 2.0 * mu * values[direction]
    for c in range(3):
        if c != direction:
            out[VOIGT[c][direction]] = mu * values[c]
    return out


def face_flux(total, difference, direction, rinv, lam, mu, speed):
    even_b = apply_b(difference, direction, rinv, lam, mu)
    odd_b = apply_b(total, direction, rinv, lam, mu)
    even, odd = [], []
    for f in range(FIELDS):
        pen_even, pen_odd = speed * total[f], speed * difference[f]
        if even_b[f] is not None:
            pen_even, pen_odd = pen_even + even_b[f], pen_odd + odd_b[f]
        even.append(-0.25 * pen_even)
        odd.append(-0.25 * pen_odd)
    return even, odd


def local_flux(evens, odds, direction, offset, keep_up, keep_down, rinv, lam, mu, speed):
    total, difference = [], []
    for f in range(FIELDS):
        upper, lower = evens[f] + odds[f], evens[f] - odds[f]
        above = pltpu.roll(lower, NE - offset, 1) * keep_up
        below = pltpu.roll(upper, offset, 1) * keep_down
        total.append((upper - above) + (lower - below))
        difference.append((upper - above) - (lower - below))
    return face_flux(total, difference, direction, rinv, lam, mu, speed)


def lane_keeps():
    lane = lax.broadcasted_iota(jnp.int32, (NP, NE), 1)
    one = lambda cond: jnp.where(cond, 1.0, 0.0)
    column = lane % EX
    return (
        (one(column != EX - 1), one(column != 0)),
        (one(lane < NE - EX), one(lane >= EX)),
    )


def mode_rows():
    k = lax.broadcasted_iota(jnp.int32, (NP, NE), 0)
    one = lambda cond: jnp.where(cond, 1.0, 0.0)
    return one(k < 7), one(k < 6), one(k < 4), (2 * k + 1).astype(f32)


def sums_above(x, keep1, keep2, keep4):
    x = pltpu.roll(x, 7, 0) * keep1
    x = x + pltpu.roll(x, 6, 0) * keep2
    return x + pltpu.roll(x, 4, 0) * keep4


def inner_kernel(step, *refs):
    if step is None:
        wave_ref, rows_ref, out_ref, flux_ref, run_ref, fluxy_ref = refs
    else:
        (begun_ref, fluxz_ref, rows_ref, wave_ref, out_ref, flux_ref, run_ref,
         fluxy_ref) = refs
        order = jnp.broadcast_to(rows_ref[4:5, :], (NP, NE))
        k = lax.broadcasted_iota(jnp.int32, (NP, NE), 0)
    rinv, lam, mu, speed = materials(rows_ref)
    keeps_x, keeps_y = lane_keeps()
    keep1, keep2, keep4, factor_z = mode_rows()
    run_ref[...] = jnp.zeros_like(run_ref)

    @pl.loop(0, NP)
    def _(g):
        i = NP - 1 - g
        parity = lax.rem(i, 2)
        factor_x = (2 * i + 1).astype(f32)

        if step is not None:
            at = pl.multiple_of(i * NP, NP)
            scales = [factor_z * mask for mask in order_masks(order, k, i, step)]
            for f in range(FIELDS):
                for j in range(NP):
                    lifted = lifted_row(fluxz_ref, f, at + j, k)
                    wave_ref[f, at + j] = begun_ref[f, at + j] + scales[j] * lifted

        evens, odds = [], []
        for f in range(FIELDS):
            col = [wave_ref[f, i * NP + j] for j in range(NP)]
            evens.append((col[0] + col[2]) + (col[4] + col[6]))
            odds.append((col[1] + col[3]) + (col[5] + col[7]))
        even, odd = local_flux(evens, odds, 1, EX, *keeps_y, rinv, lam, mu, speed)
        for f in range(FIELDS):
            fluxy_ref[0, f] = even[f]
            fluxy_ref[1, f] = odd[f]

        sums_y = {f: [None, None] for f in ACTIVE[1]}
        for j in range(NP - 1, -1, -1):
            here = [wave_ref[f, i * NP + j] for f in range(FIELDS)]
            slope = [{}, {}, {}]
            for f in ACTIVE[0]:
                slope[0][f] = factor_x * run_ref[parity, f, j]
            for f in ACTIVE[1]:
                if sums_y[f][j % 2] is not None:
                    slope[1][f] = (2.0 * j + 1.0) * sums_y[f][j % 2]
            for f in ACTIVE[2]:
                slope[2][f] = factor_z * sums_above(here[f], keep1, keep2, keep4)

            def total(pairs):
                found = [slope[a][f] for a, f in pairs if f in slope[a]]
                result = found[0]
                for item in found[1:]:
                    result = result + item
                return result

            result = [None] * FIELDS
            for c in range(3):
                result[c] = rinv * total([(a, VOIGT[c][a]) for a in range(3)])
            spread = lam * total([(a, a) for a in range(3)])
            for b in range(3):
                if b in slope[b]:
                    result[3 + b] = spread + 2.0 * mu * slope[b][b]
                else:
                    result[3 + b] = spread
            for b, c in ((1, 2), (0, 2), (0, 1)):
                result[VOIGT[b][c]] = mu * total([(b, c), (c, b)])
            for f in range(FIELDS):
                out_ref[f, i * NP + j] = result[f] + (2.0 * j + 1.0) * fluxy_ref[j % 2, f]

            for f in ACTIVE[1]:
                before = sums_y[f][1 - j % 2]
                sums_y[f][1 - j % 2] = here[f] if before is None else before + here[f]
            for f in range(FIELDS):
                run_ref[1 - parity, f, j] += here[f]

    @pl.loop(0, NP)
    def _(j):
        even_x, odd_x = local_flux(
            [run_ref[1, f, j] for f in range(FIELDS)],
            [run_ref[0, f, j] for f in range(FIELDS)],
            0, 1, *keeps_x, rinv, lam, mu, speed,
        )
        for f in range(FIELDS):
            flux_ref[0, f, j] = even_x[f]
            flux_ref[1, f, j] = odd_x[f]


def inner(wave, rows):
    return call(
        lambda *refs: inner_kernel(None, *refs),
        (wave, rows),
        [array(FIELDS, 64, NP, NE), array(2, FIELDS, NP, NP, NE)],
        [pltpu.VMEM((2, FIELDS, NP, NP, NE), f32), pltpu.VMEM((2, FIELDS, NP, NE), f32)],
    )


def complete(begun, fluxz, rows, step):
    return call(
        lambda *refs: inner_kernel(step, *refs),
        (begun, fluxz, rows),
        [
            array(FIELDS, 64, NP, NE),
            array(FIELDS, 64, NP, NE),
            array(2, FIELDS, NP, NP, NE),
        ],
        [pltpu.VMEM((2, FIELDS, NP, NP, NE), f32), pltpu.VMEM((2, FIELDS, NP, NE), f32)],
    )


def order_masks(order, k, i, step):
    highest = [jnp.maximum(k, jnp.maximum(i, j)).astype(f32) for j in range(NP)]
    return [jnp.where(h <= order, step, 0.0) for h in highest]


def lifted_row(fluxz_ref, f, at, k):
    return jnp.where(
        k % 2 == 0,
        jnp.broadcast_to(fluxz_ref[0, f, pl.ds(at, 1), :], (NP, NE)),
        jnp.broadcast_to(fluxz_ref[1, f, pl.ds(at, 1), :], (NP, NE)),
    )


def begin_kernel(half, *refs):
    refs = list(refs)
    base_ref = refs.pop(0) if half else None
    wave_ref, part_ref, flux_ref, rows_ref, out_ref, cross_ref, paired_ref = refs
    order = jnp.broadcast_to(rows_ref[4:5, :], (NP, NE))
    odd = odd_device()
    k = lax.broadcasted_iota(jnp.int32, (NP, NE), 0)

    @pl.loop(0, NP)
    def _(i):
        parity = lax.rem(i, 2)
        factor_x = (2 * i + 1).astype(f32)
        at = pl.multiple_of(i * NP, NP)
        rows = pl.ds(at, NP)
        masks = order_masks(order, k, i, 0.5 * DT if half else DT)
        for f in range(FIELDS):
            fresh = []
            for j in range(NP):
                slope = part_ref[f, at + j] + factor_x * flux_ref[parity, f, j]
                start = wave_ref[f, at + j]
                if half:
                    start = 0.5 * (base_ref[f, at + j] + start)
                new = start + masks[j] * slope
                out_ref[f, at + j] = new
                fresh.append(new)
            upper, lower = face_traces(fresh, k)
            cross_ref[f, rows] = jnp.where(odd, upper, lower)
            paired_ref[f, rows] = jnp.where(odd, lower, upper)


def begin(base, wave, part, flux, rows):
    half = base is not None
    return call(
        lambda *refs: begin_kernel(half, *refs),
        ([base] if half else []) + [wave, part, flux, rows],
        [array(FIELDS, 64, NP, NE), array(FIELDS, 64, NE), array(FIELDS, 64, NE)],
    )


def outer_kernel(
    step, cross_ref, paired_ref, got_cross_ref, got_paired_ref, begun_cross_ref,
    begun_paired_ref, rows_ref, fluxz_ref, out_cross_ref, out_paired_ref,
):
    rinv, lam, mu, speed = materials(rows_ref)
    order = jnp.broadcast_to(rows_ref[4:5, :], (NP, NE))
    side = jnp.where(odd_device(), 1.0, -1.0)
    j = lax.broadcasted_iota(jnp.int32, (NP, NE), 0)

    def factors(first):
        total = jnp.zeros((NP, NE), f32)
        for n in range(first, NP, 2):
            total = total + jnp.where(order >= float(n), 2.0 * n + 1.0, 0.0)
        return step * total

    factor_even, factor_odd = factors(0), side * factors(1)

    @pl.loop(0, NP)
    def _(i):
        rows = pl.ds(pl.multiple_of(i * NP, NP), NP)
        total, difference = [], []
        for f in range(FIELDS):
            jump_cross = cross_ref[f, rows] - got_cross_ref[f, rows]
            jump_paired = paired_ref[f, rows] - got_paired_ref[f, rows]
            total.append(jump_cross + jump_paired)
            difference.append(side * (jump_cross - jump_paired))
        even, odds = face_flux(total, difference, 2, rinv, lam, mu, speed)
        allowed = jnp.where(jnp.maximum(j, i).astype(f32) <= order, 1.0, 0.0)
        scale_even, scale_odd = allowed * factor_even, allowed * factor_odd
        for f in range(FIELDS):
            fluxz_ref[0, f, rows] = even[f]
            fluxz_ref[1, f, rows] = odds[f]
            from_even, from_odd = scale_even * even[f], scale_odd * odds[f]
            out_cross_ref[f, rows] = begun_cross_ref[f, rows] + (from_even + from_odd)
            out_paired_ref[f, rows] = begun_paired_ref[f, rows] + (from_even - from_odd)


def outer(traces, got, begun_traces, rows, step):
    trace = array(FIELDS, 64, NE)
    return call(
        lambda *refs: outer_kernel(step, *refs),
        [*traces, *got, *begun_traces, rows],
        [array(2, FIELDS, 64, NE), trace, trace],
    )


def finish_kernel(
    begun_ref, cross_ref, paired_ref, got_cross_ref, got_paired_ref, rows_ref, strain_ref,
    first_ref, out_hbm, gradient_ref, out_ref, fluxz_ref, sums_ref, out_sem,
):
    rinv, lam, mu, speed = materials(rows_ref)
    order = jnp.broadcast_to(rows_ref[4:5, :], (NP, NE))
    orient = jnp.broadcast_to(rows_ref[5:6, :], (NP, NE))
    side = jnp.where(odd_device(), 1.0, -1.0)
    k = lax.broadcasted_iota(jnp.int32, (NP, NE), 0)
    factor_z = (2 * k + 1).astype(f32)
    sums_ref[...] = jnp.zeros_like(sums_ref)

    def leave(i):
        rows = pl.ds(pl.multiple_of(i * NP, NP), NP)
        return pltpu.make_async_copy(out_ref.at[:, rows], out_hbm.at[:, rows], out_sem.at[i])

    @pl.loop(0, NP)
    def _(i):
        at = pl.multiple_of(i * NP, NP)
        rows = pl.ds(at, NP)
        total, difference = [], []
        for f in range(FIELDS):
            jump_cross = cross_ref[f, rows] - got_cross_ref[f, rows]
            jump_paired = paired_ref[f, rows] - got_paired_ref[f, rows]
            total.append(jump_cross + jump_paired)
            difference.append(side * (jump_cross - jump_paired))
        even, odds = face_flux(total, difference, 2, rinv, lam, mu, speed)
        for f in range(FIELDS):
            fluxz_ref[0, f] = even[f]
            fluxz_ref[1, f] = odds[f]

        scales = [factor_z * mask for mask in order_masks(order, k, i, 0.5 * DT)]
        flip_x = ((orient == 1.0) | (orient == 3.0)) & (lax.rem(i, 2) == 1)
        sign_x = jnp.where(flip_x, -1.0, 1.0)
        sign_y = jnp.where(orient >= 2.0, -1.0, 1.0)
        signs = [sign_x, sign_x * sign_y]
        stresses = [[] for _ in range(NP)]
        for f in range(FIELDS):
            for j in range(NP):
                lifted = lifted_row(fluxz_ref, f, j, k)
                new = begun_ref[f, at + j] + scales[j] * lifted
                out_ref[f, at + j] = new * signs[j % 2]
                if f >= 3:
                    stresses[j].append(new)
        leave(i).start()
        for j in range(NP):
            add_gradient(sums_ref, stresses[j], [strain_ref[f, at + j] for f in range(6)])

    gradient_ref[...] = first_ref[...] + gradient_rows(sums_ref)
    for i in range(NP):
        leave(i).wait()


def finish(begun, traces, got, rows, strain, first):
    return call(
        finish_kernel,
        [begun, *traces, *got, rows, strain, first],
        [array(FIELDS, 64, NP, NE), array(2, NE)],
        [
            pltpu.VMEM((FIELDS, 64, NP, NE), f32),
            pltpu.VMEM((2, FIELDS, NP, NE), f32),
            pltpu.VMEM((2, NP, NE), f32),
            pltpu.SemaphoreType.DMA((NP,)),
        ],
        hbm_out=(0,),
    )


def add_gradient(sums_ref, stress, strain):
    normal = (stress[0] + stress[1]) + stress[2]
    sums_ref[0] += normal * ((strain[0] + strain[1]) + strain[2])
    shear = stress[0] * strain[0]
    for f in range(1, 6):
        shear = shear + stress[f] * strain[f]
    sums_ref[1] += shear


def gradient_rows(sums_ref):
    first = (0.5 * DT) * jnp.sum(sums_ref[0], axis=0, keepdims=True)
    second = DT * jnp.sum(sums_ref[1], axis=0, keepdims=True)
    return jnp.concatenate([first, second], axis=0)


def velocity_kernel(second, meta_ref, pick_ref, frame_ref, *refs):
    if second:
        snap_ref, got_ref, strain_ref, *rest = refs
    else:
        wave_ref, snap_ref, got_ref, gradient_ref, *rest = refs
    vel_ref, run_ref, sums_ref = rest
    start = 3 if second else 0
    keep = meta_ref[6:7, :] > 0.5
    row = lax.broadcasted_iota(jnp.int32, (8, NE), 0)
    keep1, keep2, keep4, factor_z = mode_rows()
    weight_z = 2.0 / factor_z
    sums_ref[...] = jnp.zeros_like(sums_ref)

    def settle(c):
        block = gather_elements(pick_ref[...], got_ref, (FIELDS + start + c) * 8)
        block = jnp.concatenate([jnp.where(row == 0, 0.0, block[0:8]), block[8:]], axis=0)
        velocity = jnp.where(keep, snap_ref[start + c], block) * frame_ref[...]
        vel_ref[c] = velocity.reshape(64, NP, NE)

    def strains(use):
        run_ref[...] = jnp.zeros_like(run_ref)

        @pl.loop(0, NP)
        def _(g):
            i = NP - 1 - g
            parity = lax.rem(i, 2)
            at = pl.multiple_of(i * NP, NP)
            weight_x = 2.0 / jnp.full((NP, NE), 2 * i + 1, jnp.int32).astype(f32)
            weight_xz = 2.0 * weight_x * weight_z
            zero = jnp.zeros((NP, NE), f32)
            run_y = [[zero, zero] for _ in range(3)]
            for j in range(NP - 1, -1, -1):
                weight_y = 2.0 / (2.0 * j + 1.0)
                slopes = []
                for c in range(3):
                    here = vel_ref[c, at + j]
                    slopes.append([
                        (2.0 * weight_y) * (weight_z * run_ref[parity, c, j]),
                        weight_xz * run_y[c][j % 2],
                        (2.0 * weight_y) * (weight_x * sums_above(here, keep1, keep2, keep4)),
                    ])
                    run_y[c][1 - j % 2] = run_y[c][1 - j % 2] + here
                    run_ref[1 - parity, c, j] += here
                use(at + j, [
                    2.0 * slopes[0][0], 2.0 * slopes[1][1], 2.0 * slopes[2][2],
                    slopes[2][1] + slopes[1][2], slopes[2][0] + slopes[0][2],
                    slopes[1][0] + slopes[0][1],
                ])

    for c in range(3):
        settle(c)
    if second:

        def keep_strains(at, strain):
            for f in range(6):
                strain_ref[f, at] = strain[f]

        strains(keep_strains)
    else:
        strains(
            lambda at, strain: add_gradient(
                sums_ref, [wave_ref[3 + f, at] for f in range(6)], strain
            )
        )
        gradient_ref[...] = gradient_rows(sums_ref)


def velocities(meta, pick, frame, wave, snaps, got):
    second = wave is None
    operands = [meta, pick, frame] + ([] if second else [wave]) + [snaps, got]

    def kernel(*refs):
        velocity_kernel(second, *refs)

    (result,) = call(
        kernel,
        operands,
        [array(6, 64, NP, NE) if second else array(2, NE)],
        [
            pltpu.VMEM((3, 64, NP, NE), f32),
            pltpu.VMEM((2, 3, NP, NP, NE), f32),
            pltpu.VMEM((2, NP, NE), f32),
        ],
    )
    return result


def exchange(send):
    return lax.all_to_all(send, "dom", split_axis=0, concat_axis=0, tiled=True)


def swap_traces(cross, paired):
    ups = [(d, d + 1) for d in range(1, DEV - 1, 2)]
    pairs = [(d, d + 1) for d in range(0, DEV, 2)]
    both = lambda steps: steps + [(b, a) for a, b in steps]
    return lax.ppermute(cross, "dom", both(ups)), lax.ppermute(paired, "dom", both(pairs))


def body(
    adjoint, snapshots, density, lame_lambda, lame_mu, element_order, orient, new_owner, new_slot
):
    rows = [
        x.reshape(1, NE)
        for x in (new_owner, density, lame_lambda, lame_mu, element_order, orient, new_slot)
    ]
    snaps = snapshots.reshape(SNAPS, NM, NE)
    send, meta = pack(rows, adjoint, snaps)
    got = lax.all_to_all(send, "dom", split_axis=0, concat_axis=0, tiled=True)
    wave, *traces, rows, pick, frame = place(meta, got, adjoint)
    part, flux = inner(wave, rows)
    start, base = wave, None
    for stage in range(2 * STEPS - 1):
        got_traces = swap_traces(*traces)
        step = DT if base is None else 0.5 * DT
        begun, *begun_traces = begin(base, wave, part, flux, rows)
        if stage == 2:
            strain = velocities(meta, pick, frame, None, snaps, got)
            begun_traces[0], strain = lax.optimization_barrier((begun_traces[0], strain))
        fluxz, *traces = outer(traces, got_traces, begun_traces, rows, step)
        wave, part, flux = complete(begun, fluxz, rows, step)
        if base is None:
            base = start
        else:
            start, base = wave, None
    first = velocities(meta, pick, frame, start, snaps, got)
    got_traces = swap_traces(*traces)
    begun, *_ = begin(base, wave, part, flux, rows)
    signed, gradients = finish(begun, traces, got_traces, rows, strain, first)
    return signed.reshape(FIELDS, NM, NE), gradients


def solution(mesh):
    shard = P("dom")
    in_specs = (P(None, None, "dom"), P(None, None, None, "dom")) + (shard,) * 7
    out_specs = (P(None, None, "dom"), P(None, "dom"))
    return jax.shard_map(body, mesh=mesh, in_specs=in_specs, out_specs=out_specs, check_vma=False)
```
